128 devices in a mesh: ctx: 32 (over y, z, x_lo), wt: 4 (over x_hi, core).
Axes of the slice: x: 4 (x_hi: 2, x_lo: 2; x = x_hi * 2 + x_lo), y: 4, z: 4, core: 2. Of those that a mesh axis runs over, the one named last changes fastest.
Arguments:
- inputs: bfloat16 [4, 4096, 1600], P('wt', 'ctx'), may hold values from -6 to 6
- block_order: int32 [4, 32], P('wt'), may hold values from 0 to 31, as said below
- cotangent: bfloat16 [4, 4096, 1600], P('wt', 'ctx'), may hold values from -6 to 6
- ln1_gain: bfloat16 [1600], P('wt'), may hold values from 0.5 to 1.5
- ln1_bias: bfloat16 [1600], P('wt'), may hold values from -1.25 to 1.25
- w_qkv: bfloat16 [1600, 4800], P('wt'), may hold values from -0.15625 to 0.15625
- bias_q: bfloat16 [1600], P('wt'), may hold values from -1.25 to 1.25
- bias_v: bfloat16 [1600], P('wt'), may hold values from -1.25 to 1.25
- w_out: bfloat16 [1600, 1600], P('wt'), may hold values from -2.5 to 2.5
- bias_out: bfloat16 [1600], P('wt'), may hold values from -1.25 to 1.25
- ln2_gain: bfloat16 [1600], P('wt'), may hold values from 0.5 to 1.5
- ln2_bias: bfloat16 [1600], P('wt'), may hold values from -1.25 to 1.25
- w_fc: bfloat16 [1600, 6400], P('wt'), may hold values from -0.15625 to 0.15625
- bias_fc: bfloat16 [6400], P('wt'), may hold values from -1.25 to 1.25
- w_proj: bfloat16 [6400, 1600], P('wt'), may hold values from -0.078125 to 0.078125
- bias_proj: bfloat16 [1600], P('wt'), may hold values from -1.25 to 1.25
Outputs:
- outputs: bfloat16 [4, 4096, 1600], P('wt', 'ctx')
- grad_inputs: float32 [4, 4096, 1600], P('wt', 'ctx')
- grad_ln1_gain: float32 [1600], P('wt')
- grad_ln1_bias: float32 [1600], P('wt')
- grad_w_qkv: float32 [1600, 4800], P('wt')
- grad_bias_q: float32 [1600], P('wt')
- grad_bias_v: float32 [1600], P('wt')
- grad_w_out: float32 [1600, 1600], P('wt')
- grad_bias_out: float32 [1600], P('wt')
- grad_ln2_gain: float32 [1600], P('wt')
- grad_ln2_bias: float32 [1600], P('wt')
- grad_w_fc: float32 [1600, 6400], P('wt')
- grad_bias_fc: float32 [6400], P('wt')
- grad_w_proj: float32 [6400, 1600], P('wt')
- grad_bias_proj: float32 [1600], P('wt')
The draws below stay inside these ranges and needn't reach their ends.
Inputs may be any that keep to these rules, and one draw needn't show every extreme that they name: Each row of block_order names every block place 0 to 31 exactly once.
All inputs are finite; a program needn't handle non-finite values.
Results may differ from the reference program's by a relative error of at most 0.028.
Values may be sent and summed in bfloat16 or wider, within the bound.
A program may use at most 320 MiB of HBM per device.

```python
import jax
import jax.numpy as jnp
from jax import lax

D = 1600
HEADS = 25
HEAD_DIM = 64
FF = 6400
BLK = 128
LENGTH = 4096
SEQS = 4
N_CTX = 32


def draw_block_order(key, part):
    key = jax.random.fold_in(key, 7)
    sequence_keys = jax.random.split(key, SEQS)
    return jax.vmap(lambda one_key: jax.random.permutation(one_key, N_CTX))(sequence_keys).astype(jnp.int32)


def block_levels(rng, shape, cuts, low, largest):
    def one(position, parts):
        steps = jax.random.uniform(jax.random.fold_in(jax.random.fold_in(rng, 6), position), (parts,), jnp.float32, low / len(cuts), largest / len(cuts))
        return jnp.repeat(jnp.exp(steps), shape[position] // parts).reshape((-1,) + (1,) * (len(shape) - position - 1))

    level = one(*cuts[0])
    for cut in cuts[1:]:
        level = level * one(*cut)
    return level


def noise(stream_key, extent, deviation, bound, cuts=(), dtype=jnp.bfloat16):
    drawn = deviation * jax.random.normal(stream_key, extent, jnp.float32)
    if cuts:
        drawn = drawn * block_levels(stream_key, extent, cuts, -0.22, 0.18)
    return jnp.clip(drawn, -bound, bound).astype(dtype)


def setup_inputs(seed: int = 0) -> dict:
    key_of = jax.random.split(jax.random.key(seed), 17)
    inputs = noise(key_of[0], (SEQS, LENGTH, D), 1.0, 6.0, ((0, 4), (1, 32)))
    block_order = draw_block_order(jax.random.fold_in(key_of[16], 71), 0)
    cotangent = noise(key_of[2], (SEQS, LENGTH, D), 1.0, 6.0, ((0, 4), (1, 32)))
    ln1_gain = jnp.clip(1.0 + 0.1 * jax.random.normal(key_of[3], (D,), jnp.float32), 0.5, 1.5).astype(jnp.bfloat16)
    ln1_bias = noise(key_of[4], (D,), 0.2, 1.25, ((0, 4),))
    w_qkv = noise(key_of[5], (D, 3 * D), D ** -0.5, 0.15625, ((0, 4),))
    bias_q = noise(key_of[6], (D,), 0.2, 1.25, ((0, 4),))
    bias_v = noise(key_of[7], (D,), 0.2, 1.25, ((0, 4),))
    w_out = noise(key_of[8], (D, D), (max(1, 16 * D // LENGTH)) ** -0.5, 2.5, ((0, 4),))
    bias_out = noise(key_of[9], (D,), 0.2, 1.25, ((0, 4),))
    ln2_gain = jnp.clip(1.0 + 0.1 * jax.random.normal(key_of[10], (D,), jnp.float32), 0.5, 1.5).astype(jnp.bfloat16)
    ln2_bias = noise(key_of[11], (D,), 0.2, 1.25, ((0, 4),))
    w_fc = noise(key_of[12], (D, FF), D ** -0.5, 0.15625, ((0, 4),))
    bias_fc = noise(key_of[13], (FF,), 0.2, 1.25, ((0, 4),))
    w_proj = noise(key_of[14], (FF, D), FF ** -0.5, 0.078125, ((0, 4),))
    bias_proj = noise(key_of[15], (D,), 0.2, 1.25, ((0, 4),))
    return {"inputs": inputs, "block_order": block_order, "cotangent": cotangent, "ln1_gain": ln1_gain, "ln1_bias": ln1_bias, "w_qkv": w_qkv, "bias_q": bias_q, "bias_v": bias_v, "w_out": w_out, "bias_out": bias_out, "ln2_gain": ln2_gain, "ln2_bias": ln2_bias, "w_fc": w_fc, "bias_fc": bias_fc, "w_proj": w_proj, "bias_proj": bias_proj}


EPS = 1e-05
NEG = -1e+30
HIGH = lax.Precision.HIGHEST

@jax.custom_vjp
def low(v):
    return lax.optimization_barrier(v.astype(jnp.bfloat16)).astype(jnp.float32)

@jax.custom_vjp
def low_back(v):
    return v

def low_keep(v):
    return (low(v), None)

def low_pass(kept, grad):
    return (grad,)

def back_keep(v):
    return (v, None)

def back_low(kept, grad):
    return (low(grad),)
low.defvjp(low_keep, low_pass)
low_back.defvjp(back_keep, back_low)

def layer_norm(values, gain_row, shift_row):
    centered = values - lax.optimization_barrier(jnp.mean(values, axis=-1, keepdims=True))
    variance = lax.optimization_barrier(jnp.mean(centered * centered, axis=-1, keepdims=True))
    return centered * lax.rsqrt(variance + EPS) * gain_row + shift_row

def matmul(left, right):
    return jnp.einsum('td,df->tf', left, right, precision=HIGH)

def attend(query, key_rows, value_rows, places):
    length = query.shape[0]
    block_rows = min(512, length)
    scale = HEAD_DIM ** (-0.5)
    query_heads = query.reshape(length // block_rows, block_rows, HEADS, HEAD_DIM)
    key_heads = key_rows.reshape(length, HEADS, HEAD_DIM)
    value_heads = value_rows.reshape(length, HEADS, HEAD_DIM)

    def one_block(block_item):
        query_part, place_part = block_item
        scores = jnp.einsum('qhd,khd->hqk', query_part, key_heads, precision=HIGH) * scale
        visible = places[None, :] <= place_part[:, None]
        scores = low_back(jnp.where(visible[None], scores, NEG))
        attn_weights = jax.nn.softmax(scores, axis=-1)
        return jnp.einsum('hqk,khd->qhd', low(attn_weights), value_heads, precision=HIGH)
    result = lax.map(jax.checkpoint(one_block), (query_heads, places.reshape(length // block_rows, block_rows)))
    return result.reshape(length, HEADS * HEAD_DIM)

def forward(tokens, places, ln1_gain, ln1_bias, w_qkv, bias_q, bias_v, w_out, bias_out, ln2_gain, ln2_bias, w_fc, bias_fc, w_proj, bias_proj):
    normed_one = low(layer_norm(tokens, ln1_gain, ln1_bias))
    projected = matmul(normed_one, w_qkv)
    query = low_back(low(projected[:, :D] + bias_q))
    key_rows = low_back(low(projected[:, D:2 * D]))
    value_rows = low_back(low(projected[:, 2 * D:] + bias_v))
    attended = low_back(low(attend(query, key_rows, value_rows, places)))
    middle = tokens + low_back(matmul(attended, w_out) + bias_out)
    normed_two = low(layer_norm(middle, ln2_gain, ln2_bias))
    hidden_pre = low_back(matmul(normed_two, w_fc) + bias_fc)
    hidden_low = low(jax.nn.gelu(hidden_pre, approximate=True))
    return middle + low_back(matmul(hidden_low, w_proj) + bias_proj)

def reference(inputs, block_order, cotangent, ln1_gain, ln1_bias, w_qkv, bias_q, bias_v, w_out, bias_out, ln2_gain, ln2_bias, w_fc, bias_fc, w_proj, bias_proj):
    params = tuple((member.astype(jnp.float32) for member in (ln1_gain, ln1_bias, w_qkv, bias_q, bias_v, w_out, bias_out, ln2_gain, ln2_bias, w_fc, bias_fc, w_proj, bias_proj)))
    row_ids = jnp.arange(LENGTH).astype(jnp.int32)
    places = (block_order[:, row_ids // BLK] * BLK + row_ids % BLK).astype(jnp.int32)

    def per_sequence(totals, sequence_item):
        tokens, upstream, place_row = sequence_item
        result, pullback = jax.vjp(lambda token_rows, *weights: forward(token_rows, place_row, *weights), tokens, *params)
        gradients = pullback(upstream)
        summed = tuple((earlier + added for earlier, added in zip(totals, gradients[1:])))
        return (summed, (result.astype(jnp.bfloat16), gradients[0]))
    start_totals = tuple((jnp.zeros_like(member) for member in params))
    totals, (outputs, input_grads) = lax.scan(per_sequence, start_totals, (inputs.astype(jnp.float32), cotangent.astype(jnp.float32), places))
    return (outputs, input_grads, totals[0], totals[1], totals[2], totals[3], totals[4], totals[5], totals[6], totals[7], totals[8], totals[9], totals[10], totals[11], totals[12])
```

```python
import math

import jax
import jax.numpy as jnp
from jax import lax
from jax.experimental import pallas as pl
from jax.experimental.pallas import tpu as pltpu
from jax.sharding import PartitionSpec as P

HEADS = 25
HEAD_DIM = 64
GROUP = 7
SPAN = GROUP * HEAD_DIM
EPS = 1e-05
MESH = pl.DeviceIdType.MESH
NEG = -1e30
LOG2E = 1.4426950408889634

def attend_forward(received, inverse, place, block):
    parts, wide, rows = received.shape
    dim = wide // 3
    per = block // rows
    count = parts // per

    def kernel(inverse_ref, place_ref, in_ref, out_ref, q_ref, kt_ref, vt_ref, k_ref, v_ref, att_ref, lse_ref):
        def arrange(index, carry):
            for sub in range(per):
                piece = in_ref[inverse_ref[index * per + sub]]
                lanes = pl.ds(sub * rows, rows)
                q_ref[index, :, lanes] = piece[:dim]
                kt_ref[index, :, lanes] = piece[dim : 2 * dim]
                vt_ref[index, :, lanes] = piece[2 * dim :]
                k_ref[index, lanes, :] = piece[dim : 2 * dim].T
                v_ref[index, lanes, :] = piece[2 * dim :].T
            return carry

        lax.fori_loop(0, count, arrange, 0)
        row = lax.broadcasted_iota(jnp.int32, (block, block), 0)
        col = lax.broadcasted_iota(jnp.int32, (block, block), 1)
        factor = LOG2E * dim**-0.5

        def step(qi, kj, carry, diagonal):
            peak, mass, total = carry
            scores = jnp.dot(k_ref[kj], q_ref[qi], preferred_element_type=jnp.float32) * factor
            if diagonal:
                scores = jnp.where(row <= col, scores, NEG)
            new_peak = jnp.maximum(peak, jnp.max(scores, axis=0, keepdims=True))
            weights = jnp.exp2(scores - new_peak)
            shrink = jnp.exp2(peak - new_peak)
            mass = mass * shrink + jnp.sum(weights, axis=0, keepdims=True)
            total = total * shrink + jnp.dot(
                vt_ref[kj], weights.astype(jnp.bfloat16), preferred_element_type=jnp.float32
            )
            return (new_peak, mass, total)

        def query_block(qi, carry):
            start = (
                jnp.full((1, block), NEG, jnp.float32),
                jnp.zeros((1, block), jnp.float32),
                jnp.zeros((dim, block), jnp.float32),
            )
            state = lax.fori_loop(0, qi, lambda kj, cur: step(qi, kj, cur, False), start)
            peak, mass, total = step(qi, qi, state, True)
            att_ref[qi] = total / mass
            lse_ref[qi] = peak + jnp.log2(mass)
            return carry

        lax.fori_loop(0, count, query_block, 0)

        def give_back(index, carry):
            where = place_ref[index]
            whole = att_ref[where // per]
            picked = whole[:, :rows]
            for sub in range(1, per):
                picked = jnp.where(where % per == sub, whole[:, sub * rows : (sub + 1) * rows], picked)
            out_ref[index] = picked.astype(jnp.bfloat16)
            return carry

        lax.fori_loop(0, parts, give_back, 0)

    smem = pl.BlockSpec(memory_space=pltpu.SMEM)
    vmem = pl.BlockSpec(memory_space=pltpu.VMEM)
    lane_first = jax.ShapeDtypeStruct((count, dim, block), jnp.bfloat16)
    row_first = jax.ShapeDtypeStruct((count, block, dim), jnp.bfloat16)
    return pl.pallas_call(
        kernel,
        out_shape=(
            jax.ShapeDtypeStruct((parts, dim, rows), jnp.bfloat16),
            lane_first, lane_first, lane_first, row_first, row_first,
            jax.ShapeDtypeStruct((count, dim, block), jnp.float32),
            jax.ShapeDtypeStruct((count, 1, block), jnp.float32),
        ),
        in_specs=[smem, smem, vmem],
        out_specs=(vmem,) * 8,
        compiler_params=pltpu.CompilerParams(vmem_limit_bytes=40 * 2**20),
        name="attend_forward",
    )(inverse, place, received)


def attend_backward(upstream, inverse, place, saved, block):
    parts, dim, rows = upstream.shape
    per = block // rows
    count = parts // per
    q, kt, vt, k, v, attended, lse = saved

    def kernel(inverse_ref, place_ref, up_ref, q_ref, kt_ref, k_ref, v_ref, att_ref, lse_ref, out_ref, up_sorted, up_rows, q_rows, delta_ref, gq_ref, gk_ref, gv_ref):
        def arrange(index, carry):
            for sub in range(per):
                piece = up_ref[inverse_ref[index * per + sub]]
                lanes = pl.ds(sub * rows, rows)
                up_sorted[index, :, lanes] = piece
                up_rows[index, lanes, :] = piece.T
            q_rows[index] = q_ref[index].T
            delta_ref[index] = jnp.sum(up_sorted[index].astype(jnp.float32) * att_ref[index], axis=0, keepdims=True)
            gk_ref[index] = jnp.zeros((block, dim), jnp.float32)
            gv_ref[index] = jnp.zeros((block, dim), jnp.float32)
            return carry

        lax.fori_loop(0, count, arrange, 0)
        row = lax.broadcasted_iota(jnp.int32, (block, block), 0)
        col = lax.broadcasted_iota(jnp.int32, (block, block), 1)
        factor = LOG2E * dim**-0.5

        def step(qi, kj, total, diagonal):
            scores = jnp.dot(k_ref[kj], q_ref[qi], preferred_element_type=jnp.float32) * factor
            weights = jnp.exp2(scores - lse_ref[qi])
            if diagonal:
                weights = jnp.where(row <= col, weights, 0.0)
            prob_grad = jnp.dot(v_ref[kj], up_sorted[qi], preferred_element_type=jnp.float32)
            score_grad = (weights * (prob_grad - delta_ref[qi])).astype(jnp.bfloat16)
            gv_ref[kj] += jnp.dot(weights.astype(jnp.bfloat16), up_rows[qi], preferred_element_type=jnp.float32)
            gk_ref[kj] += jnp.dot(score_grad, q_rows[qi], preferred_element_type=jnp.float32)
            return total + jnp.dot(kt_ref[kj], score_grad, preferred_element_type=jnp.float32)

        def query_block(qi, carry):
            total = lax.fori_loop(
                0, qi, lambda kj, cur: step(qi, kj, cur, False), jnp.zeros((dim, block), jnp.float32)
            )
            gq_ref[qi] = step(qi, qi, total, True) * dim**-0.5
            return carry

        lax.fori_loop(0, count, query_block, 0)

        def give_back(index, carry):
            where = place_ref[index]
            hold = where // per
            off = where % per
            whole = gq_ref[hold]
            picked = whole[:, :rows]
            for sub in range(1, per):
                picked = jnp.where(off == sub, whole[:, sub * rows : (sub + 1) * rows], picked)
            out_ref[index, :dim] = picked.astype(jnp.bfloat16)
            line = pl.ds(pl.multiple_of(off * rows, rows), rows)
            out_ref[index, dim : 2 * dim] = (gk_ref[hold, line, :] * dim**-0.5).T.astype(jnp.bfloat16)
            out_ref[index, 2 * dim :] = gv_ref[hold, line, :].T.astype(jnp.bfloat16)
            return carry

        lax.fori_loop(0, parts, give_back, 0)

    smem = pl.BlockSpec(memory_space=pltpu.SMEM)
    vmem = pl.BlockSpec(memory_space=pltpu.VMEM)
    return pl.pallas_call(
        kernel,
        out_shape=jax.ShapeDtypeStruct((parts, 3 * dim, rows), jnp.bfloat16),
        in_specs=[smem, smem] + [vmem] * 7,
        out_specs=vmem,
        scratch_shapes=[
            pltpu.VMEM((count, dim, block), jnp.bfloat16),
            pltpu.VMEM((count, block, dim), jnp.bfloat16),
            pltpu.VMEM((count, block, dim), jnp.bfloat16),
            pltpu.VMEM((count, 1, block), jnp.float32),
            pltpu.VMEM((count, dim, block), jnp.float32),
            pltpu.VMEM((count, block, dim), jnp.float32),
            pltpu.VMEM((count, block, dim), jnp.float32),
        ],
        compiler_params=pltpu.CompilerParams(vmem_limit_bytes=40 * 2**20),
        name="attend_backward",
    )(inverse, place, upstream, q, kt, k, v, attended, lse)


def layer_norm(values, gain_row, shift_row):
    centered = values - jnp.mean(values, axis=-1, keepdims=True)
    variance = jnp.mean(centered * centered, axis=-1, keepdims=True)
    return centered * lax.rsqrt(variance + EPS) * gain_row + shift_row


def gelu_tanh(values):
    return jax.nn.gelu(values, approximate=True)


def dot(left, right, left_dim=1, right_dim=0):
    return lax.dot_general(
        left, right, (((left_dim,), (right_dim,)), ((), ())), preferred_element_type=jnp.float32
    )


def greet(peers):
    barrier = pltpu.get_barrier_semaphore()
    for peer in peers:
        pl.semaphore_signal(barrier, inc=1, device_id=peer, device_id_type=MESH)
    pl.semaphore_wait(barrier, len(peers))


def gather_wt(arrays, collective):
    count = len(arrays)

    def kernel(*refs):
        sources, targets = refs[:count], refs[count : 2 * count]
        send, receive, local = refs[2 * count :]
        ctx, wt = lax.axis_index("ctx"), lax.axis_index("wt")
        near, far = (ctx, wt ^ 1), (ctx, wt ^ 2)
        greet((near, far))

        def move(item, step, source, slot, peer):
            return pltpu.make_async_remote_copy(
                source, targets[item].at[slot], send.at[item, step], receive.at[item, step],
                device_id=peer, device_id_type=MESH,
            )

        firsts = [move(item, 0, sources[item], wt, far) for item in range(count)]
        for copy in firsts:
            copy.start()
        seconds = [move(item, 1, sources[item], wt, near) for item in range(count)]
        own = [
            pltpu.make_async_copy(sources[item], targets[item].at[wt], local.at[item])
            for item in range(count)
        ]
        for copy in seconds + own:
            copy.start()
        thirds = []
        for item in range(count):
            firsts[item].wait_recv()
            copy = move(item, 2, targets[item].at[wt ^ 2], wt ^ 2, near)
            copy.start()
            thirds.append(copy)
        for copy in firsts:
            copy.wait_send()
        for copy in seconds + thirds + own:
            copy.wait()

    hbm = pl.BlockSpec(memory_space=pl.ANY)
    return pl.pallas_call(
        kernel,
        out_shape=tuple(jax.ShapeDtypeStruct((4,) + member.shape, member.dtype) for member in arrays),
        in_specs=[hbm] * count,
        out_specs=(hbm,) * count,
        scratch_shapes=[
            pltpu.SemaphoreType.DMA((count, 3)),
            pltpu.SemaphoreType.DMA((count, 3)),
            pltpu.SemaphoreType.DMA((count,)),
        ],
        compiler_params=pltpu.CompilerParams(collective_id=collective, has_side_effects=True),
        name="gather_wt",
    )(*arrays)


def scatter_wt(parts, collective):
    count = len(parts)
    extents = [member.shape[1:] for member in parts]

    def kernel(*refs):
        terms, sums = refs[:count], refs[count : 2 * count]
        bufs = refs[2 * count : 3 * count]
        send, receive = refs[3 * count :]
        ctx, wt = lax.axis_index("ctx"), lax.axis_index("wt")
        near, far = (ctx, wt ^ 1), (ctx, wt ^ 2)
        greet((near, far))

        def move(item, step, source, target, peer):
            return pltpu.make_async_remote_copy(
                bufs[item].at[source], bufs[item].at[target], send.at[item, step], receive.at[item, step],
                device_id=peer, device_id_type=MESH,
            )

        waits = []
        for item in range(count):
            bufs[item][0] = terms[item][wt ^ 3].astype(jnp.bfloat16)
            copy = move(item, 0, 0, 3, near)
            copy.start()
            waits.append(copy)
        rests = []
        for item in range(count):
            bufs[item][1] = terms[item][wt ^ 1].astype(jnp.bfloat16)
            copy = move(item, 1, 1, 4, near)
            copy.start()
            rests.append(copy)
        lasts = []
        for item in range(count):
            waits[item].wait_recv()
            bufs[item][2] = (terms[item][wt ^ 2] + bufs[item][3].astype(jnp.float32)).astype(jnp.bfloat16)
            copy = move(item, 2, 2, 5, far)
            copy.start()
            lasts.append(copy)
        for item in range(count):
            rests[item].wait_recv()
            sums[item][...] = terms[item][wt] + bufs[item][4].astype(jnp.float32)
        for item in range(count):
            lasts[item].wait_recv()
            sums[item][...] += bufs[item][5].astype(jnp.float32)
        for copy in waits + rests + lasts:
            copy.wait_send()

    vmem = pl.BlockSpec(memory_space=pltpu.VMEM)
    return pl.pallas_call(
        kernel,
        out_shape=tuple(jax.ShapeDtypeStruct(extent, jnp.float32) for extent in extents),
        in_specs=[vmem] * count,
        out_specs=(vmem,) * count,
        scratch_shapes=[pltpu.VMEM((6,) + extent, jnp.bfloat16) for extent in extents]
        + [pltpu.SemaphoreType.DMA((count, 3)), pltpu.SemaphoreType.DMA((count, 3))],
        compiler_params=pltpu.CompilerParams(
            collective_id=collective, has_side_effects=True, vmem_limit_bytes=40 * 2**20
        ),
        name="scatter_wt",
    )(*parts)


def exchange(blocks, axis, collective):
    count = blocks.shape[0]

    def kernel(source, target, send, receive, local):
        ctx, wt = lax.axis_index("ctx"), lax.axis_index("wt")
        own = ctx if axis == "ctx" else wt

        def peer(step):
            other = lax.rem(own + step, count)
            return other, ((other, wt) if axis == "ctx" else (ctx, other))

        barrier = pltpu.get_barrier_semaphore()

        def signal(step, carry):
            pl.semaphore_signal(barrier, inc=1, device_id=peer(step)[1], device_id_type=MESH)
            return carry

        lax.fori_loop(1, count, signal, 0)
        pl.semaphore_wait(barrier, count - 1)

        def move(step):
            other, device = peer(step)
            return pltpu.make_async_remote_copy(
                source.at[other], target.at[own], send.at[step], receive.at[step],
                device_id=device, device_id_type=MESH,
            )

        def begin(step, carry):
            move(step).start()
            return carry

        def finish(step, carry):
            move(step).wait()
            return carry

        lax.fori_loop(1, count, begin, 0)
        keep = pltpu.make_async_copy(source.at[own], target.at[own], local)
        keep.start()
        keep.wait()
        lax.fori_loop(1, count, finish, 0)

    hbm = pl.BlockSpec(memory_space=pl.ANY)
    return pl.pallas_call(
        kernel,
        out_shape=jax.ShapeDtypeStruct(blocks.shape, blocks.dtype),
        in_specs=[hbm],
        out_specs=hbm,
        scratch_shapes=[
            pltpu.SemaphoreType.DMA((count,)),
            pltpu.SemaphoreType.DMA((count,)),
            pltpu.SemaphoreType.DMA,
        ],
        compiler_params=pltpu.CompilerParams(collective_id=collective, has_side_effects=True),
        name="exchange_" + axis,
    )(blocks)


def swap_wt(blocks):
    wt = lax.axis_index("wt")
    kept = lax.dynamic_index_in_dim(blocks, wt, 0, keepdims=False)
    result = jnp.zeros_like(blocks)
    result = lax.dynamic_update_index_in_dim(result, kept, wt, 0)
    for step in (1, 2, 3):
        piece = lax.dynamic_index_in_dim(blocks, wt ^ step, 0, keepdims=False)
        piece = lax.ppermute(piece, "wt", [(source, source ^ step) for source in range(4)])
        result = lax.dynamic_update_index_in_dim(result, piece, wt ^ step, 0)
    return result


def to_heads(rows_by_token):
    parts = rows_by_token.shape[0] // SPAN
    rows = rows_by_token.shape[1] // 4
    blocks = rows_by_token.reshape(parts, GROUP, HEAD_DIM, 4, rows).transpose(3, 1, 0, 2, 4)
    blocks = blocks.reshape(4 * GROUP, parts * HEAD_DIM, rows)
    spare = lax.axis_size("ctx") - 4 * GROUP
    return jnp.concatenate([blocks, jnp.zeros((spare,) + blocks.shape[1:], blocks.dtype)])


def from_heads(blocks):
    parts, rows = blocks.shape[1] // HEAD_DIM, blocks.shape[2]
    used = blocks[: 4 * GROUP].reshape(4, GROUP, parts, HEAD_DIM, rows)
    return used.transpose(2, 1, 3, 0, 4).reshape(parts * SPAN, 4 * rows)


def local(
    inputs,
    block_order,
    cotangent,
    ln1_gain,
    ln1_bias,
    w_qkv,
    bias_q,
    bias_v,
    w_out,
    bias_out,
    ln2_gain,
    ln2_bias,
    w_fc,
    bias_fc,
    w_proj,
    bias_proj,
):
    ctx, wt = lax.axis_index("ctx"), lax.axis_index("wt")
    ctx_count = lax.axis_size("ctx")
    rows, features = inputs.shape[1:]
    share = features // 4
    shift = 16 * wt

    small = jnp.stack([ln1_gain, ln1_bias, bias_q, bias_v, bias_out, ln2_gain, ln2_bias, bias_proj])
    small = jnp.pad(small, ((0, 8), (0, 0)))
    order = jnp.pad(block_order, ((0, 7), (0, 128 - ctx_count)))
    all_inputs, all_small, all_order, all_cot = gather_wt((inputs[0], small, order, cotangent[0]), 1)
    vectors = all_small[:, :8].transpose(1, 0, 2).reshape(8, features).astype(jnp.float32)
    gain_one, shift_one, full_bq, full_bv, full_bout, gain_two, shift_two, full_bproj = vectors
    orders = all_order[:, 0, :ctx_count]
    place = lax.dynamic_index_in_dim(orders, jnp.minimum(ctx // GROUP, 3), 0, keepdims=False)
    slots = jnp.arange(ctx_count, dtype=jnp.int32)
    inverse = jnp.sum(jnp.where(place[None, :] == slots[:, None], slots[None, :], 0), axis=1)

    starts = [384 * member for member in range(4)]
    columns = jnp.stack(
        [
            jnp.concatenate(
                [w_qkv[:, part * features + start : part * features + start + SPAN] for part in range(3)],
                axis=1,
            )
            for start in starts
        ]
    )
    own_qkv = exchange(columns, "wt", 2).reshape(features, 3 * SPAN)
    own_fc = swap_wt(w_fc.reshape(share, 4, -1).transpose(1, 0, 2)).reshape(features, -1)
    edge = SPAN - share
    below = lax.ppermute(w_out[share - edge :], "wt", [(source, (source + 1) % 4) for source in range(4)])
    above = lax.ppermute(w_out[:edge], "wt", [(source, (source - 1) % 4) for source in range(4)])
    wide_out = lax.dynamic_slice_in_dim(jnp.concatenate([below, w_out, above]), edge - shift, SPAN, 0)
    span_ids = jnp.arange(SPAN, dtype=jnp.int32)
    mine = (span_ids >= shift) & (span_ids < shift + share)
    masked_out = jnp.where(mine[:, None], wide_out, 0)

    group_tokens = all_inputs.reshape(4 * rows, features).astype(jnp.float32)
    normed_one = layer_norm(group_tokens, gain_one, shift_one).astype(jnp.bfloat16)
    bias_cols = jnp.concatenate(
        [
            lax.dynamic_slice_in_dim(full_bq, 384 * wt, SPAN),
            jnp.zeros((SPAN,), jnp.float32),
            lax.dynamic_slice_in_dim(full_bv, 384 * wt, SPAN),
        ]
    )
    projected = (dot(own_qkv, normed_one, 0, 1) + bias_cols[:, None]).astype(jnp.bfloat16)
    received = exchange(to_heads(projected), "ctx", 3)
    block = math.gcd(512, ctx_count * rows)
    attended_blocks, *saved = attend_forward(received, inverse, place, block)
    attended = from_heads(exchange(attended_blocks, "ctx", 4))

    tokens = inputs[0].astype(jnp.float32)
    (branch,) = scatter_wt((dot(attended, masked_out, 0, 0).reshape(4, rows, features),), 5)
    middle = tokens + branch + full_bout
    normed_two = layer_norm(middle, gain_two, shift_two).astype(jnp.bfloat16)
    (all_two,) = gather_wt((normed_two,), 6)
    all_two = all_two.reshape(4 * rows, features)
    hidden_pre = dot(all_two, own_fc) + bias_fc.astype(jnp.float32)
    hidden_low = gelu_tanh(hidden_pre).astype(jnp.bfloat16)
    group_cot = all_cot.reshape(4 * rows, features)
    hidden_grad = dot(group_cot, w_proj, 1, 1)
    unused_gelu, gelu_back = jax.vjp(gelu_tanh, hidden_pre)
    pre_grad = gelu_back(hidden_grad)[0].astype(jnp.bfloat16)
    projected_out, normed_two_grad = scatter_wt(
        (
            dot(hidden_low, w_proj).reshape(4, rows, features),
            dot(pre_grad, own_fc, 1, 1).reshape(4, rows, features),
        ),
        7,
    )
    outputs = middle + projected_out + full_bproj
    unused_norm, norm_back = jax.vjp(layer_norm, middle, gain_two, shift_two)
    middle_part, grad_gain_two, grad_shift_two = norm_back(normed_two_grad)
    middle_grad = cotangent[0].astype(jnp.float32) + middle_part
    branch_grad = middle_grad.astype(jnp.bfloat16)
    (all_branch,) = gather_wt((branch_grad,), 8)
    all_branch = all_branch.reshape(4 * rows, features)

    attended_grad = dot(wide_out, all_branch, 1, 1).astype(jnp.bfloat16)
    upstream = exchange(to_heads(attended_grad), "ctx", 9)
    grad_blocks = attend_backward(upstream, inverse, place, saved, block)
    stacked = from_heads(exchange(grad_blocks, "ctx", 10))
    masked = jnp.where(jnp.tile(mine, 3)[:, None], stacked, 0)
    (normed_one_grad,) = scatter_wt((dot(masked, own_qkv, 0, 1).reshape(4, rows, features),), 11)
    unused_first, first_back = jax.vjp(layer_norm, tokens, gain_one, shift_one)
    input_part, grad_gain_one, grad_shift_one = first_back(normed_one_grad)
    input_grad = middle_grad + input_part

    low = jnp.bfloat16
    own_stacked = lax.dynamic_slice_in_dim(stacked.reshape(3, SPAN, -1), shift, share, 1)
    own_attended = lax.dynamic_slice_in_dim(attended, shift, share, 0)
    grad_proj = dot(hidden_low, group_cot, 0, 0).astype(low)
    grad_fc = dot(pre_grad, all_two, 0, 0).astype(low)
    grad_qkv = dot(own_stacked.reshape(3 * share, -1), normed_one).astype(low)
    grad_out = dot(own_attended, all_branch).astype(low)
    column = lambda value: lax.dynamic_slice_in_dim(value, share * wt, share, 0)
    sums = jnp.sum(own_stacked.astype(jnp.float32), axis=2)
    grad_bout = column(jnp.sum(all_branch.astype(jnp.float32), axis=0))
    grad_bproj = column(jnp.sum(group_cot.astype(jnp.float32), axis=0))
    grad_bfc = jnp.sum(pre_grad.astype(jnp.float32), axis=0)
    crossed_vectors = jnp.stack([grad_gain_one, grad_shift_one, grad_gain_two, grad_shift_two]).astype(low)
    kept_vectors = jnp.stack([jnp.concatenate([sums[0], sums[2], grad_bout, grad_bproj]), grad_bfc]).astype(low)
    pad = lambda value, extent: jnp.pad(value, ((0, extent - value.shape[0]), (0, 0)))
    crossed = pad(jnp.concatenate([grad_fc, grad_qkv, crossed_vectors]), 96 * ctx_count)
    kept = pad(jnp.concatenate([grad_proj, grad_out, kept_vectors]), 64 * ctx_count)
    crossed_chunk = lax.psum_scatter(crossed, "ctx", scatter_dimension=0, tiled=True)
    kept_chunk = lax.psum_scatter(kept, "ctx", scatter_dimension=0, tiled=True)
    crossed_chunk = exchange(crossed_chunk.reshape(96, 4, share).transpose(1, 0, 2), "wt", 12)
    crossed_all = lax.all_gather(crossed_chunk, "ctx", axis=1, tiled=True).astype(jnp.float32)
    kept_all = lax.all_gather(kept_chunk, "ctx", axis=0, tiled=True).astype(jnp.float32)
    ff = grad_fc.shape[0]
    sum_fc = crossed_all[:, :ff].transpose(2, 0, 1).reshape(share, 4 * ff)
    sum_qkv = crossed_all[:, ff : ff + 3 * share].reshape(4, 3, share, share)
    sum_qkv = sum_qkv.transpose(3, 1, 0, 2).reshape(share, 3 * features)
    norms = jnp.sum(crossed_all[:, ff + 3 * share : ff + 3 * share + 4], axis=0)
    sum_proj, sum_out = kept_all[:ff], kept_all[ff : ff + share]
    kept_sums = kept_all[ff + share : ff + share + 2]
    sum_bq, sum_bv, sum_bout, sum_bproj = kept_sums[0].reshape(4, share)
    return (
        outputs.astype(jnp.bfloat16)[None],
        input_grad[None],
        norms[0],
        norms[1],
        sum_qkv,
        sum_bq,
        sum_bv,
        sum_out,
        sum_bout,
        norms[2],
        norms[3],
        sum_fc,
        kept_sums[1],
        sum_proj,
        sum_bproj,
    )


def solution(mesh):
    placed = (
        P("wt", "ctx", None),
        P("wt", None),
        P("wt", "ctx", None),
        P("wt"),
        P("wt"),
        P("wt", None),
        P("wt"),
        P("wt"),
        P("wt", None),
        P("wt"),
        P("wt"),
        P("wt"),
        P("wt", None),
        P("wt"),
        P("wt", None),
        P("wt"),
    )
    return jax.shard_map(
        local,
        mesh=mesh,
        in_specs=placed,
        out_specs=(
            P("wt", "ctx", None),
            P("wt", "ctx", None),
            P("wt"),
            P("wt"),
            P("wt", None),
            P("wt"),
            P("wt"),
            P("wt", None),
            P("wt"),
            P("wt"),
            P("wt"),
            P("wt", None),
            P("wt"),
            P("wt", None),
            P("wt"),
        ),
        check_vma=False,
    )
```

```python
import math

import jax
import jax.numpy as jnp
from jax import lax
from jax.experimental import pallas as pl
from jax.experimental.pallas import tpu as pltpu
from jax.sharding import PartitionSpec as P

HEADS = 25
HEAD_DIM = 64
GROUP = 7
SPAN = GROUP * HEAD_DIM
EPS = 1e-05
MESH = pl.DeviceIdType.MESH


def cost(micros):
    return pl.CostEstimate(flops=int(micros * 1e9), bytes_accessed=int(micros * 1e6), transcendentals=0)
NEG = -1e30
LOG2E = 1.4426950408889634

def attend_forward(received, inverse, place, block):
    parts, wide, rows = received.shape
    dim = wide // 3
    per = block // rows
    count = parts // per

    def kernel(inverse_ref, place_ref, in_ref, out_ref, q_ref, kt_ref, vt_ref, k_ref, v_ref, att_ref, lse_ref):
        def arrange(index, carry):
            for sub in range(per):
                piece = in_ref[inverse_ref[index * per + sub]]
                lanes = pl.ds(sub * rows, rows)
                q_ref[index, :, lanes] = piece[:dim]
                kt_ref[index, :, lanes] = piece[dim : 2 * dim]
                vt_ref[index, :, lanes] = piece[2 * dim :]
                k_ref[index, lanes, :] = piece[dim : 2 * dim].T
                v_ref[index, lanes, :] = piece[2 * dim :].T
            return carry

        lax.fori_loop(0, count, arrange, 0)
        row = lax.broadcasted_iota(jnp.int32, (block, block), 0)
        col = lax.broadcasted_iota(jnp.int32, (block, block), 1)
        factor = LOG2E * dim**-0.5

        def step(qi, kj, carry, diagonal):
            peak, mass, total = carry
            scores = jnp.dot(k_ref[kj], q_ref[qi], preferred_element_type=jnp.float32) * factor
            if diagonal:
                scores = jnp.where(row <= col, scores, NEG)
            new_peak = jnp.maximum(peak, jnp.max(scores, axis=0, keepdims=True))
            weights = jnp.exp2(scores - new_peak)
            shrink = jnp.exp2(peak - new_peak)
            mass = mass * shrink + jnp.sum(weights, axis=0, keepdims=True)
            total = total * shrink + jnp.dot(
                vt_ref[kj], weights.astype(jnp.bfloat16), preferred_element_type=jnp.float32
            )
            return (new_peak, mass, total)

        def query_block(qi, carry):
            start = (
                jnp.full((1, block), NEG, jnp.float32),
                jnp.zeros((1, block), jnp.float32),
                jnp.zeros((dim, block), jnp.float32),
            )
            state = lax.fori_loop(0, qi, lambda kj, cur: step(qi, kj, cur, False), start)
            peak, mass, total = step(qi, qi, state, True)
            att_ref[qi] = total / mass
            lse_ref[qi] = peak + jnp.log2(mass)
            return carry

        lax.fori_loop(0, count, query_block, 0)

        def give_back(index, carry):
            where = place_ref[index]
            whole = att_ref[where // per]
            picked = whole[:, :rows]
            for sub in range(1, per):
                picked = jnp.where(where % per == sub, whole[:, sub * rows : (sub + 1) * rows], picked)
            out_ref[index] = picked.astype(jnp.bfloat16)
            return carry

        lax.fori_loop(0, parts, give_back, 0)

    smem = pl.BlockSpec(memory_space=pltpu.SMEM)
    vmem = pl.BlockSpec(memory_space=pltpu.VMEM)
    lane_first = jax.ShapeDtypeStruct((count, dim, block), jnp.bfloat16)
    row_first = jax.ShapeDtypeStruct((count, block, dim), jnp.bfloat16)
    return pl.pallas_call(
        kernel,
        out_shape=(
            jax.ShapeDtypeStruct((parts, dim, rows), jnp.bfloat16),
            lane_first, lane_first, lane_first, row_first, row_first,
            jax.ShapeDtypeStruct((count, dim, block), jnp.float32),
            jax.ShapeDtypeStruct((count, 1, block), jnp.float32),
        ),
        in_specs=[smem, smem, vmem],
        out_specs=(vmem,) * 8,
        compiler_params=pltpu.CompilerParams(vmem_limit_bytes=40 * 2**20),
        name="attend_forward",
    )(inverse, place, received)


def attend_backward(upstream, inverse, place, saved, block):
    parts, dim, rows = upstream.shape
    per = block // rows
    count = parts // per
    q, kt, vt, k, v, attended, lse = saved

    def kernel(inverse_ref, place_ref, up_ref, q_ref, kt_ref, k_ref, v_ref, att_ref, lse_ref, out_ref, up_sorted, up_rows, q_rows, delta_ref, gq_ref, gk_ref, gv_ref):
        def arrange(index, carry):
            for sub in range(per):
                piece = up_ref[inverse_ref[index * per + sub]]
                lanes = pl.ds(sub * rows, rows)
                up_sorted[index, :, lanes] = piece
                up_rows[index, lanes, :] = piece.T
            q_rows[index] = q_ref[index].T
            delta_ref[index] = jnp.sum(up_sorted[index].astype(jnp.float32) * att_ref[index], axis=0, keepdims=True)
            gk_ref[index] = jnp.zeros((block, dim), jnp.float32)
            gv_ref[index] = jnp.zeros((block, dim), jnp.float32)
            return carry

        lax.fori_loop(0, count, arrange, 0)
        row = lax.broadcasted_iota(jnp.int32, (block, block), 0)
        col = lax.broadcasted_iota(jnp.int32, (block, block), 1)
        factor = LOG2E * dim**-0.5

        def step(qi, kj, total, diagonal):
            scores = jnp.dot(k_ref[kj], q_ref[qi], preferred_element_type=jnp.float32) * factor
            weights = jnp.exp2(scores - lse_ref[qi])
            if diagonal:
                weights = jnp.where(row <= col, weights, 0.0)
            prob_grad = jnp.dot(v_ref[kj], up_sorted[qi], preferred_element_type=jnp.float32)
            score_grad = (weights * (prob_grad - delta_ref[qi])).astype(jnp.bfloat16)
            gv_ref[kj] += jnp.dot(weights.astype(jnp.bfloat16), up_rows[qi], preferred_element_type=jnp.float32)
            gk_ref[kj] += jnp.dot(score_grad, q_rows[qi], preferred_element_type=jnp.float32)
            return total + jnp.dot(kt_ref[kj], score_grad, preferred_element_type=jnp.float32)

        def query_block(qi, carry):
            total = lax.fori_loop(
                0, qi, lambda kj, cur: step(qi, kj, cur, False), jnp.zeros((dim, block), jnp.float32)
            )
            gq_ref[qi] = step(qi, qi, total, True) * dim**-0.5
            return carry

        lax.fori_loop(0, count, query_block, 0)

        def give_back(index, carry):
            where = place_ref[index]
            hold = where // per
            off = where % per
            whole = gq_ref[hold]
            picked = whole[:, :rows]
            for sub in range(1, per):
                picked = jnp.where(off == sub, whole[:, sub * rows : (sub + 1) * rows], picked)
            out_ref[index, :dim] = picked.astype(jnp.bfloat16)
            line = pl.ds(pl.multiple_of(off * rows, rows), rows)
            out_ref[index, dim : 2 * dim] = (gk_ref[hold, line, :] * dim**-0.5).T.astype(jnp.bfloat16)
            out_ref[index, 2 * dim :] = gv_ref[hold, line, :].T.astype(jnp.bfloat16)
            return carry

        lax.fori_loop(0, parts, give_back, 0)

    smem = pl.BlockSpec(memory_space=pltpu.SMEM)
    vmem = pl.BlockSpec(memory_space=pltpu.VMEM)
    return pl.pallas_call(
        kernel,
        out_shape=jax.ShapeDtypeStruct((parts, 3 * dim, rows), jnp.bfloat16),
        in_specs=[smem, smem] + [vmem] * 7,
        out_specs=vmem,
        scratch_shapes=[
            pltpu.VMEM((count, dim, block), jnp.bfloat16),
            pltpu.VMEM((count, block, dim), jnp.bfloat16),
            pltpu.VMEM((count, block, dim), jnp.bfloat16),
            pltpu.VMEM((count, 1, block), jnp.float32),
            pltpu.VMEM((count, dim, block), jnp.float32),
            pltpu.VMEM((count, block, dim), jnp.float32),
            pltpu.VMEM((count, block, dim), jnp.float32),
        ],
        compiler_params=pltpu.CompilerParams(vmem_limit_bytes=40 * 2**20),
        name="attend_backward",
    )(inverse, place, upstream, q, kt, k, v, attended, lse)


def layer_norm(values, gain_row, shift_row):
    centered = values - jnp.mean(values, axis=-1, keepdims=True)
    variance = jnp.mean(centered * centered, axis=-1, keepdims=True)
    return centered * lax.rsqrt(variance + EPS) * gain_row + shift_row


def gelu_tanh(values):
    return jax.nn.gelu(values, approximate=True)


def dot(left, right, left_dim=1, right_dim=0):
    return lax.dot_general(
        left, right, (((left_dim,), (right_dim,)), ((), ())), preferred_element_type=jnp.float32
    )


def greet(peers):
    barrier = pltpu.get_barrier_semaphore()
    for peer in peers:
        pl.semaphore_signal(barrier, inc=1, device_id=peer, device_id_type=MESH)
    pl.semaphore_wait(barrier, len(peers))


def gather_wt(arrays, collective):
    count = len(arrays)

    def kernel(*refs):
        sources, targets = refs[:count], refs[count : 2 * count]
        send, receive, local = refs[2 * count :]
        ctx, wt = lax.axis_index("ctx"), lax.axis_index("wt")
        near, far = (ctx, wt ^ 1), (ctx, wt ^ 2)
        greet((near, far))

        def move(item, step, source, slot, peer):
            return pltpu.make_async_remote_copy(
                source, targets[item].at[slot], send.at[item, step], receive.at[item, step],
                device_id=peer, device_id_type=MESH,
            )

        firsts = [move(item, 0, sources[item], wt, far) for item in range(count)]
        for copy in firsts:
            copy.start()
        seconds = [move(item, 1, sources[item], wt, near) for item in range(count)]
        own = [
            pltpu.make_async_copy(sources[item], targets[item].at[wt], local.at[item])
            for item in range(count)
        ]
        for copy in seconds + own:
            copy.start()
        thirds = []
        for item in range(count):
            firsts[item].wait_recv()
            copy = move(item, 2, targets[item].at[wt ^ 2], wt ^ 2, near)
            copy.start()
            thirds.append(copy)
        for copy in firsts:
            copy.wait_send()
        for copy in seconds + thirds + own:
            copy.wait()

    hbm = pl.BlockSpec(memory_space=pl.ANY)
    return pl.pallas_call(
        kernel,
        out_shape=tuple(jax.ShapeDtypeStruct((4,) + member.shape, member.dtype) for member in arrays),
        in_specs=[hbm] * count,
        out_specs=(hbm,) * count,
        scratch_shapes=[
            pltpu.SemaphoreType.DMA((count, 3)),
            pltpu.SemaphoreType.DMA((count, 3)),
            pltpu.SemaphoreType.DMA((count,)),
        ],
        compiler_params=pltpu.CompilerParams(collective_id=collective, has_side_effects=True),
        name="gather_wt",
    )(*arrays)


def prologue(arrays, columns, collective):
    count = len(arrays)
    pieces = 5
    extent = columns.shape[1] // pieces

    def kernel(*refs):
        sources, (blocks,) = refs[:count], refs[count : count + 1]
        targets, (filled,) = refs[count + 1 : 2 * count + 1], refs[2 * count + 1 : 2 * count + 2]
        send, receive, local, cross_send, cross_receive, near_send, near_receive = refs[2 * count + 2 :]
        ctx, wt = lax.axis_index("ctx"), lax.axis_index("wt")
        low = lax.rem(ctx, 2)
        near, far, beside = (ctx, wt ^ 1), (ctx, wt ^ 2), (ctx ^ 1, wt)
        goes, comes = wt ^ (2 + low), wt ^ (3 - low)
        greet((near, far, beside, (ctx ^ 1, goes), (ctx ^ 1, comes)))

        def move(item, step, source, slot, peer):
            return pltpu.make_async_remote_copy(
                source, targets[item].at[slot], send.at[item, step], receive.at[item, step],
                device_id=peer, device_id_type=MESH,
            )

        def cross(index):
            span = pl.ds(index * extent, extent)
            return pltpu.make_async_remote_copy(
                blocks.at[goes, span], filled.at[wt, span], cross_send.at[0, index], cross_receive.at[0, index],
                device_id=(ctx ^ 1, goes), device_id_type=MESH,
            )

        def crossed(index):
            span = pl.ds(index * extent, extent)
            return pltpu.make_async_remote_copy(
                filled.at[comes, span], filled.at[comes, span], cross_send.at[0, index], cross_receive.at[0, index],
                device_id=(ctx ^ 1, goes), device_id_type=MESH,
            )

        def onward(index):
            span = pl.ds(index * extent, extent)
            return pltpu.make_async_remote_copy(
                filled.at[comes, span], filled.at[comes, span], cross_send.at[1, index], cross_receive.at[1, index],
                device_id=beside, device_id_type=MESH,
            )

        firsts = [move(item, 0, sources[item], wt, far) for item in range(count)]
        for copy in firsts:
            copy.start()
        crossings = [cross(index) for index in range(pieces)]
        for copy in crossings:
            copy.start()
        seconds = [move(item, 1, sources[item], wt, near) for item in range(count)]
        own = [
            pltpu.make_async_copy(sources[item], targets[item].at[wt], local.at[item])
            for item in range(count)
        ]
        own.append(pltpu.make_async_copy(blocks.at[wt], filled.at[wt], local.at[count]))
        pair = pltpu.make_async_remote_copy(
            blocks.at[wt ^ 1], filled.at[wt], near_send, near_receive, device_id=near, device_id_type=MESH
        )
        for copy in seconds + own + [pair]:
            copy.start()
        thirds = []
        for item in range(count):
            firsts[item].wait_recv()
            copy = move(item, 2, targets[item].at[wt ^ 2], wt ^ 2, near)
            copy.start()
            thirds.append(copy)
        onwards = []
        for index in range(pieces):
            crossed(index).wait_recv()
            copy = onward(index)
            copy.start()
            onwards.append(copy)
        for copy in firsts + crossings:
            copy.wait_send()
        for copy in seconds + thirds + own + [pair] + onwards:
            copy.wait()

    hbm = pl.BlockSpec(memory_space=pl.ANY)
    return pl.pallas_call(
        kernel,
        out_shape=tuple(jax.ShapeDtypeStruct((4,) + member.shape, member.dtype) for member in arrays)
        + (jax.ShapeDtypeStruct(columns.shape, columns.dtype),),
        in_specs=[hbm] * (count + 1),
        out_specs=(hbm,) * (count + 1),
        scratch_shapes=[
            pltpu.SemaphoreType.DMA((count, 3)),
            pltpu.SemaphoreType.DMA((count, 3)),
            pltpu.SemaphoreType.DMA((count + 1,)),
            pltpu.SemaphoreType.DMA((2, pieces)),
            pltpu.SemaphoreType.DMA((2, pieces)),
            pltpu.SemaphoreType.DMA,
            pltpu.SemaphoreType.DMA,
        ],
        compiler_params=pltpu.CompilerParams(collective_id=collective, has_side_effects=True),
        name="prologue",
    )(*arrays, columns)


def scatter_wt(parts, collective):
    count = len(parts)
    extents = [member.shape[1:] for member in parts]

    def kernel(*refs):
        terms, sums = refs[:count], refs[count : 2 * count]
        bufs = refs[2 * count : 3 * count]
        send, receive = refs[3 * count :]
        ctx, wt = lax.axis_index("ctx"), lax.axis_index("wt")
        near, far = (ctx, wt ^ 1), (ctx, wt ^ 2)
        greet((near, far))

        def move(item, step, source, target, peer):
            return pltpu.make_async_remote_copy(
                bufs[item].at[source], bufs[item].at[target], send.at[item, step], receive.at[item, step],
                device_id=peer, device_id_type=MESH,
            )

        waits = []
        for item in range(count):
            bufs[item][0] = terms[item][wt ^ 3].astype(jnp.bfloat16)
            copy = move(item, 0, 0, 3, near)
            copy.start()
            waits.append(copy)
        rests = []
        for item in range(count):
            bufs[item][1] = terms[item][wt ^ 1].astype(jnp.bfloat16)
            copy = move(item, 1, 1, 4, near)
            copy.start()
            rests.append(copy)
        lasts = []
        for item in range(count):
            waits[item].wait_recv()
            bufs[item][2] = (terms[item][wt ^ 2] + bufs[item][3].astype(jnp.float32)).astype(jnp.bfloat16)
            copy = move(item, 2, 2, 5, far)
            copy.start()
            lasts.append(copy)
        for item in range(count):
            rests[item].wait_recv()
            sums[item][...] = terms[item][wt] + bufs[item][4].astype(jnp.float32)
        for item in range(count):
            lasts[item].wait_recv()
            sums[item][...] += bufs[item][5].astype(jnp.float32)
        for copy in waits + rests + lasts:
            copy.wait_send()

    vmem = pl.BlockSpec(memory_space=pltpu.VMEM)
    return pl.pallas_call(
        kernel,
        out_shape=tuple(jax.ShapeDtypeStruct(extent, jnp.float32) for extent in extents),
        in_specs=[vmem] * count,
        out_specs=(vmem,) * count,
        scratch_shapes=[pltpu.VMEM((6,) + extent, jnp.bfloat16) for extent in extents]
        + [pltpu.SemaphoreType.DMA((count, 3)), pltpu.SemaphoreType.DMA((count, 3))],
        compiler_params=pltpu.CompilerParams(
            collective_id=collective, has_side_effects=True, vmem_limit_bytes=40 * 2**20
        ),
        name="scatter_wt",
    )(*parts)


def exchange(blocks, axis, collective):
    count = blocks.shape[0]

    def kernel(source, target, send, receive, local):
        ctx, wt = lax.axis_index("ctx"), lax.axis_index("wt")
        own = ctx if axis == "ctx" else wt

        def peer(step):
            other = lax.rem(own + step, count)
            return other, ((other, wt) if axis == "ctx" else (ctx, other))

        barrier = pltpu.get_barrier_semaphore()

        def signal(step, carry):
            pl.semaphore_signal(barrier, inc=1, device_id=peer(step)[1], device_id_type=MESH)
            return carry

        lax.fori_loop(1, count, signal, 0)
        pl.semaphore_wait(barrier, count - 1)

        def move(step):
            other, device = peer(step)
            return pltpu.make_async_remote_copy(
                source.at[other], target.at[own], send.at[step], receive.at[step],
                device_id=device, device_id_type=MESH,
            )

        def begin(step, carry):
            move(step).start()
            return carry

        def finish(step, carry):
            move(step).wait()
            return carry

        lax.fori_loop(1, count, begin, 0)
        keep = pltpu.make_async_copy(source.at[own], target.at[own], local)
        keep.start()
        keep.wait()
        lax.fori_loop(1, count, finish, 0)

    hbm = pl.BlockSpec(memory_space=pl.ANY)
    return pl.pallas_call(
        kernel,
        out_shape=jax.ShapeDtypeStruct(blocks.shape, blocks.dtype),
        in_specs=[hbm],
        out_specs=hbm,
        scratch_shapes=[
            pltpu.SemaphoreType.DMA((count,)),
            pltpu.SemaphoreType.DMA((count,)),
            pltpu.SemaphoreType.DMA,
        ],
        compiler_params=pltpu.CompilerParams(collective_id=collective, has_side_effects=True),
        name="exchange_" + axis,
    )(blocks)


def swap_wt(pieces):
    wt = lax.axis_index("wt")
    stacked = jnp.stack(pieces)
    result = jnp.zeros_like(stacked)
    for step in range(4):
        piece = lax.dynamic_index_in_dim(stacked, wt ^ step, 0, keepdims=False)
        if step:
            piece = lax.ppermute(piece, "wt", [(source, source ^ step) for source in range(4)])
        result = lax.dynamic_update_index_in_dim(result, piece, wt ^ step, 0)
    return result


def ring_shift(value, axis, step):
    pairs = []
    for source in range(32):
        place = [source // 8, source // 2 % 4, source % 2]
        place[axis] = (place[axis] + step) % (4, 4, 2)[axis]
        pairs.append((source, place[0] * 8 + place[1] * 2 + place[2]))
    return lax.ppermute(value, "ctx", pairs)


def spot(axis):
    ctx = lax.axis_index("ctx")
    return (ctx // 8, ctx // 2 % 4, ctx % 2)[axis]


def pieces_along(value, axis):
    own = spot(axis)
    rows = value.shape[0] // 4
    cut = lambda step: lax.dynamic_slice_in_dim(value, (own + step) % 4 * rows, rows, 0)
    return [cut(0)] + [ring_shift(cut(step), axis, step) for step in (1, 3, 2)]


def added(pieces):
    total = pieces[0].astype(jnp.float32)
    for piece in pieces[1:]:
        total = total + piece.astype(jnp.float32)
    return total.astype(pieces[0].dtype)


def passed_along(value, axis):
    return [value] + [ring_shift(value, axis, step) for step in (1, 3, 2)]


def outer_start(place):
    return pl.multiple_of(16 * (13 * place - 1 + (4 - place) // 4), 16)


def reduce_spread(first, second, outer, collective, micros):
    features = first.shape[1]
    share = features // 4
    size, inner, stride = (208, 64, 48) if outer else (400, 112, 96)
    low = jnp.bfloat16

    def kernel(first_ref, second_ref, first_out, second_out, *scratch):
        window, outer_in, inner_in, mid, pair_in, lanes_out, lanes_in, inner_all, outer_send, outer_receive, inner_send, inner_receive, pair_send, pair_receive, lane_send, lane_receive, all_send, all_receive, spread_send, spread_receive = scratch
        ctx, wt = lax.axis_index("ctx"), lax.axis_index("wt")
        y, z, low_x = ctx // 8, ctx // 2 % 4, ctx % 2
        at_y = lambda place: (place * 8 + z * 2 + low_x, wt)
        at_z = lambda place: (y * 8 + place * 2 + low_x, wt)
        beside = (ctx ^ 1, wt)
        halves = [(y, at_y, z, at_z, first_ref, first_out), (z, at_z, y, at_y, second_ref, second_out)]
        peers = [at_y((y + step) % 4) for step in (1, 2, 3)] + [at_z((z + step) % 4) for step in (1, 2, 3)]
        peers += [beside] + [(ctx, wt ^ step) for step in (1, 2, 3)]
        greet(peers)
        inner_at = lambda place: pl.ds(pl.multiple_of(stride * place, 16), inner)

        def remote(source, target, sends, receives, device):
            return pltpu.make_async_remote_copy(
                source, target, sends, receives, device_id=device, device_id_type=MESH
            )

        started = []
        if outer:
            copies = [[], []]
            for step in (1, 3, 2):
                for half, (place, at, _, _, source, _) in enumerate(halves):
                    other = (place + step) % 4
                    copy = remote(
                        source.at[pl.ds(outer_start(other), size)], outer_in.at[half, step - 1],
                        outer_send.at[half, step - 1], outer_receive.at[half, step - 1], at(other),
                    )
                    copy.start()
                    copies[half].append(copy)
            for half, (place, _, _, _, source, _) in enumerate(halves):
                for copy in copies[half]:
                    copy.wait_recv()
                total = source[pl.ds(outer_start(place), size)].astype(jnp.float32)
                for step in range(3):
                    total += outer_in[half, step].astype(jnp.float32)
                window[half] = total.astype(low)
            started += copies[0] + copies[1]
        else:
            for half in range(2):
                window[half] = halves[half][4][...]
        copies = [[], []]
        for half, (_, _, place, at, _, _) in enumerate(halves):
            for step in (1, 3, 2):
                other = (place + step) % 4
                copy = remote(
                    window.at[half, inner_at(other)], inner_in.at[half, step - 1],
                    inner_send.at[half, step - 1], inner_receive.at[half, step - 1], at(other),
                )
                copy.start()
                copies[half].append(copy)
        pairs = []
        for half, (_, _, place, _, _, _) in enumerate(halves):
            for copy in copies[half]:
                copy.wait_recv()
            total = window[half, inner_at(place)].astype(jnp.float32)
            for step in range(3):
                total += inner_in[half, step].astype(jnp.float32)
            mid[half] = total.astype(low)
            copy = remote(mid.at[half], pair_in.at[half], pair_send.at[half], pair_receive.at[half], beside)
            copy.start()
            pairs.append(copy)
        started += copies[0] + copies[1] + pairs

        def to_owners(half):
            total = (mid[half].astype(jnp.float32) + pair_in[half].astype(jnp.float32)).astype(low)
            pair_in[half] = total
            moves = []
            for owner in range(4):
                lanes_out[half, owner] = total[:, owner * share : (owner + 1) * share]
            for step in (2, 3, 1):
                copy = remote(
                    lanes_out.at[half, wt ^ step], lanes_in.at[half, wt],
                    lane_send.at[half, step - 1], lane_receive.at[half, step - 1], (ctx, wt ^ step),
                )
                copy.start()
                moves.append(copy)
            lanes_in[half, wt] = lanes_out[half, wt]
            return moves

        def from_owners(half, moves, keep):
            for copy in moves:
                copy.wait_recv()
            for sender in range(4):
                part = lanes_in[half, sender]
                if keep is not None:
                    part = jnp.where(keep, pair_in[half, :, sender * share : (sender + 1) * share], part)
                pair_in[half, :, sender * share : (sender + 1) * share] = part

        def spread_inner(half):
            _, _, place, at, _, _ = halves[half]
            moves = []
            for step in (1, 3, 2):
                copy = remote(
                    pair_in.at[half], inner_all.at[half, place],
                    all_send.at[half, step - 1], all_receive.at[half, step - 1], at((place + step) % 4),
                )
                copy.start()
                moves.append(copy)
            inner_all[half, place] = pair_in[half]
            return moves

        def fill(half, moves):
            for copy in moves:
                copy.wait_recv()
            for place in range(4):
                window[half, stride * place : stride * place + inner] = inner_all[half, place]

        pairs[0].wait_recv()
        lane_moves = to_owners(0)
        pairs[1].wait_recv()
        if outer:
            second_lanes = to_owners(1)
        else:
            pair_in[1] = (mid[1].astype(jnp.float32) + pair_in[1].astype(jnp.float32)).astype(low)
            second_lanes = []
            second_moves = spread_inner(1)
        from_owners(0, lane_moves, None)
        first_moves = spread_inner(0)
        if outer:
            from_owners(1, second_lanes, z >= 2)
            second_moves = spread_inner(1)
        for copy in started:
            copy.wait_send()
        spreads = []
        for half, moves in ((0, first_moves), (1, second_moves)):
            fill(half, moves)
            place, at, _, _, _, target = halves[half]
            if outer:
                for step in (1, 3, 2):
                    copy = remote(
                        window.at[half], target.at[place],
                        spread_send.at[half, step - 1], spread_receive.at[half, step - 1], at((place + step) % 4),
                    )
                    copy.start()
                    spreads.append(copy)
                target[place] = window[half]
            else:
                target[...] = window[half]
        for copy in lane_moves + second_lanes + first_moves + second_moves:
            copy.wait_send()
        for copy in spreads:
            copy.wait()

    vmem = pl.BlockSpec(memory_space=pltpu.VMEM)
    result = jax.ShapeDtypeStruct((4, size, features) if outer else (size, features), low)
    pairs_of = lambda: [pltpu.SemaphoreType.DMA((2, 3)), pltpu.SemaphoreType.DMA((2, 3))]
    return pl.pallas_call(
        kernel,
        out_shape=(result, result),
        in_specs=[vmem] * 2,
        out_specs=(vmem,) * 2,
        scratch_shapes=[
            pltpu.VMEM((2, size, features), low),
            pltpu.VMEM((2, 3, size if outer else 16, features), low),
            pltpu.VMEM((2, 3, inner, features), low),
            pltpu.VMEM((2, inner, features), low),
            pltpu.VMEM((2, inner, features), low),
            pltpu.VMEM((2, 4, inner, share), low),
            pltpu.VMEM((2, 4, inner, share), low),
            pltpu.VMEM((2, 4, inner, features), low),
        ]
        + pairs_of()
        + pairs_of()
        + [pltpu.SemaphoreType.DMA((2,)), pltpu.SemaphoreType.DMA((2,))]
        + pairs_of()
        + pairs_of()
        + pairs_of(),
        compiler_params=pltpu.CompilerParams(
            collective_id=collective, has_side_effects=True, vmem_limit_bytes=48 * 2**20
        ),
        cost_estimate=cost(micros),
        name="reduce_spread",
    )(first, second)


def turn_rows(pieces, place, width):
    rows, features = pieces[0].shape
    share = features // 4

    def kernel(place_ref, *refs):
        out, held = refs[4:]
        for step, piece in zip((0, 1, 3, 2), refs[:4]):
            held[lax.rem(place_ref[0] + 4 - step, 4)] = piece[...]
        for block in range(4):
            for sender in range(4):
                part = held[block, :, sender * share : (sender + 1) * share].astype(jnp.float32).T
                start = sender * width + block * rows
                out[:, start : start + rows] = part

    vmem = pl.BlockSpec(memory_space=pltpu.VMEM)
    return pl.pallas_call(
        kernel,
        out_shape=jax.ShapeDtypeStruct((share, 4 * width), jnp.float32),
        in_specs=[pl.BlockSpec(memory_space=pltpu.SMEM)] + [vmem] * 4,
        out_specs=vmem,
        scratch_shapes=[pltpu.VMEM((4, rows, features), pieces[0].dtype)],
        compiler_params=pltpu.CompilerParams(vmem_limit_bytes=48 * 2**20),
        cost_estimate=cost(9),
        name="turn_rows",
    )(place.reshape(1), *pieces)


def place_rows(pieces, place):
    rows, features = pieces[0].shape

    def kernel(place_ref, *refs):
        out = refs[4]
        for step, piece in zip((0, 1, 3, 2), refs[:4]):
            start = pl.multiple_of(lax.rem(place_ref[0] + 4 - step, 4) * rows, 16)
            out[pl.ds(start, rows), :] = piece[...].astype(jnp.float32)

    vmem = pl.BlockSpec(memory_space=pltpu.VMEM)
    return pl.pallas_call(
        kernel,
        out_shape=jax.ShapeDtypeStruct((4 * rows, features), jnp.float32),
        in_specs=[pl.BlockSpec(memory_space=pltpu.SMEM)] + [vmem] * 4,
        out_specs=vmem,
        compiler_params=pltpu.CompilerParams(vmem_limit_bytes=48 * 2**20),
        cost_estimate=cost(6),
        name="place_rows",
    )(place.reshape(1), *pieces)


def turn_windows(first, second):
    size, features = first.shape[1:]
    share = features // 4
    cut = 2 * size - share

    def kernel(first_ref, second_ref, qkv_ref, out_ref):
        def lay(source, block, skip, start):
            rows = size - skip
            for sender in range(4):
                part = source[block, skip:, sender * share : (sender + 1) * share].astype(jnp.float32).T
                at = start + sender * share
                qkv_ref[:, at : at + rows] = part

        lay(first_ref, 0, 0, 0)
        lay(first_ref, 1, cut, size)
        lay(first_ref, 2, cut, features)
        lay(first_ref, 3, 0, features + size - cut)
        lay(second_ref, 0, 0, 2 * features)
        lay(second_ref, 1, cut, 2 * features + size)
        out_ref[: size - cut] = second_ref[2, cut:].astype(jnp.float32)
        out_ref[size - cut :] = second_ref[3].astype(jnp.float32)

    vmem = pl.BlockSpec(memory_space=pltpu.VMEM)
    return pl.pallas_call(
        kernel,
        out_shape=(
            jax.ShapeDtypeStruct((share, 3 * features), jnp.float32),
            jax.ShapeDtypeStruct((share, features), jnp.float32),
        ),
        in_specs=[vmem] * 2,
        out_specs=(vmem,) * 2,
        compiler_params=pltpu.CompilerParams(vmem_limit_bytes=48 * 2**20),
        cost_estimate=cost(9),
        name="turn_windows",
    )(first, second)


def to_heads(rows_by_token):
    parts = rows_by_token.shape[0] // SPAN
    rows = rows_by_token.shape[1] // 4
    blocks = rows_by_token.reshape(parts, GROUP, HEAD_DIM, 4, rows).transpose(3, 1, 0, 2, 4)
    blocks = blocks.reshape(4 * GROUP, parts * HEAD_DIM, rows)
    spare = lax.axis_size("ctx") - 4 * GROUP
    return jnp.concatenate([blocks, jnp.zeros((spare,) + blocks.shape[1:], blocks.dtype)])


def from_heads(blocks):
    parts, rows = blocks.shape[1] // HEAD_DIM, blocks.shape[2]
    used = blocks[: 4 * GROUP].reshape(4, GROUP, parts, HEAD_DIM, rows)
    return used.transpose(2, 1, 3, 0, 4).reshape(parts * SPAN, 4 * rows)


def local(
    inputs,
    block_order,
    cotangent,
    ln1_gain,
    ln1_bias,
    w_qkv,
    bias_q,
    bias_v,
    w_out,
    bias_out,
    ln2_gain,
    ln2_bias,
    w_fc,
    bias_fc,
    w_proj,
    bias_proj,
):
    ctx, wt = lax.axis_index("ctx"), lax.axis_index("wt")
    ctx_count = lax.axis_size("ctx")
    rows, features = inputs.shape[1:]
    share = features // 4
    ff = w_fc.shape[1] // 4
    shift = 16 * wt

    small = jnp.stack([ln1_gain, ln1_bias, bias_q, bias_v, bias_out, ln2_gain, ln2_bias, bias_proj])
    small = jnp.pad(small, ((0, 8), (0, 0)))
    order = jnp.pad(block_order, ((0, 7), (0, 128 - ctx_count)))
    starts = [384 * member for member in range(4)]
    columns = jnp.stack(
        [
            jnp.concatenate(
                [w_qkv[:, part * features + start : part * features + start + SPAN] for part in range(3)],
                axis=1,
            )
            for start in starts
        ]
    )
    all_inputs, all_small, all_order, own_qkv = prologue((inputs[0], small, order), columns, 1)
    own_qkv = own_qkv.reshape(features, 3 * SPAN)
    vectors = all_small[:, :8].transpose(1, 0, 2).reshape(8, features).astype(jnp.float32)
    gain_one, shift_one, full_bq, full_bv, full_bout, gain_two, shift_two, full_bproj = vectors
    orders = all_order[:, 0, :ctx_count]
    place = lax.dynamic_index_in_dim(orders, jnp.minimum(ctx // GROUP, 3), 0, keepdims=False)
    slots = jnp.arange(ctx_count, dtype=jnp.int32)
    inverse = jnp.sum(jnp.where(place[None, :] == slots[:, None], slots[None, :], 0), axis=1)
    later_fc, later_out, later_cot, own_qkv = lax.optimization_barrier((w_fc, w_out, cotangent[0], own_qkv))
    own_fc = swap_wt([later_fc[:, rows_ff * ff : (rows_ff + 1) * ff] for rows_ff in range(4)]).reshape(features, ff)
    group_cot = swap_wt([later_cot] * 4).reshape(4 * rows, features)
    edge = SPAN - share
    below = lax.ppermute(later_out[share - edge :], "wt", [(source, (source + 1) % 4) for source in range(4)])
    above = lax.ppermute(later_out[:edge], "wt", [(source, (source - 1) % 4) for source in range(4)])
    wide_out = lax.dynamic_slice_in_dim(jnp.concatenate([below, later_out, above]), edge - shift, SPAN, 0)
    span_ids = jnp.arange(SPAN, dtype=jnp.int32)
    mine = (span_ids >= shift) & (span_ids < shift + share)
    masked_out = jnp.where(mine[:, None], wide_out, 0)

    group_tokens = all_inputs.reshape(4 * rows, features).astype(jnp.float32)
    normed_one = layer_norm(group_tokens, gain_one, shift_one).astype(jnp.bfloat16)
    bias_cols = jnp.concatenate(
        [
            lax.dynamic_slice_in_dim(full_bq, 384 * wt, SPAN),
            jnp.zeros((SPAN,), jnp.float32),
            lax.dynamic_slice_in_dim(full_bv, 384 * wt, SPAN),
        ]
    )
    projected = (dot(own_qkv, normed_one, 0, 1) + bias_cols[:, None]).astype(jnp.bfloat16)
    received = exchange(to_heads(projected), "ctx", 3)
    block = math.gcd(512, ctx_count * rows)
    attended_blocks, *saved = attend_forward(received, inverse, place, block)
    attended = from_heads(exchange(attended_blocks, "ctx", 4))

    tokens = inputs[0].astype(jnp.float32)
    (branch,) = scatter_wt((dot(attended, masked_out, 0, 0).reshape(4, rows, features),), 5)
    middle = tokens + branch + full_bout
    normed_two = layer_norm(middle, gain_two, shift_two).astype(jnp.bfloat16)
    (all_two,) = gather_wt((normed_two,), 6)
    all_two = all_two.reshape(4 * rows, features)
    hidden_pre = dot(all_two, own_fc) + bias_fc.astype(jnp.float32)
    hidden_low = gelu_tanh(hidden_pre).astype(jnp.bfloat16)
    hidden_grad = dot(group_cot, w_proj, 1, 1)
    unused_gelu, gelu_back = jax.vjp(gelu_tanh, hidden_pre)
    pre_grad = gelu_back(hidden_grad)[0].astype(jnp.bfloat16)
    low = jnp.bfloat16
    grad_fc = dot(pre_grad, all_two, 0, 0).astype(low)
    grad_proj = dot(hidden_low, group_cot, 0, 0).astype(low)
    terms_two = (
        dot(hidden_low, w_proj).reshape(4, rows, features),
        dot(pre_grad, own_fc, 1, 1).reshape(4, rows, features),
    )
    terms_two, grad_fc, grad_proj = lax.optimization_barrier((terms_two, grad_fc, grad_proj))
    window_fc = added(pieces_along(grad_fc, 0))
    window_proj = added(pieces_along(grad_proj, 1))
    projected_out, normed_two_grad = scatter_wt(terms_two, 7)
    outputs = middle + projected_out + full_bproj
    unused_norm, norm_back = jax.vjp(layer_norm, middle, gain_two, shift_two)
    middle_part, grad_gain_two, grad_shift_two = norm_back(normed_two_grad)
    middle_grad = cotangent[0].astype(jnp.float32) + middle_part
    branch_grad = middle_grad.astype(jnp.bfloat16)
    (all_branch,) = gather_wt((branch_grad,), 8)
    all_branch = all_branch.reshape(4 * rows, features)

    attended_grad = dot(wide_out, all_branch, 1, 1).astype(jnp.bfloat16)
    upstream = exchange(to_heads(attended_grad), "ctx", 9)
    upstream, window_fc, window_proj = lax.optimization_barrier((upstream, window_fc, window_proj))
    window_fc, window_proj = reduce_spread(window_fc, window_proj, False, 12, 30)
    upstream, window_fc, window_proj = lax.optimization_barrier((upstream, window_fc, window_proj))
    all_fc, all_proj = passed_along(window_fc, 0), passed_along(window_proj, 1)
    grad_blocks = attend_backward(upstream, inverse, place, saved, block)
    stacked = from_heads(exchange(grad_blocks, "ctx", 10))
    masked = jnp.where(jnp.tile(mine, 3)[:, None], stacked, 0)
    (normed_one_grad,) = scatter_wt((dot(masked, own_qkv, 0, 1).reshape(4, rows, features),), 11)
    unused_first, first_back = jax.vjp(layer_norm, tokens, gain_one, shift_one)
    input_part, grad_gain_one, grad_shift_one = first_back(normed_one_grad)
    input_grad = middle_grad + input_part

    own_stacked = lax.dynamic_slice_in_dim(stacked.reshape(3, SPAN, -1), shift, share, 1)
    own_attended = lax.dynamic_slice_in_dim(attended, shift, share, 0)
    grad_qkv = dot(own_stacked.reshape(3 * share, -1), normed_one).astype(low)
    grad_out = dot(own_attended, all_branch).astype(low)
    column = lambda value: lax.dynamic_slice_in_dim(value, share * wt, share, 0)
    sums = jnp.sum(own_stacked.astype(jnp.float32), axis=2)
    grad_bout = column(jnp.sum(all_branch.astype(jnp.float32), axis=0))
    grad_bproj = column(jnp.sum(group_cot.astype(jnp.float32), axis=0))
    grad_bfc = jnp.sum(pre_grad.astype(jnp.float32), axis=0)
    crossed_vectors = jnp.stack([grad_gain_one, grad_shift_one, grad_gain_two, grad_shift_two]).astype(low)
    kept_vectors = jnp.stack([jnp.concatenate([sums[0], sums[2], grad_bout, grad_bproj]), grad_bfc]).astype(low)
    tail = lambda value: jnp.pad(value, ((0, 16 - value.shape[0]), (0, 0)))
    first = jnp.concatenate([grad_qkv[:share], tail(crossed_vectors), grad_qkv[share : 2 * share]])
    second = jnp.concatenate([grad_qkv[2 * share :], tail(kept_vectors), grad_out])
    first, second = reduce_spread(first, second, True, 13, 110)
    sum_fc = turn_rows(all_fc, spot(0), ff)
    sum_proj = place_rows(all_proj, spot(1))
    sum_qkv, sum_out = turn_windows(first, second)
    norms = jnp.sum(first[2, :4].reshape(4, 4, share).astype(jnp.float32), axis=1)
    kept_sums = second[2, :2].astype(jnp.float32)
    sum_bq, sum_bv, sum_bout, sum_bproj = kept_sums[0].reshape(4, share)
    return (
        outputs.astype(jnp.bfloat16)[None],
        input_grad[None],
        norms[0],
        norms[1],
        sum_qkv,
        sum_bq,
        sum_bv,
        sum_out,
        sum_bout,
        norms[2],
        norms[3],
        sum_fc,
        kept_sums[1],
        sum_proj,
        sum_bproj,
    )


def solution(mesh):
    placed = (
        P("wt", "ctx", None),
        P("wt", None),
        P("wt", "ctx", None),
        P("wt"),
        P("wt"),
        P("wt", None),
        P("wt"),
        P("wt"),
        P("wt", None),
        P("wt"),
        P("wt"),
        P("wt"),
        P("wt", None),
        P("wt"),
        P("wt", None),
        P("wt"),
    )
    return jax.shard_map(
        local,
        mesh=mesh,
        in_specs=placed,
        out_specs=(
            P("wt", "ctx", None),
            P("wt", "ctx", None),
            P("wt"),
            P("wt"),
            P("wt", None),
            P("wt"),
            P("wt"),
            P("wt", None),
            P("wt"),
            P("wt"),
            P("wt"),
            P("wt", None),
            P("wt"),
            P("wt", None),
            P("wt"),
        ),
        check_vma=False,
    )
```

```python
import math

import jax
import jax.numpy as jnp
from jax import lax
from jax.experimental import pallas as pl
from jax.experimental.pallas import tpu as pltpu
from jax.sharding import PartitionSpec as P

HEADS = 25
HEAD_DIM = 64
GROUP = 7
SPAN = GROUP * HEAD_DIM
EPS = 1e-05
MESH = pl.DeviceIdType.MESH


def cost(micros):
    return pl.CostEstimate(flops=int(micros * 1e9), bytes_accessed=int(micros * 1e6), transcendentals=0)
NEG = -1e30
LOG2E = 1.4426950408889634

def layer_norm(values, gain_row, shift_row):
    centered = values - jnp.mean(values, axis=-1, keepdims=True)
    variance = jnp.mean(centered * centered, axis=-1, keepdims=True)
    return centered * lax.rsqrt(variance + EPS) * gain_row + shift_row


def gelu_tanh(values):
    return jax.nn.gelu(values, approximate=True)


def dot(left, right, left_dim=1, right_dim=0):
    return lax.dot_general(
        left, right, (((left_dim,), (right_dim,)), ((), ())), preferred_element_type=jnp.float32
    )


def greet(peers):
    barrier = pltpu.get_barrier_semaphore()
    for peer in peers:
        pl.semaphore_signal(barrier, inc=1, device_id=peer, device_id_type=MESH)
    pl.semaphore_wait(barrier, len(peers))


def prologue(arrays, columns, collective):
    count = len(arrays)
    pieces = 5
    extent = columns.shape[1] // pieces

    def kernel(*refs):
        sources, (blocks,) = refs[:count], refs[count : count + 1]
        targets, (filled,) = refs[count + 1 : 2 * count + 1], refs[2 * count + 1 : 2 * count + 2]
        send, receive, local, cross_send, cross_receive, near_send, near_receive = refs[2 * count + 2 :]
        ctx, wt = lax.axis_index("ctx"), lax.axis_index("wt")
        low = lax.rem(ctx, 2)
        near, far, beside = (ctx, wt ^ 1), (ctx, wt ^ 2), (ctx ^ 1, wt)
        goes, comes = wt ^ (2 + low), wt ^ (3 - low)
        greet((near, far, beside, (ctx ^ 1, goes), (ctx ^ 1, comes)))

        def move(item, step, source, slot, peer):
            return pltpu.make_async_remote_copy(
                source, targets[item].at[slot], send.at[item, step], receive.at[item, step],
                device_id=peer, device_id_type=MESH,
            )

        def cross(index):
            span = pl.ds(index * extent, extent)
            return pltpu.make_async_remote_copy(
                blocks.at[goes, span], filled.at[wt, span], cross_send.at[0, index], cross_receive.at[0, index],
                device_id=(ctx ^ 1, goes), device_id_type=MESH,
            )

        def crossed(index):
            span = pl.ds(index * extent, extent)
            return pltpu.make_async_remote_copy(
                filled.at[comes, span], filled.at[comes, span], cross_send.at[0, index], cross_receive.at[0, index],
                device_id=(ctx ^ 1, goes), device_id_type=MESH,
            )

        def onward(index):
            span = pl.ds(index * extent, extent)
            return pltpu.make_async_remote_copy(
                filled.at[comes, span], filled.at[comes, span], cross_send.at[1, index], cross_receive.at[1, index],
                device_id=beside, device_id_type=MESH,
            )

        firsts = [move(item, 0, sources[item], wt, far) for item in range(count)]
        for copy in firsts:
            copy.start()
        crossings = [cross(index) for index in range(pieces)]
        for copy in crossings:
            copy.start()
        seconds = [move(item, 1, sources[item], wt, near) for item in range(count)]
        own = [
            pltpu.make_async_copy(sources[item], targets[item].at[wt], local.at[item])
            for item in range(count)
        ]
        own.append(pltpu.make_async_copy(blocks.at[wt], filled.at[wt], local.at[count]))
        pair = pltpu.make_async_remote_copy(
            blocks.at[wt ^ 1], filled.at[wt], near_send, near_receive, device_id=near, device_id_type=MESH
        )
        for copy in seconds + own + [pair]:
            copy.start()
        thirds = []
        for item in range(count):
            firsts[item].wait_recv()
            copy = move(item, 2, targets[item].at[wt ^ 2], wt ^ 2, near)
            copy.start()
            thirds.append(copy)
        onwards = []
        for index in range(pieces):
            crossed(index).wait_recv()
            copy = onward(index)
            copy.start()
            onwards.append(copy)
        for copy in firsts + crossings:
            copy.wait_send()
        for copy in seconds + thirds + own + [pair] + onwards:
            copy.wait()

    hbm = pl.BlockSpec(memory_space=pl.ANY)
    return pl.pallas_call(
        kernel,
        out_shape=tuple(jax.ShapeDtypeStruct((4,) + member.shape, member.dtype) for member in arrays)
        + (jax.ShapeDtypeStruct(columns.shape, columns.dtype),),
        in_specs=[hbm] * (count + 1),
        out_specs=(hbm,) * (count + 1),
        scratch_shapes=[
            pltpu.SemaphoreType.DMA((count, 3)),
            pltpu.SemaphoreType.DMA((count, 3)),
            pltpu.SemaphoreType.DMA((count + 1,)),
            pltpu.SemaphoreType.DMA((2, pieces)),
            pltpu.SemaphoreType.DMA((2, pieces)),
            pltpu.SemaphoreType.DMA,
            pltpu.SemaphoreType.DMA,
        ],
        compiler_params=pltpu.CompilerParams(collective_id=collective, has_side_effects=True),
        name="prologue",
    )(*arrays, columns)


def exchange(blocks, axis, collective):
    count = blocks.shape[0]

    def kernel(source, target, send, receive, local):
        ctx, wt = lax.axis_index("ctx"), lax.axis_index("wt")
        own = ctx if axis == "ctx" else wt

        def peer(step):
            other = lax.rem(own + step, count)
            return other, ((other, wt) if axis == "ctx" else (ctx, other))

        barrier = pltpu.get_barrier_semaphore()

        def signal(step, carry):
            pl.semaphore_signal(barrier, inc=1, device_id=peer(step)[1], device_id_type=MESH)
            return carry

        lax.fori_loop(1, count, signal, 0)
        pl.semaphore_wait(barrier, count - 1)

        def move(step):
            other, device = peer(step)
            return pltpu.make_async_remote_copy(
                source.at[other], target.at[own], send.at[step], receive.at[step],
                device_id=device, device_id_type=MESH,
            )

        def begin(step, carry):
            move(step).start()
            return carry

        def finish(step, carry):
            move(step).wait()
            return carry

        lax.fori_loop(1, count, begin, 0)
        keep = pltpu.make_async_copy(source.at[own], target.at[own], local)
        keep.start()
        keep.wait()
        lax.fori_loop(1, count, finish, 0)

    hbm = pl.BlockSpec(memory_space=pl.ANY)
    return pl.pallas_call(
        kernel,
        out_shape=jax.ShapeDtypeStruct(blocks.shape, blocks.dtype),
        in_specs=[hbm],
        out_specs=hbm,
        scratch_shapes=[
            pltpu.SemaphoreType.DMA((count,)),
            pltpu.SemaphoreType.DMA((count,)),
            pltpu.SemaphoreType.DMA,
        ],
        compiler_params=pltpu.CompilerParams(collective_id=collective, has_side_effects=True),
        name="exchange_" + axis,
    )(blocks)


def remote(source, target, send, receive, device):
    return pltpu.make_async_remote_copy(source, target, send, receive, device_id=device, device_id_type=MESH)


def greet_ctx(ctx, wt, others):
    barrier = pltpu.get_barrier_semaphore()

    def signal(step, carry):
        pl.semaphore_signal(barrier, inc=1, device_id=((ctx + step) % 32, wt), device_id_type=MESH)
        return carry

    lax.fori_loop(1, 32, signal, 0)
    for other in others:
        pl.semaphore_signal(barrier, inc=1, device_id=other, device_id_type=MESH)
    pl.semaphore_wait(barrier, 31 + len(others))


class RingSum:
    def __init__(self, source, rows, place, at, relay, arrive, send, receive):
        self.source, self.rows, self.place = source, rows, place
        self.relay, self.arrive, self.send, self.receive = relay, arrive, send, receive
        self.up, self.down = (place + 1) % 4, (place + 3) % 4
        self.to = (at(self.up), at(self.down))
        cut = (rows // 32) * 16 + 16
        self.parts = ((0, cut), (cut, rows - cut))

    def block(self, place, part):
        start, extent = self.parts[part]
        return pl.ds(pl.multiple_of(place * self.rows + start, 16), extent)

    def copy(self, index):
        first, second = self.parts
        opposite = (self.place + 2) % 4
        ends = (
            (self.source.at[self.block(opposite, 0)], self.relay.at[0, pl.ds(0, first[1])], 0),
            (self.source.at[self.block(opposite, 1)], self.relay.at[1, pl.ds(0, second[1])], 1),
            (self.source.at[self.block(self.up, 1)], self.arrive.at[0, pl.ds(*second)], 0),
            (self.source.at[self.block(self.down, 0)], self.arrive.at[1, pl.ds(*first)], 1),
            (self.source.at[self.block(self.up, 0)], self.arrive.at[0, pl.ds(*first)], 0),
            (self.source.at[self.block(self.down, 1)], self.arrive.at[1, pl.ds(*second)], 1),
        )
        source, target, way = ends[index]
        return remote(source, target, self.send.at[index], self.receive.at[index], self.to[way])

    def begin(self):
        for index in range(4):
            self.copy(index).start()

    def pass_on(self):
        for way in range(2):
            self.copy(way).wait_recv()
            extent = self.parts[way][1]
            mine = self.block(self.up if way == 0 else self.down, way)
            total = self.source[mine].astype(jnp.float32) + self.relay[way, :extent].astype(jnp.float32)
            self.source[mine] = total.astype(self.source.dtype)
            self.copy(4 + way).start()

    def finish(self):
        for index in (2, 3, 4, 5):
            self.copy(index).wait_recv()
        mine = pl.ds(pl.multiple_of(self.place * self.rows, 16), self.rows)
        total = self.source[mine].astype(jnp.float32)
        return total + self.arrive[0].astype(jnp.float32) + self.arrive[1].astype(jnp.float32)

    def drain(self):
        for index in range(6):
            self.copy(index).wait_send()


class RingSpread:
    def __init__(self, target, place, at, send, receive):
        self.target, self.place, self.send, self.receive = target, place, send, receive
        self.up, self.down = (place + 1) % 4, (place + 3) % 4
        self.to = (at(self.up), at(self.down))
        rows = target.shape[1]
        cut = (rows // 32) * 16 + 16
        self.parts = (pl.ds(0, cut), pl.ds(cut, rows - cut))

    def whole(self, way, slot):
        return remote(self.target.at[slot], self.target.at[slot], self.send.at[way], self.receive.at[way], self.to[way])

    def half(self, way, slot):
        piece = self.target.at[slot, self.parts[way]]
        return remote(piece, piece, self.send.at[2 + way], self.receive.at[2 + way], self.to[way])

    def begin(self):
        self.whole(0, self.place).start()
        self.whole(1, self.place).start()

    def pass_on(self):
        self.whole(0, self.down).wait_recv()
        self.half(0, self.down).start()
        self.whole(1, self.up).wait_recv()
        self.half(1, self.up).start()

    def finish(self):
        opposite = (self.place + 2) % 4
        self.half(0, opposite).wait_recv()
        self.half(1, opposite).wait_recv()

    def drain(self):
        for way in range(2):
            self.whole(way, self.place).wait_send()
            self.half(way, self.down if way == 0 else self.up).wait_send()


class Inner:
    def __init__(self, window, inner, place, at, ctx, wt, crosses, bufs, sems):
        self.window, self.inner, self.place, self.at, self.ctx, self.wt, self.crosses = window, inner, place, at, ctx, wt, crosses
        self.came, self.mid, self.pair, self.lanes_out, self.lanes_in, self.all = bufs
        self.inner_send, self.inner_receive, self.lane_send, self.lane_receive, self.all_send, self.all_receive, self.pair_sems = sems
        self.stride = (window.shape[0] - inner) // 3
        self.share = window.shape[1] // 4

    def rows(self, place):
        return pl.ds(pl.multiple_of(self.stride * place, 16), self.inner)

    def outward(self, step):
        other = (self.place + step) % 4
        return remote(
            self.window.at[self.rows(other)], self.came.at[step - 1],
            self.inner_send.at[step - 1], self.inner_receive.at[step - 1], self.at(other),
        )

    def beside(self):
        return remote(self.mid, self.pair, self.pair_sems.at[0], self.pair_sems.at[1], (self.ctx ^ 1, self.wt))

    def lane(self, step):
        return remote(
            self.lanes_out.at[self.wt ^ step], self.lanes_in.at[self.wt],
            self.lane_send.at[step - 1], self.lane_receive.at[step - 1], (self.ctx, self.wt ^ step),
        )

    def around(self, step):
        return remote(
            self.pair, self.all.at[self.place],
            self.all_send.at[step - 1], self.all_receive.at[step - 1], self.at((self.place + step) % 4),
        )

    def begin(self):
        for step in (1, 3, 2):
            self.outward(step).start()

    def add_inner(self):
        for step in (1, 3, 2):
            self.outward(step).wait_recv()
        total = self.window[self.rows(self.place)].astype(jnp.float32)
        for step in range(3):
            total += self.came[step].astype(jnp.float32)
        self.mid[...] = total.astype(self.mid.dtype)
        self.beside().start()

    def add_beside(self):
        self.beside().wait_recv()
        total = (self.mid[...].astype(jnp.float32) + self.pair[...].astype(jnp.float32)).astype(self.mid.dtype)
        self.pair[...] = total
        if self.crosses is False:
            self.spread()
            return
        for owner in range(4):
            self.lanes_out[owner] = total[:, owner * self.share : (owner + 1) * self.share]
        for step in (2, 3, 1):
            self.lane(step).start()
        self.lanes_in[self.wt] = self.lanes_out[self.wt]

    def spread(self):
        for step in (1, 3, 2):
            self.around(step).start()
        self.all[self.place] = self.pair[...]

    def collect(self):
        if self.crosses is False:
            return
        for step in (1, 2, 3):
            self.lane(step).wait_recv()
        for sender in range(4):
            span = slice(sender * self.share, (sender + 1) * self.share)
            part = self.lanes_in[sender]
            if self.crosses is not True:
                part = jnp.where(self.crosses, part, self.pair[:, span])
            self.pair[:, span] = part
        self.spread()

    def fill(self):
        for step in (1, 2, 3):
            self.outward(step).wait_send()
            self.around(step).wait_recv()
        for place in range(4):
            start = self.stride * place
            self.window[start : start + self.inner] = self.all[place]

    def drain(self):
        self.beside().wait_send()
        for step in (1, 2, 3):
            self.around(step).wait_send()
            if self.crosses is not False:
                self.lane(step).wait_send()


def inner_scratch(inner, features):
    low = jnp.bfloat16
    share = features // 4
    return [
        pltpu.VMEM((2, 3, inner, features), low),
        pltpu.VMEM((2, inner, features), low),
        pltpu.VMEM((2, inner, features), low),
        pltpu.VMEM((2, 4, inner, share), low),
        pltpu.VMEM((2, 4, inner, share), low),
        pltpu.VMEM((2, 4, inner, features), low),
    ] + [pltpu.SemaphoreType.DMA((2, 3))] * 6 + [pltpu.SemaphoreType.DMA((2, 2))]


def inners(windows, inner, y, z, at_y, at_z, ctx, wt, crosses, scratch):
    pick = lambda half: [ref.at[half] for ref in scratch]
    return [
        Inner(windows[0], inner, z, at_z, ctx, wt, crosses[0], pick(0)[:6], pick(0)[6:]),
        Inner(windows[1], inner, y, at_y, ctx, wt, crosses[1], pick(1)[:6], pick(1)[6:]),
    ]


def attend(received, inverse, place, placed_out, tokens, small, pieces, cotangent, collective):
    parts, wide, rows = received.shape
    dim = wide // 3
    features = tokens.shape[1]
    block = math.gcd(512, parts * rows)
    per = block // rows
    count = parts // per
    chunks = 5
    extent = pieces.shape[1] // chunks
    low = jnp.bfloat16
    hold, off = place // per, place % per

    def kernel(
        inverse_ref, hold_ref, off_ref, in_ref, weight_ref, token_ref, small_ref, pieces_ref, cot_ref,
        q_ref, kt_ref, k_ref, v_ref, att_ref, lse_ref, stacked_ref, middle_ref, all_ref, fc_ref, all_cot_ref,
        vt_ref, blocks_ref, came_ref, turned_ref, terms_ref, bufs,
        head_send, head_receive, term_send, term_receive, all_send, all_receive,
        cross_send, cross_receive, cot_send, cot_receive, near_sems, local_sems,
    ):
        ctx, wt = lax.axis_index("ctx"), lax.axis_index("wt")
        low_x = ctx % 2
        near, far, beside = (ctx, wt ^ 1), (ctx, wt ^ 2), (ctx ^ 1, wt)
        goes, comes = wt ^ (2 + low_x), wt ^ (3 - low_x)
        greet_ctx(ctx, wt, (near, far, (ctx ^ 1, goes), (ctx ^ 1, comes)))

        def cross(index, source, slot):
            span = pl.ds(index * extent, extent)
            return remote(
                source.at[slot, span], fc_ref.at[wt, span], cross_send.at[0, index], cross_receive.at[0, index], (ctx ^ 1, goes)
            )

        def onward(index):
            piece = fc_ref.at[comes, pl.ds(index * extent, extent)]
            return remote(piece, piece, cross_send.at[1, index], cross_receive.at[1, index], beside)

        def upstream(step, source, slot, peer):
            return remote(source, all_cot_ref.at[slot], cot_send.at[step], cot_receive.at[step], peer)

        pair = remote(pieces_ref.at[wt ^ 1], fc_ref.at[wt], near_sems.at[0], near_sems.at[1], near)
        own = (
            pltpu.make_async_copy(pieces_ref.at[wt], fc_ref.at[wt], local_sems.at[0]),
            pltpu.make_async_copy(cot_ref, all_cot_ref.at[wt], local_sems.at[1]),
        )
        for index in range(chunks):
            cross(index, pieces_ref, goes).start()
        upstream(0, cot_ref, wt, far).start()
        upstream(1, cot_ref, wt, near).start()
        pair.start()
        for copy in own:
            copy.start()

        def arrange(index, carry):
            for sub in range(per):
                piece = in_ref[inverse_ref[index * per + sub]]
                lanes = pl.ds(sub * rows, rows)
                q_ref[index, :, lanes] = piece[:dim]
                kt_ref[index, :, lanes] = piece[dim : 2 * dim]
                vt_ref[index, :, lanes] = piece[2 * dim :]
                k_ref[index, lanes, :] = piece[dim : 2 * dim].T
                v_ref[index, lanes, :] = piece[2 * dim :].T
            return carry

        lax.fori_loop(0, count, arrange, 0)
        row = lax.broadcasted_iota(jnp.int32, (block, block), 0)
        col = lax.broadcasted_iota(jnp.int32, (block, block), 1)
        factor = LOG2E * dim**-0.5

        def step(qi, kj, carry, diagonal):
            peak, mass, total = carry
            scores = jnp.dot(k_ref[kj], q_ref[qi], preferred_element_type=jnp.float32) * factor
            if diagonal:
                scores = jnp.where(row <= col, scores, NEG)
            new_peak = jnp.maximum(peak, jnp.max(scores, axis=0, keepdims=True))
            weights = jnp.exp2(scores - new_peak)
            shrink = jnp.exp2(peak - new_peak)
            mass = mass * shrink + jnp.sum(weights, axis=0, keepdims=True)
            total = total * shrink + jnp.dot(vt_ref[kj], weights.astype(low), preferred_element_type=jnp.float32)
            return (new_peak, mass, total)

        def query_block(qi, carry):
            start = (
                jnp.full((1, block), NEG, jnp.float32),
                jnp.zeros((1, block), jnp.float32),
                jnp.zeros((dim, block), jnp.float32),
            )
            state = lax.fori_loop(0, qi, lambda kj, cur: step(qi, kj, cur, False), start)
            peak, mass, total = step(qi, qi, state, True)
            att_ref[qi] = total / mass
            lse_ref[qi] = peak + jnp.log2(mass)
            return carry

        lax.fori_loop(0, count, query_block, 0)

        def to_owner(index):
            return remote(blocks_ref.at[index], came_ref.at[ctx], head_send.at[index], head_receive.at[ctx], (index, wt))

        def give_back(index, carry):
            whole = att_ref[hold_ref[index]]
            picked = whole[:, :rows]
            for sub in range(1, per):
                picked = jnp.where(off_ref[index] == sub, whole[:, sub * rows : (sub + 1) * rows], picked)
            blocks_ref[index] = picked.astype(low)

            @pl.when(index != ctx)
            def _():
                to_owner(index).start()

            @pl.when(index == ctx)
            def _():
                came_ref[index] = blocks_ref[index]

            return carry

        @pl.when(ctx < 4 * GROUP)
        def _():
            lax.fori_loop(0, parts, give_back, 0)

        for index in range(chunks):
            cross(index, pieces_ref, goes).wait_recv()
            onward(index).start()
        upstream(0, cot_ref, wt ^ 2, far).wait_recv()
        upstream(2, all_cot_ref.at[wt ^ 2], wt ^ 2, near).start()

        def owner_here(source, carry):
            @pl.when(source != ctx)
            def _():
                remote(
                    blocks_ref.at[0], came_ref.at[source], head_send.at[0], head_receive.at[source], (source, wt)
                ).wait_recv()

            return carry

        lax.fori_loop(0, 4 * GROUP, owner_here, 0)

        def make_terms(sequence):
            for head in range(GROUP):
                turned_ref[head * dim : (head + 1) * dim] = came_ref[sequence * GROUP + head]
            stacked_ref[sequence] = turned_ref[...].T
            terms_ref[...] = jnp.dot(stacked_ref[sequence], weight_ref[...], preferred_element_type=jnp.float32)

        def term(index, source, target, peer):
            return remote(bufs.at[source], bufs.at[target], term_send.at[index], term_receive.at[index], peer)

        make_terms(wt ^ 3)
        bufs[0] = terms_ref[...].astype(low)
        term(0, 0, 3, near).start()
        make_terms(wt ^ 1)
        bufs[1] = terms_ref[...].astype(low)
        term(1, 1, 4, near).start()
        make_terms(wt ^ 2)
        term(0, 0, 3, near).wait_recv()
        bufs[2] = (terms_ref[...] + bufs[3].astype(jnp.float32)).astype(low)
        term(2, 2, 5, far).start()
        make_terms(wt)
        middle_ref[...] = token_ref[...].astype(jnp.float32) + terms_ref[...] + small_ref[0:1]
        term(1, 1, 4, near).wait_recv()
        middle_ref[...] += bufs[4].astype(jnp.float32)
        term(2, 2, 5, far).wait_recv()
        middle_ref[...] += bufs[5].astype(jnp.float32)
        all_ref[wt] = layer_norm(middle_ref[...], small_ref[1:2], small_ref[2:3]).astype(low)

        def normed(step, slot, peer):
            return remote(all_ref.at[slot], all_ref.at[slot], all_send.at[step], all_receive.at[step], peer)

        normed(0, wt, far).start()
        normed(1, wt, near).start()
        normed(0, wt ^ 2, far).wait_recv()
        normed(2, wt ^ 2, near).start()
        normed(1, wt ^ 1, near).wait_recv()
        normed(2, wt ^ 3, near).wait_recv()
        normed(0, wt, far).wait_send()
        normed(1, wt, near).wait_send()
        normed(2, wt ^ 2, near).wait_send()
        term(0, 0, 3, near).wait_send()
        term(1, 1, 4, near).wait_send()
        term(2, 2, 5, far).wait_send()
        upstream(1, cot_ref, wt ^ 1, near).wait_recv()
        upstream(2, all_cot_ref.at[wt ^ 2], wt ^ 3, near).wait_recv()
        upstream(0, cot_ref, wt, far).wait_send()
        upstream(1, cot_ref, wt, near).wait_send()
        upstream(2, all_cot_ref.at[wt ^ 2], wt ^ 2, near).wait_send()
        pair.wait()
        for copy in own:
            copy.wait()
        for index in range(chunks):
            cross(index, pieces_ref, goes).wait_send()
            onward(index).wait()

        def sent(index, carry):
            @pl.when(index != ctx)
            def _():
                to_owner(index).wait_send()

            return carry

        @pl.when(ctx < 4 * GROUP)
        def _():
            lax.fori_loop(0, parts, sent, 0)

    smem = pl.BlockSpec(memory_space=pltpu.SMEM)
    vmem = pl.BlockSpec(memory_space=pltpu.VMEM)
    hbm = pl.BlockSpec(memory_space=pl.ANY)
    lane_first = jax.ShapeDtypeStruct((count, dim, block), low)
    row_first = jax.ShapeDtypeStruct((count, block, dim), low)
    return pl.pallas_call(
        kernel,
        out_shape=(
            lane_first,
            lane_first,
            row_first,
            row_first,
            jax.ShapeDtypeStruct((count, dim, block), jnp.float32),
            jax.ShapeDtypeStruct((count, 1, block), jnp.float32),
            jax.ShapeDtypeStruct((4, rows, SPAN), low),
            jax.ShapeDtypeStruct((rows, features), jnp.float32),
            jax.ShapeDtypeStruct((4, rows, features), low),
            jax.ShapeDtypeStruct(pieces.shape, low),
            jax.ShapeDtypeStruct((4, rows, features), low),
        ),
        in_specs=[smem] * 3 + [vmem] * 4 + [hbm] * 2,
        out_specs=(vmem,) * 9 + (hbm,) * 2,
        scratch_shapes=[
            pltpu.VMEM((count, dim, block), low),
            pltpu.VMEM((parts, dim, rows), low),
            pltpu.VMEM((parts, dim, rows), low),
            pltpu.VMEM((SPAN, rows), low),
            pltpu.VMEM((rows, features), jnp.float32),
            pltpu.VMEM((6, rows, features), low),
            pltpu.SemaphoreType.DMA((parts,)),
            pltpu.SemaphoreType.DMA((parts,)),
            pltpu.SemaphoreType.DMA((3,)),
            pltpu.SemaphoreType.DMA((3,)),
            pltpu.SemaphoreType.DMA((3,)),
            pltpu.SemaphoreType.DMA((3,)),
            pltpu.SemaphoreType.DMA((2, chunks)),
            pltpu.SemaphoreType.DMA((2, chunks)),
            pltpu.SemaphoreType.DMA((3,)),
            pltpu.SemaphoreType.DMA((3,)),
            pltpu.SemaphoreType.DMA((2,)),
            pltpu.SemaphoreType.DMA((2,)),
        ],
        compiler_params=pltpu.CompilerParams(
            collective_id=collective, has_side_effects=True, vmem_limit_bytes=56 * 2**20
        ),
        name="attend",
    )(inverse, hold, off, received, placed_out, tokens, small, pieces, cotangent)


def feed_back(terms_out, terms_two, grad_fc, grad_proj, middle, gain, cotangent, wide_out, collective):
    rows, features = middle.shape
    block = grad_fc.shape[0] // 4
    low = jnp.bfloat16

    def kernel(
        out_terms, two_terms, fc_ref, proj_ref, middle_ref, gain_ref, cot_ref, wide_ref,
        out_ref, middle_grad_ref, vectors_ref, all_ref, up_ref, fc_out, proj_out,
        fc_work, proj_work, bufs, relay, arrive, blocks_ref,
        ring_send, ring_receive, term_send, term_receive, all_send, all_receive, head_send, head_receive, fetch,
    ):
        ctx, wt = lax.axis_index("ctx"), lax.axis_index("wt")
        y, z, low_x = ctx // 8, ctx // 2 % 4, ctx % 2
        at_y = lambda place: (place * 8 + z * 2 + low_x, wt)
        at_z = lambda place: (y * 8 + place * 2 + low_x, wt)
        near, far = (ctx, wt ^ 1), (ctx, wt ^ 2)
        loads = [
            pltpu.make_async_copy(source, target, fetch.at[index])
            for index, (source, target) in enumerate(((fc_ref, fc_work), (proj_ref, proj_work)))
        ]
        for load in loads:
            load.start()
        greet_ctx(ctx, wt, (near, far))

        def term(item, step, source, target, peer):
            return remote(
                bufs.at[item, source], bufs.at[item, target], term_send.at[item, step], term_receive.at[item, step], peer
            )

        terms = (two_terms, out_terms)

        def begin_terms(item):
            bufs[item, 0] = terms[item][wt ^ 3].astype(low)
            term(item, 0, 0, 3, near).start()
            bufs[item, 1] = terms[item][wt ^ 1].astype(low)
            term(item, 1, 1, 4, near).start()

        def pass_terms(item):
            term(item, 0, 0, 3, near).wait_recv()
            bufs[item, 2] = (terms[item][wt ^ 2] + bufs[item, 3].astype(jnp.float32)).astype(low)
            term(item, 2, 2, 5, far).start()

        def end_terms(item):
            term(item, 1, 1, 4, near).wait_recv()
            total = terms[item][wt] + bufs[item, 4].astype(jnp.float32)
            term(item, 2, 2, 5, far).wait_recv()
            return total + bufs[item, 5].astype(jnp.float32)

        begin_terms(0)
        rings = [
            RingSum(fc_work, block, y, at_y, relay.at[0], arrive.at[0], ring_send.at[0], ring_receive.at[0]),
            RingSum(proj_work, block, z, at_z, relay.at[1], arrive.at[1], ring_send.at[1], ring_receive.at[1]),
        ]
        for load, ring in zip(loads, rings):
            load.wait()
            ring.begin()
        pass_terms(0)
        begin_terms(1)
        pass_terms(1)
        grad = end_terms(0)
        values = middle_ref[...]
        centered = values - jnp.mean(values, axis=-1, keepdims=True)
        scale = lax.rsqrt(jnp.mean(centered * centered, axis=-1, keepdims=True) + EPS)
        normed = centered * scale
        vectors_ref[0:1] = jnp.sum(grad * normed, axis=0, keepdims=True)
        vectors_ref[1:2] = jnp.sum(grad, axis=0, keepdims=True)
        weighted = grad * gain_ref[...]
        part = weighted - jnp.mean(weighted, axis=-1, keepdims=True)
        part = part - normed * jnp.mean(weighted * normed, axis=-1, keepdims=True)
        middle_grad = cot_ref[...].astype(jnp.float32) + scale * part
        middle_grad_ref[...] = middle_grad
        all_ref[wt] = middle_grad.astype(low)

        def branch(step, slot, peer):
            return remote(all_ref.at[slot], all_ref.at[slot], all_send.at[step], all_receive.at[step], peer)

        branch(0, wt, far).start()
        branch(1, wt, near).start()

        def to_head(index, other):
            return remote(
                blocks_ref.at[index], up_ref.at[ctx], head_send.at[index], head_receive.at[ctx], (other, wt)
            )

        def heads(turn, sequence):
            grads = lax.dot_general(
                wide_ref[...], all_ref[sequence], (((1,), (1,)), ((), ())), preferred_element_type=jnp.float32
            ).astype(low)
            for head in range(GROUP):
                index, other = turn * GROUP + head, sequence * GROUP + head
                blocks_ref[index] = grads[head * HEAD_DIM : (head + 1) * HEAD_DIM]

                @pl.when(other != ctx)
                def _():
                    to_head(index, other).start()

                @pl.when(other == ctx)
                def _():
                    up_ref[other] = blocks_ref[index]

        heads(0, wt)
        branch(0, wt ^ 2, far).wait_recv()
        branch(2, wt ^ 2, near).start()
        branch(1, wt ^ 1, near).wait_recv()
        heads(1, wt ^ 1)
        heads(2, wt ^ 2)
        branch(2, wt ^ 3, near).wait_recv()
        heads(3, wt ^ 3)
        for ring in rings:
            ring.pass_on()
        out_ref[...] = end_terms(1)
        fc_out[...] = rings[0].finish().astype(low)
        proj_out[...] = rings[1].finish().astype(low)

        def head_here(step, carry):
            source = (ctx + step) % 32
            remote(blocks_ref.at[0], up_ref.at[source], head_send.at[0], head_receive.at[source], (source, wt)).wait_recv()
            return carry

        @pl.when(ctx < 4 * GROUP)
        def _():
            lax.fori_loop(1, 32, head_here, 0)

        for turn, sequence in enumerate((wt, wt ^ 1, wt ^ 2, wt ^ 3)):
            for head in range(GROUP):
                index, other = turn * GROUP + head, sequence * GROUP + head

                @pl.when(other != ctx)
                def _():
                    to_head(index, other).wait_send()

        for item in range(2):
            term(item, 0, 0, 3, near).wait_send()
            term(item, 1, 1, 4, near).wait_send()
            term(item, 2, 2, 5, far).wait_send()
        branch(0, wt, far).wait_send()
        branch(1, wt, near).wait_send()
        branch(2, wt ^ 2, near).wait_send()
        for ring in rings:
            ring.drain()

    vmem = pl.BlockSpec(memory_space=pltpu.VMEM)
    hbm = pl.BlockSpec(memory_space=pl.ANY)
    cut = (block // 32) * 16 + 16
    return pl.pallas_call(
        kernel,
        out_shape=(
            jax.ShapeDtypeStruct((rows, features), jnp.float32),
            jax.ShapeDtypeStruct((rows, features), jnp.float32),
            jax.ShapeDtypeStruct((8, features), jnp.float32),
            jax.ShapeDtypeStruct((4, rows, features), low),
            jax.ShapeDtypeStruct((32, HEAD_DIM, rows), low),
            jax.ShapeDtypeStruct((block, features), low),
            jax.ShapeDtypeStruct((block, features), low),
        ),
        in_specs=[vmem, vmem, hbm, hbm, vmem, vmem, vmem, vmem],
        out_specs=(vmem,) * 7,
        scratch_shapes=[
            pltpu.VMEM(grad_fc.shape, low),
            pltpu.VMEM(grad_proj.shape, low),
            pltpu.VMEM((2, 6, rows, features), low),
            pltpu.VMEM((2, 2, cut, features), low),
            pltpu.VMEM((2, 2, block, features), low),
            pltpu.VMEM((4 * GROUP, HEAD_DIM, rows), low),
            pltpu.SemaphoreType.DMA((2, 6)),
            pltpu.SemaphoreType.DMA((2, 6)),
            pltpu.SemaphoreType.DMA((2, 3)),
            pltpu.SemaphoreType.DMA((2, 3)),
            pltpu.SemaphoreType.DMA((3,)),
            pltpu.SemaphoreType.DMA((3,)),
            pltpu.SemaphoreType.DMA((4 * GROUP,)),
            pltpu.SemaphoreType.DMA((32,)),
            pltpu.SemaphoreType.DMA((2,)),
        ],
        compiler_params=pltpu.CompilerParams(
            collective_id=collective, has_side_effects=True, vmem_limit_bytes=56 * 2**20
        ),
        name="feed_back",
    )(terms_out, terms_two, grad_fc, grad_proj, middle, gain, cotangent, wide_out)


def attend_back(upstream, inverse, place, saved, window_fc, window_proj, own_qkv, collective):
    parts, dim, rows = upstream.shape
    q, kt, k, v, attended, lse = saved
    count, block = k.shape[:2]
    per = block // rows
    features = window_fc.shape[1]
    inner = 112
    low = jnp.bfloat16
    hold, off = place // per, place % per

    def kernel(
        inverse_ref, hold_ref, off_ref, up_ref, q_ref, kt_ref, k_ref, v_ref, att_ref, lse_ref, fc_ref, proj_ref, qkv_ref,
        stacked_ref, grad_ref, fc_out, proj_out,
        up_sorted, up_rows, q_rows, delta_ref, gq_ref, gk_ref, gv_ref, blocks_ref, came_ref, turned_ref, terms_ref, bufs,
        head_send, head_receive, term_send, term_receive, *scratch,
    ):
        ctx, wt = lax.axis_index("ctx"), lax.axis_index("wt")
        y, z, low_x = ctx // 8, ctx // 2 % 4, ctx % 2
        at_y = lambda where: (where * 8 + z * 2 + low_x, wt)
        at_z = lambda where: (y * 8 + where * 2 + low_x, wt)
        near, far = (ctx, wt ^ 1), (ctx, wt ^ 2)
        fc_out[...] = fc_ref[...]
        proj_out[...] = proj_ref[...]
        greet_ctx(ctx, wt, (near, far, (ctx, wt ^ 3)))
        steps = inners((fc_out, proj_out), inner, y, z, at_y, at_z, ctx, wt, (True, False), scratch)
        for one in steps:
            one.begin()

        def arrange(index, carry):
            for sub in range(per):
                piece = up_ref[inverse_ref[index * per + sub]]
                lanes = pl.ds(sub * rows, rows)
                up_sorted[index, :, lanes] = piece
                up_rows[index, lanes, :] = piece.T
            q_rows[index] = q_ref[index].T
            delta_ref[index] = jnp.sum(up_sorted[index].astype(jnp.float32) * att_ref[index], axis=0, keepdims=True)
            gk_ref[index] = jnp.zeros((block, dim), jnp.float32)
            gv_ref[index] = jnp.zeros((block, dim), jnp.float32)
            return carry

        lax.fori_loop(0, count, arrange, 0)
        row = lax.broadcasted_iota(jnp.int32, (block, block), 0)
        col = lax.broadcasted_iota(jnp.int32, (block, block), 1)
        factor = LOG2E * dim**-0.5

        def step(qi, kj, total, diagonal):
            scores = jnp.dot(k_ref[kj], q_ref[qi], preferred_element_type=jnp.float32) * factor
            weights = jnp.exp2(scores - lse_ref[qi])
            if diagonal:
                weights = jnp.where(row <= col, weights, 0.0)
            prob_grad = jnp.dot(v_ref[kj], up_sorted[qi], preferred_element_type=jnp.float32)
            score_grad = (weights * (prob_grad - delta_ref[qi])).astype(low)
            gv_ref[kj] += jnp.dot(weights.astype(low), up_rows[qi], preferred_element_type=jnp.float32)
            gk_ref[kj] += jnp.dot(score_grad, q_rows[qi], preferred_element_type=jnp.float32)
            return total + jnp.dot(kt_ref[kj], score_grad, preferred_element_type=jnp.float32)

        def query_block(qi, carry):
            total = lax.fori_loop(
                0, qi, lambda kj, cur: step(qi, kj, cur, False), jnp.zeros((dim, block), jnp.float32)
            )
            gq_ref[qi] = step(qi, qi, total, True) * dim**-0.5
            return carry

        lax.fori_loop(0, 6, query_block, 0)
        for one in steps:
            one.add_inner()
        lax.fori_loop(6, count, query_block, 0)
        for one in steps:
            one.add_beside()

        def to_owner(index):
            return remote(blocks_ref.at[index], came_ref.at[ctx], head_send.at[index], head_receive.at[ctx], (index, wt))

        def give_back(index, carry):
            def pick(whole, axis):
                cuts = [lax.slice_in_dim(whole, sub * rows, (sub + 1) * rows, axis=axis) for sub in range(per)]
                picked = cuts[0]
                for sub in range(1, per):
                    picked = jnp.where(off_ref[index] == sub, cuts[sub], picked)
                return picked

            blocks_ref[index, :dim] = pick(gq_ref[hold_ref[index]], 1).astype(low)
            blocks_ref[index, dim : 2 * dim] = (pick(gk_ref[hold_ref[index]], 0) * dim**-0.5).T.astype(low)
            blocks_ref[index, 2 * dim :] = pick(gv_ref[hold_ref[index]], 0).T.astype(low)

            @pl.when(index != ctx)
            def _():
                to_owner(index).start()

            @pl.when(index == ctx)
            def _():
                came_ref[index] = blocks_ref[index]

            return carry

        @pl.when(ctx < 4 * GROUP)
        def _():
            lax.fori_loop(0, parts, give_back, 0)

        for one in steps:
            one.collect()

        def owner_here(source, carry):
            @pl.when(source != ctx)
            def _():
                remote(
                    blocks_ref.at[0], came_ref.at[source], head_send.at[0], head_receive.at[source], (source, wt)
                ).wait_recv()

            return carry

        lax.fori_loop(0, 4 * GROUP, owner_here, 0)
        feature = lax.broadcasted_iota(jnp.int32, (dim, rows), 0)

        def make_terms(sequence):
            for head in range(GROUP):
                piece = came_ref[sequence * GROUP + head]
                place_in = feature + head * dim
                mine = (place_in >= 16 * wt) & (place_in < 16 * wt + features // 4)
                for part in range(3):
                    start = part * SPAN + head * dim
                    turned_ref[start : start + dim] = jnp.where(
                        mine, piece[part * dim : (part + 1) * dim].astype(jnp.float32), 0.0
                    ).astype(low)
            stacked_ref[sequence] = turned_ref[...].T
            terms_ref[...] = lax.dot_general(
                stacked_ref[sequence], qkv_ref[...], (((1,), (1,)), ((), ())), preferred_element_type=jnp.float32
            )

        def term(index, source, target, peer):
            return remote(bufs.at[source], bufs.at[target], term_send.at[index], term_receive.at[index], peer)

        make_terms(wt ^ 3)
        bufs[0] = terms_ref[...].astype(low)
        term(0, 0, 3, near).start()
        make_terms(wt ^ 1)
        bufs[1] = terms_ref[...].astype(low)
        term(1, 1, 4, near).start()
        make_terms(wt ^ 2)
        term(0, 0, 3, near).wait_recv()
        bufs[2] = (terms_ref[...] + bufs[3].astype(jnp.float32)).astype(low)
        term(2, 2, 5, far).start()
        make_terms(wt)
        for one in steps:
            one.fill()
        term(1, 1, 4, near).wait_recv()
        grad_ref[...] = terms_ref[...] + bufs[4].astype(jnp.float32)
        term(2, 2, 5, far).wait_recv()
        grad_ref[...] += bufs[5].astype(jnp.float32)
        term(0, 0, 3, near).wait_send()
        term(1, 1, 4, near).wait_send()
        term(2, 2, 5, far).wait_send()

        def sent(index, carry):
            @pl.when(index != ctx)
            def _():
                to_owner(index).wait_send()

            return carry

        @pl.when(ctx < 4 * GROUP)
        def _():
            lax.fori_loop(0, parts, sent, 0)

        for one in steps:
            one.drain()

    smem = pl.BlockSpec(memory_space=pltpu.SMEM)
    vmem = pl.BlockSpec(memory_space=pltpu.VMEM)
    return pl.pallas_call(
        kernel,
        out_shape=(
            jax.ShapeDtypeStruct((4, rows, 3 * SPAN), low),
            jax.ShapeDtypeStruct((rows, features), jnp.float32),
            jax.ShapeDtypeStruct(window_fc.shape, low),
            jax.ShapeDtypeStruct(window_proj.shape, low),
        ),
        in_specs=[smem] * 3 + [vmem] * 10,
        out_specs=(vmem,) * 4,
        scratch_shapes=[
            pltpu.VMEM((count, dim, block), low),
            pltpu.VMEM((count, block, dim), low),
            pltpu.VMEM((count, block, dim), low),
            pltpu.VMEM((count, 1, block), jnp.float32),
            pltpu.VMEM((count, dim, block), jnp.float32),
            pltpu.VMEM((count, block, dim), jnp.float32),
            pltpu.VMEM((count, block, dim), jnp.float32),
            pltpu.VMEM((parts, 3 * dim, rows), low),
            pltpu.VMEM((parts, 3 * dim, rows), low),
            pltpu.VMEM((3 * SPAN, rows), low),
            pltpu.VMEM((rows, features), jnp.float32),
            pltpu.VMEM((6, rows, features), low),
            pltpu.SemaphoreType.DMA((parts,)),
            pltpu.SemaphoreType.DMA((parts,)),
            pltpu.SemaphoreType.DMA((3,)),
            pltpu.SemaphoreType.DMA((3,)),
        ]
        + inner_scratch(inner, features),
        compiler_params=pltpu.CompilerParams(
            collective_id=collective, has_side_effects=True, vmem_limit_bytes=56 * 2**20
        ),
        name="attend_back",
    )(inverse, hold, off, upstream, q, kt, k, v, attended, lse, window_fc, window_proj, own_qkv)


def finish_gradients(first, second, window_fc, window_proj, collective):
    _, size, features = first.shape
    block = window_fc.shape[0]
    inner = 64
    low = jnp.bfloat16

    def kernel(
        first_ref, second_ref, fc_ref, proj_ref, first_out, second_out, fc_out, proj_out,
        work, relay, arrive, ring_send, ring_receive, mlp_send, mlp_receive, out_send, out_receive, fetch, *scratch,
    ):
        ctx, wt = lax.axis_index("ctx"), lax.axis_index("wt")
        y, z, low_x = ctx // 8, ctx // 2 % 4, ctx % 2
        at_y = lambda place: (place * 8 + z * 2 + low_x, wt)
        at_z = lambda place: (y * 8 + place * 2 + low_x, wt)
        loads = [
            pltpu.make_async_copy(first_ref, work.at[0], fetch.at[0]),
            pltpu.make_async_copy(second_ref, work.at[1], fetch.at[1]),
            pltpu.make_async_copy(fc_ref, fc_out.at[y], fetch.at[2]),
            pltpu.make_async_copy(proj_ref, proj_out.at[z], fetch.at[3]),
        ]
        for load in loads:
            load.start()
        peers = [at_y((y + step) % 4) for step in (1, 2, 3)] + [at_z((z + step) % 4) for step in (1, 2, 3)]
        greet(peers + [(ctx ^ 1, wt)] + [(ctx, wt ^ step) for step in (1, 2, 3)])
        for load in loads:
            load.wait()
        rings = [
            RingSum(work.at[0], size, y, at_y, relay.at[0], arrive.at[0], ring_send.at[0], ring_receive.at[0]),
            RingSum(work.at[1], size, z, at_z, relay.at[1], arrive.at[1], ring_send.at[1], ring_receive.at[1]),
        ]
        mlp = [
            RingSpread(fc_out, y, at_y, mlp_send.at[0], mlp_receive.at[0]),
            RingSpread(proj_out, z, at_z, mlp_send.at[1], mlp_receive.at[1]),
        ]
        for ring in rings:
            ring.begin()
        for ring in rings:
            ring.pass_on()
        for one in mlp:
            one.begin()
        first_out[y] = rings[0].finish().astype(low)
        second_out[z] = rings[1].finish().astype(low)
        steps = inners(
            (first_out.at[y], second_out.at[z]), inner, y, z, at_y, at_z, ctx, wt, (True, z < 2), scratch
        )
        for one in steps:
            one.begin()
        for one in steps:
            one.add_inner()
        for one in steps:
            one.add_beside()
        for one in steps:
            one.collect()
        for one in mlp:
            one.pass_on()
        for one in steps:
            one.fill()
        spreads = [
            RingSpread(first_out, y, at_y, out_send.at[0], out_receive.at[0]),
            RingSpread(second_out, z, at_z, out_send.at[1], out_receive.at[1]),
        ]
        for one in spreads:
            one.begin()
        for one in spreads:
            one.pass_on()
        for one in mlp + spreads:
            one.finish()
        for one in rings + steps + mlp + spreads:
            one.drain()

    vmem = pl.BlockSpec(memory_space=pltpu.VMEM)
    hbm = pl.BlockSpec(memory_space=pl.ANY)
    cut = (size // 32) * 16 + 16
    small = jax.ShapeDtypeStruct((4, size, features), low)
    large = jax.ShapeDtypeStruct((4, block, features), low)
    return pl.pallas_call(
        kernel,
        out_shape=(small, small, large, large),
        in_specs=[hbm] * 4,
        out_specs=(vmem,) * 4,
        scratch_shapes=[
            pltpu.VMEM((2, 4 * size, features), low),
            pltpu.VMEM((2, 2, cut, features), low),
            pltpu.VMEM((2, 2, size, features), low),
            pltpu.SemaphoreType.DMA((2, 6)),
            pltpu.SemaphoreType.DMA((2, 6)),
            pltpu.SemaphoreType.DMA((2, 4)),
            pltpu.SemaphoreType.DMA((2, 4)),
            pltpu.SemaphoreType.DMA((2, 4)),
            pltpu.SemaphoreType.DMA((2, 4)),
            pltpu.SemaphoreType.DMA((4,)),
        ]
        + inner_scratch(inner, features),
        compiler_params=pltpu.CompilerParams(
            collective_id=collective, has_side_effects=True, vmem_limit_bytes=56 * 2**20
        ),
        name="finish_gradients",
    )(first.reshape(4 * size, features), second.reshape(4 * size, features), window_fc, window_proj)


def turn_rows(blocks, width):
    _, rows, features = blocks.shape
    share = features // 4

    def kernel(source, out):
        for block in range(4):
            for sender in range(4):
                part = source[block, :, sender * share : (sender + 1) * share].astype(jnp.float32).T
                start = sender * width + block * rows
                out[:, start : start + rows] = part

    vmem = pl.BlockSpec(memory_space=pltpu.VMEM)
    return pl.pallas_call(
        kernel,
        out_shape=jax.ShapeDtypeStruct((share, 4 * width), jnp.float32),
        in_specs=[vmem],
        out_specs=vmem,
        compiler_params=pltpu.CompilerParams(vmem_limit_bytes=48 * 2**20),
        name="turn_rows",
    )(blocks)


def turn_windows(first, second):
    size, features = first.shape[1:]
    share = features // 4
    rest = share - size

    def kernel(first_ref, second_ref, qkv_ref, out_ref):
        def lay(source, block, rows, start):
            for sender in range(4):
                part = source[block, :rows, sender * share : (sender + 1) * share].astype(jnp.float32).T
                at = start + sender * share
                qkv_ref[:, at : at + rows] = part

        for part, (source, block) in enumerate(((first_ref, 0), (first_ref, 2), (second_ref, 0))):
            lay(source, block, size, part * features)
            lay(source, block + 1, rest, part * features + size)
        out_ref[:size] = second_ref[2].astype(jnp.float32)
        out_ref[size:] = second_ref[3, :rest].astype(jnp.float32)

    vmem = pl.BlockSpec(memory_space=pltpu.VMEM)
    return pl.pallas_call(
        kernel,
        out_shape=(
            jax.ShapeDtypeStruct((share, 3 * features), jnp.float32),
            jax.ShapeDtypeStruct((share, features), jnp.float32),
        ),
        in_specs=[vmem] * 2,
        out_specs=(vmem,) * 2,
        compiler_params=pltpu.CompilerParams(vmem_limit_bytes=48 * 2**20),
        cost_estimate=cost(9),
        name="turn_windows",
    )(first, second)


def to_heads(rows_by_token):
    parts = rows_by_token.shape[0] // SPAN
    rows = rows_by_token.shape[1] // 4
    blocks = rows_by_token.reshape(parts, GROUP, HEAD_DIM, 4, rows).transpose(3, 1, 0, 2, 4)
    blocks = blocks.reshape(4 * GROUP, parts * HEAD_DIM, rows)
    spare = lax.axis_size("ctx") - 4 * GROUP
    return jnp.concatenate([blocks, jnp.zeros((spare,) + blocks.shape[1:], blocks.dtype)])


def from_heads(blocks):
    parts, rows = blocks.shape[1] // HEAD_DIM, blocks.shape[2]
    used = blocks[: 4 * GROUP].reshape(4, GROUP, parts, HEAD_DIM, rows)
    return used.transpose(2, 1, 3, 0, 4).reshape(parts * SPAN, 4 * rows)


def local(
    inputs,
    block_order,
    cotangent,
    ln1_gain,
    ln1_bias,
    w_qkv,
    bias_q,
    bias_v,
    w_out,
    bias_out,
    ln2_gain,
    ln2_bias,
    w_fc,
    bias_fc,
    w_proj,
    bias_proj,
):
    ctx, wt = lax.axis_index("ctx"), lax.axis_index("wt")
    ctx_count = lax.axis_size("ctx")
    rows, features = inputs.shape[1:]
    share = features // 4
    ff = w_fc.shape[1] // 4
    shift = 16 * wt

    small = jnp.stack([ln1_gain, ln1_bias, bias_q, bias_v, bias_out, ln2_gain, ln2_bias, bias_proj])
    small = jnp.pad(small, ((0, 8), (0, 0)))
    order = jnp.pad(block_order, ((0, 7), (0, 128 - ctx_count)))
    starts = [384 * member for member in range(4)]
    columns = jnp.stack(
        [
            jnp.concatenate(
                [w_qkv[:, part * features + start : part * features + start + SPAN] for part in range(3)],
                axis=1,
            )
            for start in starts
        ]
    )
    all_inputs, all_small, all_order, own_qkv = prologue((inputs[0], small, order), columns, 1)
    own_qkv = own_qkv.reshape(features, 3 * SPAN)
    vectors = all_small[:, :8].transpose(1, 0, 2).reshape(8, features).astype(jnp.float32)
    gain_one, shift_one, full_bq, full_bv, full_bout, gain_two, shift_two, full_bproj = vectors
    orders = all_order[:, 0, :ctx_count]
    place = lax.dynamic_index_in_dim(orders, jnp.minimum(ctx // GROUP, 3), 0, keepdims=False)
    slots = jnp.arange(ctx_count, dtype=jnp.int32)
    inverse = jnp.sum(jnp.where(place[None, :] == slots[:, None], slots[None, :], 0), axis=1)
    edge = SPAN - share
    below = lax.ppermute(w_out[share - edge :], "wt", [(source, (source + 1) % 4) for source in range(4)])
    above = lax.ppermute(w_out[:edge], "wt", [(source, (source - 1) % 4) for source in range(4)])
    wide_out = lax.dynamic_slice_in_dim(jnp.concatenate([below, w_out, above]), edge - shift, SPAN, 0)
    placed_out = lax.dynamic_update_slice_in_dim(jnp.zeros((SPAN, features), w_out.dtype), w_out, shift, 0)
    pieces = jnp.stack([w_fc[:, member * ff : (member + 1) * ff] for member in range(4)])

    group_tokens = all_inputs.reshape(4 * rows, features).astype(jnp.float32)
    normed_one = layer_norm(group_tokens, gain_one, shift_one).astype(jnp.bfloat16)
    bias_cols = jnp.concatenate(
        [
            lax.dynamic_slice_in_dim(full_bq, 384 * wt, SPAN),
            jnp.zeros((SPAN,), jnp.float32),
            lax.dynamic_slice_in_dim(full_bv, 384 * wt, SPAN),
        ]
    )
    projected = (dot(own_qkv, normed_one, 0, 1) + bias_cols[:, None]).astype(jnp.bfloat16)
    received = exchange(to_heads(projected), "ctx", 3)
    *saved, attended, middle, all_two, own_fc, group_cot = attend(
        received,
        inverse,
        place,
        placed_out,
        inputs[0],
        jnp.concatenate([full_bout[None], gain_two[None], shift_two[None], jnp.zeros((5, features), jnp.float32)]),
        pieces,
        cotangent[0],
        4,
    )

    tokens = inputs[0].astype(jnp.float32)
    all_two = all_two.reshape(4 * rows, features)
    own_fc = own_fc.reshape(features, ff)
    group_cot = group_cot.reshape(4 * rows, features)
    hidden_pre = dot(all_two, own_fc) + bias_fc.astype(jnp.float32)
    hidden_low = gelu_tanh(hidden_pre).astype(jnp.bfloat16)
    hidden_grad = dot(group_cot, w_proj, 1, 1)
    unused_gelu, gelu_back = jax.vjp(gelu_tanh, hidden_pre)
    pre_grad = gelu_back(hidden_grad)[0].astype(jnp.bfloat16)
    low = jnp.bfloat16
    grad_fc = dot(pre_grad, all_two, 0, 0).astype(low)
    grad_proj = dot(hidden_low, group_cot, 0, 0).astype(low)
    projected_out, middle_grad, norm_sums, all_branch, upstream, window_fc, window_proj = feed_back(
        dot(hidden_low, w_proj).reshape(4, rows, features),
        dot(pre_grad, own_fc, 1, 1).reshape(4, rows, features),
        grad_fc,
        grad_proj,
        middle,
        gain_two[None],
        cotangent[0],
        wide_out,
        7,
    )
    outputs = middle + projected_out + full_bproj
    grad_gain_two, grad_shift_two = norm_sums[0], norm_sums[1]
    all_branch = all_branch.reshape(4 * rows, features)

    stacked, normed_one_grad, window_fc, window_proj = attend_back(
        upstream, inverse, place, saved, window_fc, window_proj, own_qkv, 8
    )
    unused_first, first_back = jax.vjp(layer_norm, tokens, gain_one, shift_one)
    input_part, grad_gain_one, grad_shift_one = first_back(normed_one_grad)
    input_grad = middle_grad + input_part

    stacked = stacked.reshape(4 * rows, 3, SPAN)
    own_stacked = lax.dynamic_slice_in_dim(stacked, shift, share, 2).reshape(4 * rows, 3 * share)
    own_attended = lax.dynamic_slice_in_dim(attended.reshape(4 * rows, SPAN), shift, share, 1)
    grad_qkv = dot(own_stacked, normed_one, 0, 0).astype(low)
    grad_out = dot(own_attended, all_branch, 0, 0).astype(low)
    column = lambda value: lax.dynamic_slice_in_dim(value, share * wt, share, 0)
    sums = jnp.sum(own_stacked.astype(jnp.float32), axis=0).reshape(3, share)
    grad_bout = column(jnp.sum(all_branch.astype(jnp.float32), axis=0))
    grad_bproj = column(jnp.sum(group_cot.astype(jnp.float32), axis=0))
    grad_bfc = jnp.sum(pre_grad.astype(jnp.float32), axis=0)
    crossed_vectors = jnp.stack([grad_gain_one, grad_shift_one, grad_gain_two, grad_shift_two]).astype(low)
    kept_vectors = jnp.stack([jnp.concatenate([sums[0], sums[2], grad_bout, grad_bproj]), grad_bfc]).astype(low)
    tail = lambda value: jnp.pad(value, ((0, 16 - value.shape[0]), (0, 0)))
    spare = jnp.zeros((16, features), low)
    first = jnp.concatenate([grad_qkv[:share], tail(crossed_vectors), grad_qkv[share : 2 * share], spare])
    second = jnp.concatenate([grad_qkv[2 * share :], spare, grad_out, tail(kept_vectors)])
    window = (share + 16) // 2
    first, second, all_fc, all_proj = finish_gradients(
        first.reshape(4, window, features), second.reshape(4, window, features), window_fc, window_proj, 9
    )
    sum_fc = turn_rows(all_fc, ff)
    sum_proj = all_proj.reshape(ff, features).astype(jnp.float32)
    sum_qkv, sum_out = turn_windows(first, second)
    rest = share - window
    norms = jnp.sum(first[1, rest : rest + 4].reshape(4, 4, share).astype(jnp.float32), axis=1)
    kept_sums = second[3, rest : rest + 2].astype(jnp.float32)
    sum_bq, sum_bv, sum_bout, sum_bproj = kept_sums[0].reshape(4, share)
    return (
        outputs.astype(jnp.bfloat16)[None],
        input_grad[None],
        norms[0],
        norms[1],
        sum_qkv,
        sum_bq,
        sum_bv,
        sum_out,
        sum_bout,
        norms[2],
        norms[3],
        sum_fc,
        kept_sums[1],
        sum_proj,
        sum_bproj,
    )


def solution(mesh):
    placed = (
        P("wt", "ctx", None),
        P("wt", None),
        P("wt", "ctx", None),
        P("wt"),
        P("wt"),
        P("wt", None),
        P("wt"),
        P("wt"),
        P("wt", None),
        P("wt"),
        P("wt"),
        P("wt"),
        P("wt", None),
        P("wt"),
        P("wt", None),
        P("wt"),
    )
    return jax.shard_map(
        local,
        mesh=mesh,
        in_specs=placed,
        out_specs=(
            P("wt", "ctx", None),
            P("wt", "ctx", None),
            P("wt"),
            P("wt"),
            P("wt", None),
            P("wt"),
            P("wt"),
            P("wt", None),
            P("wt"),
            P("wt"),
            P("wt"),
            P("wt", None),
            P("wt"),
            P("wt", None),
            P("wt"),
        ),
        check_vma=False,
    )
```

```python
import math

import jax
import jax.numpy as jnp
from jax import lax
from jax.experimental import pallas as pl
from jax.experimental.pallas import tpu as pltpu
from jax.sharding import PartitionSpec as P

HEADS = 25
HEAD_DIM = 64
GROUP = 7
SPAN = GROUP * HEAD_DIM
EPS = 1e-05
MESH = pl.DeviceIdType.MESH


def cost(micros):
    return pl.CostEstimate(flops=int(micros * 1e9), bytes_accessed=int(micros * 1e6), transcendentals=0)
NEG = -1e30
LOG2E = 1.4426950408889634

def layer_norm(values, gain_row, shift_row):
    centered = values - jnp.mean(values, axis=-1, keepdims=True)
    variance = jnp.mean(centered * centered, axis=-1, keepdims=True)
    return centered * lax.rsqrt(variance + EPS) * gain_row + shift_row


def gelu_tanh(values):
    return jax.nn.gelu(values, approximate=True)


def dot(left, right, left_dim=1, right_dim=0):
    return lax.dot_general(
        left, right, (((left_dim,), (right_dim,)), ((), ())), preferred_element_type=jnp.float32
    )


def greet(peers):
    barrier = pltpu.get_barrier_semaphore()
    for peer in peers:
        pl.semaphore_signal(barrier, inc=1, device_id=peer, device_id_type=MESH)
    pl.semaphore_wait(barrier, len(peers))


def remote(source, target, send, receive, device):
    return pltpu.make_async_remote_copy(source, target, send, receive, device_id=device, device_id_type=MESH)


def greet_ctx(ctx, wt, others):
    barrier = pltpu.get_barrier_semaphore()

    def signal(step, carry):
        pl.semaphore_signal(barrier, inc=1, device_id=((ctx + step) % 32, wt), device_id_type=MESH)
        return carry

    lax.fori_loop(1, 32, signal, 0)
    for other in others:
        pl.semaphore_signal(barrier, inc=1, device_id=other, device_id_type=MESH)
    pl.semaphore_wait(barrier, 31 + len(others))


class RingSum:
    def __init__(self, source, rows, place, at, relay, arrive, send, receive):
        self.source, self.rows, self.place = source, rows, place
        self.relay, self.arrive, self.send, self.receive = relay, arrive, send, receive
        self.up, self.down = (place + 1) % 4, (place + 3) % 4
        self.to = (at(self.up), at(self.down))
        cut = (rows // 32) * 16 + 16
        self.parts = ((0, cut), (cut, rows - cut))

    def block(self, place, part):
        start, extent = self.parts[part]
        return pl.ds(pl.multiple_of(place * self.rows + start, 16), extent)

    def copy(self, index):
        first, second = self.parts
        opposite = (self.place + 2) % 4
        ends = (
            (self.source.at[self.block(opposite, 0)], self.relay.at[0, pl.ds(0, first[1])], 0),
            (self.source.at[self.block(opposite, 1)], self.relay.at[1, pl.ds(0, second[1])], 1),
            (self.source.at[self.block(self.up, 1)], self.arrive.at[0, pl.ds(*second)], 0),
            (self.source.at[self.block(self.down, 0)], self.arrive.at[1, pl.ds(*first)], 1),
            (self.source.at[self.block(self.up, 0)], self.arrive.at[0, pl.ds(*first)], 0),
            (self.source.at[self.block(self.down, 1)], self.arrive.at[1, pl.ds(*second)], 1),
        )
        source, target, way = ends[index]
        return remote(source, target, self.send.at[index], self.receive.at[index], self.to[way])

    def begin(self):
        for index in range(4):
            self.copy(index).start()

    def pass_on(self):
        for way in range(2):
            self.copy(way).wait_recv()
            extent = self.parts[way][1]
            mine = self.block(self.up if way == 0 else self.down, way)
            total = self.source[mine].astype(jnp.float32) + self.relay[way, :extent].astype(jnp.float32)
            self.source[mine] = total.astype(self.source.dtype)
            self.copy(4 + way).start()

    def finish(self):
        for index in (2, 3, 4, 5):
            self.copy(index).wait_recv()
        mine = pl.ds(pl.multiple_of(self.place * self.rows, 16), self.rows)
        total = self.source[mine].astype(jnp.float32)
        return total + self.arrive[0].astype(jnp.float32) + self.arrive[1].astype(jnp.float32)

    def drain(self):
        for index in range(6):
            self.copy(index).wait_send()


class RingSpread:
    def __init__(self, target, place, at, beside, low_x, send, receive):
        self.target, self.place, self.beside, self.send, self.receive = target, place, beside, send, receive
        self.up, self.down, self.opposite = (place + 1) % 4, (place + 3) % 4, (place + 2) % 4
        self.to = (at(self.up), at(self.down))
        rows = target.shape[1]
        alone = (rows + 40) // 80 * 16
        ring = rows - alone
        cut = (rows // 32) * 16
        row = lambda start, extent: pl.ds(pl.multiple_of(start, 16), extent)
        self.parts = (pl.ds(0, cut), pl.ds(cut, rows - cut))
        self.mine, self.other = row(low_x * ring, alone), row((1 - low_x) * ring, alone)
        self.common = row(alone, ring - alone)

    def move(self, slot, rows, index, device):
        piece = self.target.at[slot, rows]
        return remote(piece, piece, self.send.at[index], self.receive.at[index], device)

    def early(self, way, slot):
        return self.move(slot, self.mine, way, self.to[way])

    def rest(self, way, slot):
        return self.move(slot, self.common, 2 + way, self.to[way])

    def half(self, way, slot):
        return self.move(slot, self.parts[way], 4 + way, self.to[way])

    def aside(self, way, rows):
        return self.move((self.down, self.up)[way], rows, 6 + way, self.beside)

    def begin(self):
        for way in range(2):
            self.early(way, self.place).start()
        for way in range(2):
            self.rest(way, self.place).start()

    def share(self):
        for way, slot in enumerate((self.down, self.up)):
            self.early(way, slot).wait_recv()
            self.aside(way, self.mine).start()

    def pass_on(self):
        for way, slot in enumerate((self.down, self.up)):
            self.rest(way, slot).wait_recv()
            self.aside(way, self.other).wait_recv()
            self.half(way, slot).start()

    def finish(self):
        for way in range(2):
            self.half(way, self.opposite).wait_recv()

    def drain(self):
        for way, slot in enumerate((self.down, self.up)):
            self.early(way, self.place).wait_send()
            self.rest(way, self.place).wait_send()
            self.aside(way, self.mine).wait_send()
            self.half(way, slot).wait_send()


class Inner:
    def __init__(self, window, inner, place, at, ctx, wt, crosses, bufs, sems):
        self.window, self.inner, self.place, self.at, self.ctx, self.wt, self.crosses = window, inner, place, at, ctx, wt, crosses
        self.came, self.mid, self.pair, self.lanes_out, self.lanes_in, self.all = bufs
        self.inner_send, self.inner_receive, self.lane_send, self.lane_receive, self.all_send, self.all_receive, self.pair_sems = sems
        self.stride = (window.shape[0] - inner) // 3
        self.share = window.shape[1] // 4

    def rows(self, place):
        return pl.ds(pl.multiple_of(self.stride * place, 16), self.inner)

    def outward(self, step):
        other = (self.place + step) % 4
        return remote(
            self.window.at[self.rows(other)], self.came.at[step - 1],
            self.inner_send.at[step - 1], self.inner_receive.at[step - 1], self.at(other),
        )

    def beside(self):
        return remote(self.mid, self.pair, self.pair_sems.at[0], self.pair_sems.at[1], (self.ctx ^ 1, self.wt))

    def lane(self, step):
        return remote(
            self.lanes_out.at[self.wt ^ step], self.lanes_in.at[self.wt],
            self.lane_send.at[step - 1], self.lane_receive.at[step - 1], (self.ctx, self.wt ^ step),
        )

    def around(self, step):
        return remote(
            self.pair, self.all.at[self.place],
            self.all_send.at[step - 1], self.all_receive.at[step - 1], self.at((self.place + step) % 4),
        )

    def begin(self):
        for step in (1, 3, 2):
            self.outward(step).start()

    def add_inner(self):
        for step in (1, 3, 2):
            self.outward(step).wait_recv()
        total = self.window[self.rows(self.place)].astype(jnp.float32)
        for step in range(3):
            total += self.came[step].astype(jnp.float32)
        self.mid[...] = total.astype(self.mid.dtype)
        self.beside().start()

    def add_beside(self):
        self.beside().wait_recv()
        total = (self.mid[...].astype(jnp.float32) + self.pair[...].astype(jnp.float32)).astype(self.mid.dtype)
        self.pair[...] = total
        if self.crosses is False:
            self.spread()
            return
        for owner in range(4):
            self.lanes_out[owner] = total[:, owner * self.share : (owner + 1) * self.share]
        for step in (2, 3, 1):
            self.lane(step).start()
        self.lanes_in[self.wt] = self.lanes_out[self.wt]

    def spread(self):
        for step in (1, 3, 2):
            self.around(step).start()
        self.all[self.place] = self.pair[...]

    def collect(self):
        if self.crosses is False:
            return
        for step in (1, 2, 3):
            self.lane(step).wait_recv()
        for sender in range(4):
            span = slice(sender * self.share, (sender + 1) * self.share)
            part = self.lanes_in[sender]
            if self.crosses is not True:
                part = jnp.where(self.crosses, part, self.pair[:, span])
            self.pair[:, span] = part
        self.spread()

    def fill(self):
        for step in (1, 2, 3):
            self.outward(step).wait_send()
            self.around(step).wait_recv()
        for place in range(4):
            start = self.stride * place
            self.window[start : start + self.inner] = self.all[place]

    def drain(self):
        self.beside().wait_send()
        for step in (1, 2, 3):
            self.around(step).wait_send()
            if self.crosses is not False:
                self.lane(step).wait_send()


def inner_scratch(inner, features):
    low = jnp.bfloat16
    share = features // 4
    return [
        pltpu.VMEM((2, 3, inner, features), low),
        pltpu.VMEM((2, inner, features), low),
        pltpu.VMEM((2, inner, features), low),
        pltpu.VMEM((2, 4, inner, share), low),
        pltpu.VMEM((2, 4, inner, share), low),
        pltpu.VMEM((2, 4, inner, features), low),
    ] + [pltpu.SemaphoreType.DMA((2, 3))] * 6 + [pltpu.SemaphoreType.DMA((2, 2))]


def inners(windows, inner, y, z, at_y, at_z, ctx, wt, crosses, scratch):
    pick = lambda half: [ref.at[half] for ref in scratch]
    return [
        Inner(windows[0], inner, z, at_z, ctx, wt, crosses[0], pick(0)[:6], pick(0)[6:]),
        Inner(windows[1], inner, y, at_y, ctx, wt, crosses[1], pick(1)[:6], pick(1)[6:]),
    ]


def project(inputs, block_order, vectors, w_qkv, w_fc, collective):
    rows, features = inputs.shape
    share = w_qkv.shape[0]
    ff = w_fc.shape[1] // 4
    count = vectors.shape[0]
    chunks = 5
    extent = share // chunks
    low = jnp.bfloat16
    wide = 3 * SPAN

    def kernel(token_ref, order_ref, *refs):
        (
            vectors_ref, qkv_ref, fc_ref,
            received_ref, orders_ref, vec_ref, own_ref, normed_ref, fc_out,
            all_ref, small_ref, columns_ref, pieces_ref, parts_ref, sum_ref, turned_ref, blocks_ref,
            gather_send, gather_receive, cross_send, cross_receive, fc_send, fc_receive, near_send, near_receive,
            head_send, head_receive,
        ) = refs
        ctx, wt = lax.axis_index("ctx"), lax.axis_index("wt")
        low_x = ctx % 2
        near, far, beside = (ctx, wt ^ 1), (ctx, wt ^ 2), (ctx ^ 1, wt)
        goes, comes = wt ^ (2 + low_x), wt ^ (3 - low_x)
        across = (ctx ^ 1, goes)
        small_ref[wt, :count] = vectors_ref[...]
        orders_ref[wt, :1, :32] = order_ref[...]
        all_ref[wt] = token_ref[...]

        def columns(slot, owner):
            start = 384 * owner
            columns_ref[slot, :, :SPAN] = qkv_ref[:, pl.ds(pl.multiple_of(start, 128), SPAN)]
            keys = qkv_ref[:, pl.ds(pl.multiple_of(features - 64 + start, 128), SPAN + 64)]
            columns_ref[slot, :, SPAN : 2 * SPAN] = keys[:, 64:]
            columns_ref[slot, :, 2 * SPAN :] = qkv_ref[:, pl.ds(pl.multiple_of(2 * features + start, 128), SPAN)]

        def piece(target, slot, owner):
            start = pl.multiple_of(128 * ((25 * owner) // 2), 128)
            held = fc_ref[:, pl.ds(start, ff + 64)]

            @pl.when(owner % 2 == 0)
            def _():
                target[slot] = held[:, :ff]

            @pl.when(owner % 2 == 1)
            def _():
                target[slot] = held[:, 64:]

        gathered = (all_ref, small_ref, orders_ref)

        def gather(item, step, slot, peer):
            ref = gathered[item].at[slot]
            return remote(ref, ref, gather_send.at[item, step], gather_receive.at[item, step], peer)

        def cross(index):
            span = pl.ds(index * extent, extent)
            return remote(columns_ref.at[0, span], own_ref.at[wt, span], cross_send.at[0, index], cross_receive.at[0, index], across)

        def onward(index):
            part = own_ref.at[comes, pl.ds(index * extent, extent)]
            return remote(part, part, cross_send.at[1, index], cross_receive.at[1, index], beside)

        def cross_fc():
            return remote(pieces_ref.at[0], fc_out.at[wt], fc_send, fc_receive, across)

        pair = lambda: remote(columns_ref.at[1], own_ref.at[wt], near_send.at[0], near_receive.at[0], near)
        pair_fc = lambda: remote(pieces_ref.at[1], fc_out.at[wt], near_send.at[1], near_receive.at[1], near)

        columns(0, goes)
        greet_ctx(ctx, wt, (near, far, across, (ctx ^ 1, comes)))
        for item in range(3):
            gather(item, 0, wt, far).start()
        for index in range(chunks):
            cross(index).start()
        for item in range(3):
            gather(item, 1, wt, near).start()
        columns(1, wt ^ 1)
        pair().start()
        columns(2, wt)
        own_ref[wt] = columns_ref[2]
        piece(pieces_ref, 0, goes)
        piece(pieces_ref, 1, wt ^ 1)
        piece(fc_out, wt, wt)
        for item in range(3):
            gather(item, 0, wt ^ 2, far).wait_recv()
            gather(item, 2, wt ^ 2, near).start()
        for item in range(3):
            gather(item, 1, wt ^ 1, near).wait_recv()
        for item in range(3):
            gather(item, 2, wt ^ 3, near).wait_recv()
        for sender in range(4):
            span = slice(sender * share, (sender + 1) * share)
            vec_ref[:, span] = small_ref[sender, :8].astype(jnp.float32)

        def norm(sequence, carry):
            normed = layer_norm(all_ref[sequence].astype(jnp.float32), vec_ref[0:1], vec_ref[1:2]).astype(low)
            normed_ref[sequence] = normed
            tokens = pl.ds(pl.multiple_of(sequence * rows, rows), rows)
            for sender in range(4):
                parts_ref[sender, tokens] = normed[:, sender * share : (sender + 1) * share]
            return carry

        lax.fori_loop(0, 4, norm, 0)
        start = pl.ds(pl.multiple_of(384 * wt, 128), SPAN)
        bias = (vec_ref[2:3, start], jnp.zeros((1, SPAN), jnp.float32), vec_ref[3:4, start])
        for part in range(3):
            sum_ref[:, part * SPAN : (part + 1) * SPAN] = jnp.broadcast_to(bias[part], (4 * rows, SPAN))

        def add(sender):
            sum_ref[...] += jnp.dot(parts_ref[sender], own_ref[sender], preferred_element_type=jnp.float32)

        add(wt)
        pair().wait_recv()
        add(wt ^ 1)
        for index in range(chunks):
            cross(index).wait_recv()
            onward(index).start()
        cross_fc().start()
        pair_fc().start()
        add(comes)
        for index in range(chunks):
            onward(index).wait_recv()
        add(goes)

        def to_head(index):
            return remote(blocks_ref.at[index], received_ref.at[ctx], head_send.at[index], head_receive.at[ctx], (index, wt))

        def heads(sequence, carry):
            tokens = pl.ds(pl.multiple_of(sequence * rows, rows), rows)
            turned_ref[...] = sum_ref[tokens].astype(low).T
            for head in range(GROUP):
                index = sequence * GROUP + head
                for part in range(3):
                    line = part * SPAN + head * HEAD_DIM
                    blocks_ref[index, part * HEAD_DIM : (part + 1) * HEAD_DIM] = turned_ref[line : line + HEAD_DIM]

                @pl.when(index != ctx)
                def _():
                    to_head(index).start()

                @pl.when(index == ctx)
                def _():
                    received_ref[index] = blocks_ref[index]

            return carry

        lax.fori_loop(0, 4, heads, 0)

        def head_here(step, carry):
            source = (ctx + step) % 32
            remote(
                blocks_ref.at[0], received_ref.at[source], head_send.at[0], head_receive.at[source], (source, wt)
            ).wait_recv()
            return carry

        @pl.when(ctx < 4 * GROUP)
        def _():
            lax.fori_loop(1, 32, head_here, 0)

        def sent(index, carry):
            @pl.when(index != ctx)
            def _():
                to_head(index).wait_send()

            return carry

        lax.fori_loop(0, 4 * GROUP, sent, 0)
        for item in range(3):
            gather(item, 0, wt, far).wait_send()
            gather(item, 1, wt, near).wait_send()
            gather(item, 2, wt ^ 2, near).wait_send()
        pair().wait_send()
        for index in range(chunks):
            cross(index).wait_send()
            onward(index).wait_send()
        cross_fc().wait()
        pair_fc().wait()

    vmem = pl.BlockSpec(memory_space=pltpu.VMEM)
    hbm = pl.BlockSpec(memory_space=pl.ANY)
    return pl.pallas_call(
        kernel,
        out_shape=(
            jax.ShapeDtypeStruct((32, 3 * HEAD_DIM, rows), low),
            jax.ShapeDtypeStruct((4, 8, 128), jnp.int32),
            jax.ShapeDtypeStruct((8, features), jnp.float32),
            jax.ShapeDtypeStruct((4, share, wide), low),
            jax.ShapeDtypeStruct((4, rows, features), low),
            jax.ShapeDtypeStruct((4, share, ff), low),
        ),
        in_specs=[vmem] * 5,
        out_specs=(vmem,) * 6,
        scratch_shapes=[
            pltpu.VMEM((4, rows, features), low),
            pltpu.VMEM((4, 16, share), low),
            pltpu.VMEM((3, share, wide), low),
            pltpu.VMEM((2, share, ff), low),
            pltpu.VMEM((4, 4 * rows, share), low),
            pltpu.VMEM((4 * rows, wide), jnp.float32),
            pltpu.VMEM((wide, rows), low),
            pltpu.VMEM((4 * GROUP, 3 * HEAD_DIM, rows), low),
            pltpu.SemaphoreType.DMA((3, 3)),
            pltpu.SemaphoreType.DMA((3, 3)),
            pltpu.SemaphoreType.DMA((2, chunks)),
            pltpu.SemaphoreType.DMA((2, chunks)),
            pltpu.SemaphoreType.DMA,
            pltpu.SemaphoreType.DMA,
            pltpu.SemaphoreType.DMA((2,)),
            pltpu.SemaphoreType.DMA((2,)),
            pltpu.SemaphoreType.DMA((4 * GROUP,)),
            pltpu.SemaphoreType.DMA((32,)),
        ],
        compiler_params=pltpu.CompilerParams(
            collective_id=collective, has_side_effects=True, vmem_limit_bytes=56 * 2**20
        ),
        name="project",
    )(inputs, block_order, vectors, w_qkv, w_fc)


def attend(received, inverse, place, placed_out, tokens, small, pieces, cotangent, collective):
    parts, wide, rows = received.shape
    dim = wide // 3
    features = tokens.shape[1]
    block = math.gcd(512, parts * rows)
    per = block // rows
    count = parts // per
    chunks = 5
    extent = pieces.shape[1] // chunks
    low = jnp.bfloat16
    hold, off = place // per, place % per

    def kernel(
        inverse_ref, hold_ref, off_ref, in_ref, weight_ref, token_ref, small_ref, pieces_ref, cot_ref,
        q_ref, kt_ref, k_ref, v_ref, att_ref, lse_ref, stacked_ref, middle_ref, all_ref, fc_ref, all_cot_ref,
        vt_ref, blocks_ref, came_ref, turned_ref, terms_ref, bufs,
        head_send, head_receive, term_send, term_receive, all_send, all_receive,
        cross_send, cross_receive, cot_send, cot_receive,
    ):
        ctx, wt = lax.axis_index("ctx"), lax.axis_index("wt")
        low_x = ctx % 2
        near, far, beside = (ctx, wt ^ 1), (ctx, wt ^ 2), (ctx ^ 1, wt)
        comes = wt ^ (3 - low_x)
        greet_ctx(ctx, wt, (near, far))

        def onward(index):
            span = pl.ds(index * extent, extent)
            return remote(
                pieces_ref.at[comes, span], fc_ref.at[comes, span], cross_send.at[index], cross_receive.at[index], beside
            )

        def upstream(step, source, slot, peer):
            return remote(source, all_cot_ref.at[slot], cot_send.at[step], cot_receive.at[step], peer)

        for index in range(chunks):
            onward(index).start()
        upstream(0, cot_ref, wt, far).start()
        upstream(1, cot_ref, wt, near).start()
        all_cot_ref[wt] = cot_ref[...]
        for slot in (wt, wt ^ 1, comes):
            fc_ref[slot] = pieces_ref[slot]

        def arrange(index, carry):
            for sub in range(per):
                piece = in_ref[inverse_ref[index * per + sub]]
                lanes = pl.ds(sub * rows, rows)
                q_ref[index, :, lanes] = piece[:dim]
                kt_ref[index, :, lanes] = piece[dim : 2 * dim]
                vt_ref[index, :, lanes] = piece[2 * dim :]
                k_ref[index, lanes, :] = piece[dim : 2 * dim].T
                v_ref[index, lanes, :] = piece[2 * dim :].T
            return carry

        lax.fori_loop(0, count, arrange, 0)
        row = lax.broadcasted_iota(jnp.int32, (block, block), 0)
        col = lax.broadcasted_iota(jnp.int32, (block, block), 1)
        factor = LOG2E * dim**-0.5

        def step(qi, kj, carry, diagonal):
            peak, mass, total = carry
            scores = jnp.dot(k_ref[kj], q_ref[qi], preferred_element_type=jnp.float32) * factor
            if diagonal:
                scores = jnp.where(row <= col, scores, NEG)
            new_peak = jnp.maximum(peak, jnp.max(scores, axis=0, keepdims=True))
            weights = jnp.exp2(scores - new_peak)
            shrink = jnp.exp2(peak - new_peak)
            mass = mass * shrink + jnp.sum(weights, axis=0, keepdims=True)
            total = total * shrink + jnp.dot(vt_ref[kj], weights.astype(low), preferred_element_type=jnp.float32)
            return (new_peak, mass, total)

        def query_block(qi, carry):
            start = (
                jnp.full((1, block), NEG, jnp.float32),
                jnp.zeros((1, block), jnp.float32),
                jnp.zeros((dim, block), jnp.float32),
            )
            state = lax.fori_loop(0, qi, lambda kj, cur: step(qi, kj, cur, False), start)
            peak, mass, total = step(qi, qi, state, True)
            att_ref[qi] = total / mass
            lse_ref[qi] = peak + jnp.log2(mass)
            return carry

        lax.fori_loop(0, count, query_block, 0)

        def to_owner(index):
            return remote(blocks_ref.at[index], came_ref.at[ctx], head_send.at[index], head_receive.at[ctx], (index, wt))

        def give_back(index, carry):
            whole = att_ref[hold_ref[index]]
            picked = whole[:, :rows]
            for sub in range(1, per):
                picked = jnp.where(off_ref[index] == sub, whole[:, sub * rows : (sub + 1) * rows], picked)
            blocks_ref[index] = picked.astype(low)

            @pl.when(index != ctx)
            def _():
                to_owner(index).start()

            @pl.when(index == ctx)
            def _():
                came_ref[index] = blocks_ref[index]

            return carry

        @pl.when(ctx < 4 * GROUP)
        def _():
            lax.fori_loop(0, parts, give_back, 0)

        upstream(0, cot_ref, wt ^ 2, far).wait_recv()
        upstream(2, all_cot_ref.at[wt ^ 2], wt ^ 2, near).start()

        def owner_here(source, carry):
            @pl.when(source != ctx)
            def _():
                remote(
                    blocks_ref.at[0], came_ref.at[source], head_send.at[0], head_receive.at[source], (source, wt)
                ).wait_recv()

            return carry

        lax.fori_loop(0, 4 * GROUP, owner_here, 0)

        def make_terms(sequence):
            for head in range(GROUP):
                turned_ref[head * dim : (head + 1) * dim] = came_ref[sequence * GROUP + head]
            stacked_ref[sequence] = turned_ref[...].T
            terms_ref[...] = jnp.dot(stacked_ref[sequence], weight_ref[...], preferred_element_type=jnp.float32)

        def term(index, source, target, peer):
            return remote(bufs.at[source], bufs.at[target], term_send.at[index], term_receive.at[index], peer)

        make_terms(wt ^ 3)
        bufs[0] = terms_ref[...].astype(low)
        term(0, 0, 3, near).start()
        make_terms(wt ^ 1)
        bufs[1] = terms_ref[...].astype(low)
        term(1, 1, 4, near).start()
        make_terms(wt ^ 2)
        term(0, 0, 3, near).wait_recv()
        bufs[2] = (terms_ref[...] + bufs[3].astype(jnp.float32)).astype(low)
        term(2, 2, 5, far).start()
        make_terms(wt)
        middle_ref[...] = token_ref[...].astype(jnp.float32) + terms_ref[...] + small_ref[0:1]
        term(1, 1, 4, near).wait_recv()
        middle_ref[...] += bufs[4].astype(jnp.float32)
        term(2, 2, 5, far).wait_recv()
        middle_ref[...] += bufs[5].astype(jnp.float32)
        all_ref[wt] = layer_norm(middle_ref[...], small_ref[1:2], small_ref[2:3]).astype(low)

        def normed(step, slot, peer):
            return remote(all_ref.at[slot], all_ref.at[slot], all_send.at[step], all_receive.at[step], peer)

        normed(0, wt, far).start()
        normed(1, wt, near).start()
        normed(0, wt ^ 2, far).wait_recv()
        normed(2, wt ^ 2, near).start()
        normed(1, wt ^ 1, near).wait_recv()
        normed(2, wt ^ 3, near).wait_recv()
        normed(0, wt, far).wait_send()
        normed(1, wt, near).wait_send()
        normed(2, wt ^ 2, near).wait_send()
        term(0, 0, 3, near).wait_send()
        term(1, 1, 4, near).wait_send()
        term(2, 2, 5, far).wait_send()
        upstream(1, cot_ref, wt ^ 1, near).wait_recv()
        upstream(2, all_cot_ref.at[wt ^ 2], wt ^ 3, near).wait_recv()
        upstream(0, cot_ref, wt, far).wait_send()
        upstream(1, cot_ref, wt, near).wait_send()
        upstream(2, all_cot_ref.at[wt ^ 2], wt ^ 2, near).wait_send()
        for index in range(chunks):
            onward(index).wait()

        def sent(index, carry):
            @pl.when(index != ctx)
            def _():
                to_owner(index).wait_send()

            return carry

        @pl.when(ctx < 4 * GROUP)
        def _():
            lax.fori_loop(0, parts, sent, 0)

    smem = pl.BlockSpec(memory_space=pltpu.SMEM)
    vmem = pl.BlockSpec(memory_space=pltpu.VMEM)
    hbm = pl.BlockSpec(memory_space=pl.ANY)
    lane_first = jax.ShapeDtypeStruct((count, dim, block), low)
    row_first = jax.ShapeDtypeStruct((count, block, dim), low)
    return pl.pallas_call(
        kernel,
        out_shape=(
            lane_first,
            lane_first,
            row_first,
            row_first,
            jax.ShapeDtypeStruct((count, dim, block), jnp.float32),
            jax.ShapeDtypeStruct((count, 1, block), jnp.float32),
            jax.ShapeDtypeStruct((4, rows, SPAN), low),
            jax.ShapeDtypeStruct((rows, features), jnp.float32),
            jax.ShapeDtypeStruct((4, rows, features), low),
            jax.ShapeDtypeStruct(pieces.shape, low),
            jax.ShapeDtypeStruct((4, rows, features), low),
        ),
        in_specs=[smem] * 3 + [vmem] * 6,
        out_specs=(vmem,) * 11,
        scratch_shapes=[
            pltpu.VMEM((count, dim, block), low),
            pltpu.VMEM((parts, dim, rows), low),
            pltpu.VMEM((parts, dim, rows), low),
            pltpu.VMEM((SPAN, rows), low),
            pltpu.VMEM((rows, features), jnp.float32),
            pltpu.VMEM((6, rows, features), low),
            pltpu.SemaphoreType.DMA((parts,)),
            pltpu.SemaphoreType.DMA((parts,)),
            pltpu.SemaphoreType.DMA((3,)),
            pltpu.SemaphoreType.DMA((3,)),
            pltpu.SemaphoreType.DMA((3,)),
            pltpu.SemaphoreType.DMA((3,)),
            pltpu.SemaphoreType.DMA((chunks,)),
            pltpu.SemaphoreType.DMA((chunks,)),
            pltpu.SemaphoreType.DMA((3,)),
            pltpu.SemaphoreType.DMA((3,)),
        ],
        compiler_params=pltpu.CompilerParams(
            collective_id=collective, has_side_effects=True, vmem_limit_bytes=56 * 2**20
        ),
        name="attend",
    )(inverse, hold, off, received, placed_out, tokens, small, pieces, cotangent)


def feed_back(hidden, pre_grad, w_proj, own_fc, grad_fc, grad_proj, middle, gain, cotangent, wide_out, collective):
    rows, features = middle.shape
    block = grad_fc.shape[0] // 4
    low = jnp.bfloat16

    def kernel(
        hidden_ref, pre_ref, w_proj_ref, w_fc_ref, fc_ref, proj_ref, middle_ref, gain_ref, cot_ref, wide_ref,
        out_ref, middle_grad_ref, vectors_ref, all_ref, up_ref, fc_out, proj_out,
        fc_work, proj_work, terms_ref, bufs, relay, arrive, blocks_ref,
        ring_send, ring_receive, term_send, term_receive, all_send, all_receive, head_send, head_receive, fetch,
    ):
        ctx, wt = lax.axis_index("ctx"), lax.axis_index("wt")
        y, z, low_x = ctx // 8, ctx // 2 % 4, ctx % 2
        at_y = lambda place: (place * 8 + z * 2 + low_x, wt)
        at_z = lambda place: (y * 8 + place * 2 + low_x, wt)
        near, far = (ctx, wt ^ 1), (ctx, wt ^ 2)
        loads = [
            pltpu.make_async_copy(source, target, fetch.at[index])
            for index, (source, target) in enumerate(((fc_ref, fc_work), (proj_ref, proj_work)))
        ]
        for load in loads:
            load.start()
        greet_ctx(ctx, wt, (near, far))

        def term(item, step, source, target, peer):
            return remote(
                bufs.at[item, source], bufs.at[item, target], term_send.at[item, step], term_receive.at[item, step], peer
            )

        def tokens(sequence):
            return terms_ref[pl.ds(pl.multiple_of(sequence * rows, rows), rows)]

        def begin_terms(item):
            bufs[item, 0] = tokens(wt ^ 3).astype(low)
            term(item, 0, 0, 3, near).start()
            bufs[item, 1] = tokens(wt ^ 1).astype(low)
            term(item, 1, 1, 4, near).start()

        def pass_terms(item):
            term(item, 0, 0, 3, near).wait_recv()
            bufs[item, 2] = (tokens(wt ^ 2) + bufs[item, 3].astype(jnp.float32)).astype(low)
            term(item, 2, 2, 5, far).start()

        def end_terms(item):
            term(item, 1, 1, 4, near).wait_recv()
            total = tokens(wt) + bufs[item, 4].astype(jnp.float32)
            term(item, 2, 2, 5, far).wait_recv()
            return total + bufs[item, 5].astype(jnp.float32)

        rings = [
            RingSum(fc_work, block, y, at_y, relay.at[0], arrive.at[0], ring_send.at[0], ring_receive.at[0]),
            RingSum(proj_work, block, z, at_z, relay.at[1], arrive.at[1], ring_send.at[1], ring_receive.at[1]),
        ]
        for load, ring in zip(loads, rings):
            load.wait()
            ring.begin()
        terms_ref[...] = lax.dot_general(
            pre_ref[...], w_fc_ref[...], (((1,), (1,)), ((), ())), preferred_element_type=jnp.float32
        )
        begin_terms(0)
        pass_terms(0)
        grad = end_terms(0)
        values = middle_ref[...]
        centered = values - jnp.mean(values, axis=-1, keepdims=True)
        scale = lax.rsqrt(jnp.mean(centered * centered, axis=-1, keepdims=True) + EPS)
        normed = centered * scale
        vectors_ref[0:1] = jnp.sum(grad * normed, axis=0, keepdims=True)
        vectors_ref[1:2] = jnp.sum(grad, axis=0, keepdims=True)
        weighted = grad * gain_ref[...]
        part = weighted - jnp.mean(weighted, axis=-1, keepdims=True)
        part = part - normed * jnp.mean(weighted * normed, axis=-1, keepdims=True)
        middle_grad = cot_ref[...].astype(jnp.float32) + scale * part
        middle_grad_ref[...] = middle_grad
        all_ref[wt] = middle_grad.astype(low)

        def branch(step, slot, peer):
            return remote(all_ref.at[slot], all_ref.at[slot], all_send.at[step], all_receive.at[step], peer)

        branch(0, wt, far).start()
        branch(1, wt, near).start()

        def to_head(index, other):
            return remote(
                blocks_ref.at[index], up_ref.at[ctx], head_send.at[index], head_receive.at[ctx], (other, wt)
            )

        def heads(turn, sequence):
            grads = lax.dot_general(
                wide_ref[...], all_ref[sequence], (((1,), (1,)), ((), ())), preferred_element_type=jnp.float32
            ).astype(low)
            for head in range(GROUP):
                index, other = turn * GROUP + head, sequence * GROUP + head
                blocks_ref[index] = grads[head * HEAD_DIM : (head + 1) * HEAD_DIM]

                @pl.when(other != ctx)
                def _():
                    to_head(index, other).start()

                @pl.when(other == ctx)
                def _():
                    up_ref[other] = blocks_ref[index]

        heads(0, wt)
        terms_ref[...] = jnp.dot(hidden_ref[...], w_proj_ref[...], preferred_element_type=jnp.float32)
        begin_terms(1)
        branch(0, wt ^ 2, far).wait_recv()
        branch(2, wt ^ 2, near).start()
        branch(1, wt ^ 1, near).wait_recv()
        heads(1, wt ^ 1)
        heads(2, wt ^ 2)
        pass_terms(1)
        branch(2, wt ^ 3, near).wait_recv()
        heads(3, wt ^ 3)
        for ring in rings:
            ring.pass_on()
        out_ref[...] = end_terms(1)
        fc_out[...] = rings[0].finish().astype(low)
        proj_out[...] = rings[1].finish().astype(low)

        def head_here(step, carry):
            source = (ctx + step) % 32
            remote(blocks_ref.at[0], up_ref.at[source], head_send.at[0], head_receive.at[source], (source, wt)).wait_recv()
            return carry

        @pl.when(ctx < 4 * GROUP)
        def _():
            lax.fori_loop(1, 32, head_here, 0)

        for turn, sequence in enumerate((wt, wt ^ 1, wt ^ 2, wt ^ 3)):
            for head in range(GROUP):
                index, other = turn * GROUP + head, sequence * GROUP + head

                @pl.when(other != ctx)
                def _():
                    to_head(index, other).wait_send()

        for item in range(2):
            term(item, 0, 0, 3, near).wait_send()
            term(item, 1, 1, 4, near).wait_send()
            term(item, 2, 2, 5, far).wait_send()
        branch(0, wt, far).wait_send()
        branch(1, wt, near).wait_send()
        branch(2, wt ^ 2, near).wait_send()
        for ring in rings:
            ring.drain()

    vmem = pl.BlockSpec(memory_space=pltpu.VMEM)
    hbm = pl.BlockSpec(memory_space=pl.ANY)
    cut = (block // 32) * 16 + 16
    return pl.pallas_call(
        kernel,
        out_shape=(
            jax.ShapeDtypeStruct((rows, features), jnp.float32),
            jax.ShapeDtypeStruct((rows, features), jnp.float32),
            jax.ShapeDtypeStruct((8, features), jnp.float32),
            jax.ShapeDtypeStruct((4, rows, features), low),
            jax.ShapeDtypeStruct((32, HEAD_DIM, rows), low),
            jax.ShapeDtypeStruct((block, features), low),
            jax.ShapeDtypeStruct((block, features), low),
        ),
        in_specs=[vmem] * 4 + [hbm] * 2 + [vmem] * 4,
        out_specs=(vmem,) * 7,
        scratch_shapes=[
            pltpu.VMEM(grad_fc.shape, low),
            pltpu.VMEM(grad_proj.shape, low),
            pltpu.VMEM((4 * rows, features), jnp.float32),
            pltpu.VMEM((2, 6, rows, features), low),
            pltpu.VMEM((2, 2, cut, features), low),
            pltpu.VMEM((2, 2, block, features), low),
            pltpu.VMEM((4 * GROUP, HEAD_DIM, rows), low),
            pltpu.SemaphoreType.DMA((2, 6)),
            pltpu.SemaphoreType.DMA((2, 6)),
            pltpu.SemaphoreType.DMA((2, 3)),
            pltpu.SemaphoreType.DMA((2, 3)),
            pltpu.SemaphoreType.DMA((3,)),
            pltpu.SemaphoreType.DMA((3,)),
            pltpu.SemaphoreType.DMA((4 * GROUP,)),
            pltpu.SemaphoreType.DMA((32,)),
            pltpu.SemaphoreType.DMA((2,)),
        ],
        compiler_params=pltpu.CompilerParams(
            collective_id=collective, has_side_effects=True, vmem_limit_bytes=56 * 2**20
        ),
        name="feed_back",
    )(hidden, pre_grad, w_proj, own_fc, grad_fc, grad_proj, middle, gain, cotangent, wide_out)


def attend_back(upstream, inverse, place, saved, window_fc, window_proj, own_qkv, collective):
    parts, dim, rows = upstream.shape
    q, kt, k, v, attended, lse = saved
    count, block = k.shape[:2]
    per = block // rows
    features = window_fc.shape[1]
    inner = 112
    low = jnp.bfloat16
    hold, off = place // per, place % per

    def kernel(
        inverse_ref, hold_ref, off_ref, up_ref, q_ref, kt_ref, k_ref, v_ref, att_ref, lse_ref, fc_ref, proj_ref, qkv_ref,
        stacked_ref, grad_ref, fc_out, proj_out,
        up_sorted, up_rows, q_rows, delta_ref, gq_ref, gk_ref, gv_ref, blocks_ref, came_ref, turned_ref, terms_ref, bufs,
        head_send, head_receive, term_send, term_receive, *scratch,
    ):
        ctx, wt = lax.axis_index("ctx"), lax.axis_index("wt")
        y, z, low_x = ctx // 8, ctx // 2 % 4, ctx % 2
        at_y = lambda where: (where * 8 + z * 2 + low_x, wt)
        at_z = lambda where: (y * 8 + where * 2 + low_x, wt)
        near, far = (ctx, wt ^ 1), (ctx, wt ^ 2)
        fc_out[...] = fc_ref[...]
        proj_out[...] = proj_ref[...]
        greet_ctx(ctx, wt, (near, far, (ctx, wt ^ 3)))
        steps = inners((fc_out, proj_out), inner, y, z, at_y, at_z, ctx, wt, (True, False), scratch)
        for one in steps:
            one.begin()

        def arrange(index, carry):
            for sub in range(per):
                piece = up_ref[inverse_ref[index * per + sub]]
                lanes = pl.ds(sub * rows, rows)
                up_sorted[index, :, lanes] = piece
                up_rows[index, lanes, :] = piece.T
            q_rows[index] = q_ref[index].T
            delta_ref[index] = jnp.sum(up_sorted[index].astype(jnp.float32) * att_ref[index], axis=0, keepdims=True)
            gk_ref[index] = jnp.zeros((block, dim), jnp.float32)
            gv_ref[index] = jnp.zeros((block, dim), jnp.float32)
            return carry

        lax.fori_loop(0, count, arrange, 0)
        row = lax.broadcasted_iota(jnp.int32, (block, block), 0)
        col = lax.broadcasted_iota(jnp.int32, (block, block), 1)
        factor = LOG2E * dim**-0.5

        def step(qi, kj, total, diagonal):
            scores = jnp.dot(k_ref[kj], q_ref[qi], preferred_element_type=jnp.float32) * factor
            weights = jnp.exp2(scores - lse_ref[qi])
            if diagonal:
                weights = jnp.where(row <= col, weights, 0.0)
            prob_grad = jnp.dot(v_ref[kj], up_sorted[qi], preferred_element_type=jnp.float32)
            score_grad = (weights * (prob_grad - delta_ref[qi])).astype(low)
            gv_ref[kj] += jnp.dot(weights.astype(low), up_rows[qi], preferred_element_type=jnp.float32)
            gk_ref[kj] += jnp.dot(score_grad, q_rows[qi], preferred_element_type=jnp.float32)
            return total + jnp.dot(kt_ref[kj], score_grad, preferred_element_type=jnp.float32)

        def query_block(qi, carry):
            total = lax.fori_loop(
                0, qi, lambda kj, cur: step(qi, kj, cur, False), jnp.zeros((dim, block), jnp.float32)
            )
            gq_ref[qi] = step(qi, qi, total, True) * dim**-0.5
            return carry

        lax.fori_loop(0, 6, query_block, 0)
        for one in steps:
            one.add_inner()
        lax.fori_loop(6, count, query_block, 0)
        for one in steps:
            one.add_beside()

        def to_owner(index):
            return remote(blocks_ref.at[index], came_ref.at[ctx], head_send.at[index], head_receive.at[ctx], (index, wt))

        def give_back(index, carry):
            def pick(whole, axis):
                cuts = [lax.slice_in_dim(whole, sub * rows, (sub + 1) * rows, axis=axis) for sub in range(per)]
                picked = cuts[0]
                for sub in range(1, per):
                    picked = jnp.where(off_ref[index] == sub, cuts[sub], picked)
                return picked

            blocks_ref[index, :dim] = pick(gq_ref[hold_ref[index]], 1).astype(low)
            blocks_ref[index, dim : 2 * dim] = (pick(gk_ref[hold_ref[index]], 0) * dim**-0.5).T.astype(low)
            blocks_ref[index, 2 * dim :] = pick(gv_ref[hold_ref[index]], 0).T.astype(low)

            @pl.when(index != ctx)
            def _():
                to_owner(index).start()

            @pl.when(index == ctx)
            def _():
                came_ref[index] = blocks_ref[index]

            return carry

        @pl.when(ctx < 4 * GROUP)
        def _():
            lax.fori_loop(0, parts, give_back, 0)

        def owner_here(source, carry):
            @pl.when(source != ctx)
            def _():
                remote(
                    blocks_ref.at[0], came_ref.at[source], head_send.at[0], head_receive.at[source], (source, wt)
                ).wait_recv()

            return carry

        lax.fori_loop(0, 4 * GROUP, owner_here, 0)
        for one in steps:
            one.collect()
        feature = lax.broadcasted_iota(jnp.int32, (dim, rows), 0)

        def make_terms(sequence):
            for head in range(GROUP):
                piece = came_ref[sequence * GROUP + head]
                place_in = feature + head * dim
                mine = (place_in >= 16 * wt) & (place_in < 16 * wt + features // 4)
                for part in range(3):
                    start = part * SPAN + head * dim
                    turned_ref[start : start + dim] = jnp.where(
                        mine, piece[part * dim : (part + 1) * dim].astype(jnp.float32), 0.0
                    ).astype(low)
            stacked_ref[sequence] = turned_ref[...].T
            terms_ref[...] = lax.dot_general(
                stacked_ref[sequence], qkv_ref[...], (((1,), (1,)), ((), ())), preferred_element_type=jnp.float32
            )

        def term(index, source, target, peer):
            return remote(bufs.at[source], bufs.at[target], term_send.at[index], term_receive.at[index], peer)

        make_terms(wt ^ 3)
        bufs[0] = terms_ref[...].astype(low)
        term(0, 0, 3, near).start()
        make_terms(wt ^ 1)
        bufs[1] = terms_ref[...].astype(low)
        term(1, 1, 4, near).start()
        make_terms(wt ^ 2)
        term(0, 0, 3, near).wait_recv()
        bufs[2] = (terms_ref[...] + bufs[3].astype(jnp.float32)).astype(low)
        term(2, 2, 5, far).start()
        make_terms(wt)
        term(1, 1, 4, near).wait_recv()
        grad_ref[...] = terms_ref[...] + bufs[4].astype(jnp.float32)
        term(2, 2, 5, far).wait_recv()
        grad_ref[...] += bufs[5].astype(jnp.float32)
        term(0, 0, 3, near).wait_send()
        term(1, 1, 4, near).wait_send()
        term(2, 2, 5, far).wait_send()

        def sent(index, carry):
            @pl.when(index != ctx)
            def _():
                to_owner(index).wait_send()

            return carry

        @pl.when(ctx < 4 * GROUP)
        def _():
            lax.fori_loop(0, parts, sent, 0)

        for one in steps:
            one.fill()
        for one in steps:
            one.drain()

    smem = pl.BlockSpec(memory_space=pltpu.SMEM)
    vmem = pl.BlockSpec(memory_space=pltpu.VMEM)
    return pl.pallas_call(
        kernel,
        out_shape=(
            jax.ShapeDtypeStruct((4, rows, 3 * SPAN), low),
            jax.ShapeDtypeStruct((rows, features), jnp.float32),
            jax.ShapeDtypeStruct(window_fc.shape, low),
            jax.ShapeDtypeStruct(window_proj.shape, low),
        ),
        in_specs=[smem] * 3 + [vmem] * 10,
        out_specs=(vmem,) * 4,
        scratch_shapes=[
            pltpu.VMEM((count, dim, block), low),
            pltpu.VMEM((count, block, dim), low),
            pltpu.VMEM((count, block, dim), low),
            pltpu.VMEM((count, 1, block), jnp.float32),
            pltpu.VMEM((count, dim, block), jnp.float32),
            pltpu.VMEM((count, block, dim), jnp.float32),
            pltpu.VMEM((count, block, dim), jnp.float32),
            pltpu.VMEM((parts, 3 * dim, rows), low),
            pltpu.VMEM((parts, 3 * dim, rows), low),
            pltpu.VMEM((3 * SPAN, rows), low),
            pltpu.VMEM((rows, features), jnp.float32),
            pltpu.VMEM((6, rows, features), low),
            pltpu.SemaphoreType.DMA((parts,)),
            pltpu.SemaphoreType.DMA((parts,)),
            pltpu.SemaphoreType.DMA((3,)),
            pltpu.SemaphoreType.DMA((3,)),
        ]
        + inner_scratch(inner, features),
        compiler_params=pltpu.CompilerParams(
            collective_id=collective, has_side_effects=True, vmem_limit_bytes=56 * 2**20
        ),
        name="attend_back",
    )(inverse, hold, off, upstream, q, kt, k, v, attended, lse, window_fc, window_proj, own_qkv)


def finish_gradients(grad_qkv, grad_out, crossed, kept, window_fc, window_proj, collective):
    share, features = grad_out.shape
    extra = crossed.shape[0]
    size = (share + extra) // 2
    block = window_fc.shape[0]
    inner = 64
    low = jnp.bfloat16

    def kernel(
        qkv_ref, out_ref, crossed_ref, kept_ref, fc_ref, proj_ref,
        qkv_turned, out_rows, crossed_rows, kept_rows, fc_turned, proj_out,
        first_out, second_out, fc_out, work, relay, arrive, ring_send, ring_receive, mlp_send, mlp_receive, out_send, out_receive, fetch, *scratch,
    ):
        ctx, wt = lax.axis_index("ctx"), lax.axis_index("wt")
        y, z, low_x = ctx // 8, ctx // 2 % 4, ctx % 2
        at_y = lambda place: (place * 8 + z * 2 + low_x, wt)
        at_z = lambda place: (y * 8 + place * 2 + low_x, wt)
        moves = [
            (qkv_ref.at[pl.ds(0, share)], work.at[0, pl.ds(0, share)]),
            (crossed_ref, work.at[0, pl.ds(share, extra)]),
            (qkv_ref.at[pl.ds(share, share)], work.at[0, pl.ds(share + extra, share)]),
            (qkv_ref.at[pl.ds(2 * share, share)], work.at[1, pl.ds(0, share)]),
            (out_ref, work.at[1, pl.ds(share + extra, share)]),
            (kept_ref, work.at[1, pl.ds(2 * share + extra, extra)]),
        ]
        moves += [(fc_ref, fc_out.at[y]), (proj_ref, proj_out.at[z])]
        loads = [pltpu.make_async_copy(source, target, fetch.at[index]) for index, (source, target) in enumerate(moves)]
        work[0, 2 * share + extra :] = jnp.zeros((extra, features), low)
        work[1, share : share + extra] = jnp.zeros((extra, features), low)
        for load in loads:
            load.start()
        peers = [at_y((y + step) % 4) for step in (1, 2, 3)] + [at_z((z + step) % 4) for step in (1, 2, 3)]
        greet(peers + [(ctx ^ 1, wt)] + [(ctx, wt ^ step) for step in (1, 2, 3)])
        for load in loads[:6]:
            load.wait()
        rings = [
            RingSum(work.at[0], size, y, at_y, relay.at[0], arrive.at[0], ring_send.at[0], ring_receive.at[0]),
            RingSum(work.at[1], size, z, at_z, relay.at[1], arrive.at[1], ring_send.at[1], ring_receive.at[1]),
        ]
        beside = (ctx ^ 1, wt)
        mlp = [
            RingSpread(fc_out, y, at_y, beside, low_x, mlp_send.at[0], mlp_receive.at[0]),
            RingSpread(proj_out, z, at_z, beside, low_x, mlp_send.at[1], mlp_receive.at[1]),
        ]
        for ring in rings:
            ring.begin()
        for load in loads[6:]:
            load.wait()
        for ring in rings:
            ring.pass_on()
        for one in mlp:
            one.begin()
        first_out[y] = rings[0].finish().astype(low)
        second_out[z] = rings[1].finish().astype(low)
        steps = inners(
            (first_out.at[y], second_out.at[z]), inner, y, z, at_y, at_z, ctx, wt, (True, z < 2), scratch
        )
        for one in steps:
            one.begin()
        for one in mlp:
            one.share()
        for one in steps:
            one.add_inner()
        for one in steps:
            one.add_beside()
        for one in steps:
            one.collect()
        for one in mlp:
            one.pass_on()
        for one in steps:
            one.fill()
        spreads = [
            RingSpread(first_out, y, at_y, beside, low_x, out_send.at[0], out_receive.at[0]),
            RingSpread(second_out, z, at_z, beside, low_x, out_send.at[1], out_receive.at[1]),
        ]
        for one in spreads:
            one.begin()
        for one in mlp:
            one.finish()
        for one in spreads:
            one.share()

        def turn(source, place, extent, target, start, width):
            for sender in range(4):
                part = source[place, :extent, sender * share : (sender + 1) * share].astype(jnp.float32).T.astype(low)
                at = start + sender * width
                target[:, at : at + extent] = part

        turn(fc_out, 0, block, fc_turned, 0, 4 * block)
        for one in spreads:
            one.pass_on()
        for place in range(1, 4):
            turn(fc_out, place, block, fc_turned, place * block, 4 * block)
        for one in spreads:
            one.finish()
        left = share - size
        for part, (source, place) in enumerate(((first_out, 0), (first_out, 2), (second_out, 0))):
            turn(source, place, size, qkv_turned, part * features, share)
            turn(source, place + 1, left, qkv_turned, part * features + size, share)
        out_rows[:size] = second_out[2]
        out_rows[size:] = second_out[3, :left]
        crossed_rows[...] = first_out[1, left:]
        kept_rows[...] = second_out[3, left:]
        for one in rings + steps + mlp + spreads:
            one.drain()

    vmem = pl.BlockSpec(memory_space=pltpu.VMEM)
    hbm = pl.BlockSpec(memory_space=pl.ANY)
    cut = (size // 32) * 16 + 16
    return pl.pallas_call(
        kernel,
        out_shape=(
            jax.ShapeDtypeStruct((share, 3 * features), low),
            jax.ShapeDtypeStruct((share, features), low),
            jax.ShapeDtypeStruct((extra, features), low),
            jax.ShapeDtypeStruct((extra, features), low),
            jax.ShapeDtypeStruct((share, 16 * block), low),
            jax.ShapeDtypeStruct((4, block, features), low),
        ),
        in_specs=[hbm] * 6,
        out_specs=(vmem,) * 6,
        scratch_shapes=[
            pltpu.VMEM((4, size, features), low),
            pltpu.VMEM((4, size, features), low),
            pltpu.VMEM((4, block, features), low),
            pltpu.VMEM((2, 4 * size, features), low),
            pltpu.VMEM((2, 2, cut, features), low),
            pltpu.VMEM((2, 2, size, features), low),
            pltpu.SemaphoreType.DMA((2, 6)),
            pltpu.SemaphoreType.DMA((2, 6)),
            pltpu.SemaphoreType.DMA((2, 8)),
            pltpu.SemaphoreType.DMA((2, 8)),
            pltpu.SemaphoreType.DMA((2, 8)),
            pltpu.SemaphoreType.DMA((2, 8)),
            pltpu.SemaphoreType.DMA((8,)),
        ]
        + inner_scratch(inner, features),
        compiler_params=pltpu.CompilerParams(
            collective_id=collective, has_side_effects=True, vmem_limit_bytes=56 * 2**20
        ),
        name="finish_gradients",
    )(grad_qkv, grad_out, crossed, kept, window_fc, window_proj)


def local(
    inputs,
    block_order,
    cotangent,
    ln1_gain,
    ln1_bias,
    w_qkv,
    bias_q,
    bias_v,
    w_out,
    bias_out,
    ln2_gain,
    ln2_bias,
    w_fc,
    bias_fc,
    w_proj,
    bias_proj,
):
    ctx, wt = lax.axis_index("ctx"), lax.axis_index("wt")
    ctx_count = lax.axis_size("ctx")
    rows, features = inputs.shape[1:]
    share = features // 4
    ff = w_fc.shape[1] // 4
    shift = 16 * wt

    small = jnp.stack([ln1_gain, ln1_bias, bias_q, bias_v, bias_out, ln2_gain, ln2_bias, bias_proj])
    received, all_order, vectors, own_qkv, normed_one, pieces = project(
        inputs[0], block_order, small, w_qkv, w_fc, 1
    )
    own_qkv = own_qkv.reshape(features, 3 * SPAN)
    normed_one = normed_one.reshape(4 * rows, features)
    gain_one, shift_one, _, _, full_bout, gain_two, shift_two, full_bproj = vectors
    orders = all_order[:, 0, :ctx_count]
    place = lax.dynamic_index_in_dim(orders, jnp.minimum(ctx // GROUP, 3), 0, keepdims=False)
    slots = jnp.arange(ctx_count, dtype=jnp.int32)
    inverse = jnp.sum(jnp.where(place[None, :] == slots[:, None], slots[None, :], 0), axis=1)
    edge = SPAN - share
    below = lax.ppermute(w_out[share - edge :], "wt", [(source, (source + 1) % 4) for source in range(4)])
    above = lax.ppermute(w_out[:edge], "wt", [(source, (source - 1) % 4) for source in range(4)])
    wide_out = lax.dynamic_slice_in_dim(jnp.concatenate([below, w_out, above]), edge - shift, SPAN, 0)
    placed_out = lax.dynamic_update_slice_in_dim(jnp.zeros((SPAN, features), w_out.dtype), w_out, shift, 0)

    *saved, attended, middle, all_two, own_fc, group_cot = attend(
        received,
        inverse,
        place,
        placed_out,
        inputs[0],
        jnp.concatenate([full_bout[None], gain_two[None], shift_two[None], jnp.zeros((5, features), jnp.float32)]),
        pieces,
        cotangent[0],
        4,
    )

    tokens = inputs[0].astype(jnp.float32)
    all_two = all_two.reshape(4 * rows, features)
    own_fc = own_fc.reshape(features, ff)
    group_cot = group_cot.reshape(4 * rows, features)
    hidden_pre = dot(all_two, own_fc) + bias_fc.astype(jnp.float32)
    hidden_low = gelu_tanh(hidden_pre).astype(jnp.bfloat16)
    hidden_grad = dot(group_cot, w_proj, 1, 1)
    unused_gelu, gelu_back = jax.vjp(gelu_tanh, hidden_pre)
    pre_grad = gelu_back(hidden_grad)[0].astype(jnp.bfloat16)
    low = jnp.bfloat16
    grad_fc = dot(pre_grad, all_two, 0, 0).astype(low)
    grad_proj = dot(hidden_low, group_cot, 0, 0).astype(low)
    projected_out, middle_grad, norm_sums, all_branch, upstream, window_fc, window_proj = feed_back(
        hidden_low,
        pre_grad,
        w_proj,
        own_fc,
        grad_fc,
        grad_proj,
        middle,
        gain_two[None],
        cotangent[0],
        wide_out,
        7,
    )
    outputs = middle + projected_out + full_bproj
    grad_gain_two, grad_shift_two = norm_sums[0], norm_sums[1]
    all_branch = all_branch.reshape(4 * rows, features)

    stacked, normed_one_grad, window_fc, window_proj = attend_back(
        upstream, inverse, place, saved, window_fc, window_proj, own_qkv, 8
    )
    unused_first, first_back = jax.vjp(layer_norm, tokens, gain_one, shift_one)
    input_part, grad_gain_one, grad_shift_one = first_back(normed_one_grad)
    input_grad = middle_grad + input_part

    stacked = stacked.reshape(4 * rows, 3, SPAN)
    own_stacked = lax.dynamic_slice_in_dim(stacked, shift, share, 2).reshape(4 * rows, 3 * share)
    own_attended = lax.dynamic_slice_in_dim(attended.reshape(4 * rows, SPAN), shift, share, 1)
    grad_qkv = dot(own_stacked, normed_one, 0, 0).astype(low)
    grad_out = dot(own_attended, all_branch, 0, 0).astype(low)
    column = lambda value: lax.dynamic_slice_in_dim(value, share * wt, share, 0)
    sums = jnp.sum(own_stacked.astype(jnp.float32), axis=0).reshape(3, share)
    grad_bout = column(jnp.sum(all_branch.astype(jnp.float32), axis=0))
    grad_bproj = column(jnp.sum(group_cot.astype(jnp.float32), axis=0))
    grad_bfc = jnp.sum(pre_grad.astype(jnp.float32), axis=0)
    crossed_vectors = jnp.stack([grad_gain_one, grad_shift_one, grad_gain_two, grad_shift_two]).astype(low)
    kept_vectors = jnp.stack([jnp.concatenate([sums[0], sums[2], grad_bout, grad_bproj]), grad_bfc]).astype(low)
    tail = lambda value: jnp.pad(value, ((0, 16 - value.shape[0]), (0, 0)))
    sum_qkv, sum_out, crossed, kept, sum_fc, sum_proj = finish_gradients(
        grad_qkv, grad_out, tail(crossed_vectors), tail(kept_vectors), window_fc, window_proj, 9
    )
    sum_qkv, sum_out, sum_fc = (member.astype(jnp.float32) for member in (sum_qkv, sum_out, sum_fc))
    sum_proj = sum_proj.reshape(ff, features).astype(jnp.float32)
    norms = jnp.sum(crossed[:4].reshape(4, 4, share).astype(jnp.float32), axis=1)
    kept_sums = kept[:2].astype(jnp.float32)
    sum_bq, sum_bv, sum_bout, sum_bproj = kept_sums[0].reshape(4, share)
    return (
        outputs.astype(jnp.bfloat16)[None],
        input_grad[None],
        norms[0],
        norms[1],
        sum_qkv,
        sum_bq,
        sum_bv,
        sum_out,
        sum_bout,
        norms[2],
        norms[3],
        sum_fc,
        kept_sums[1],
        sum_proj,
        sum_bproj,
    )


def solution(mesh):
    placed = (
        P("wt", "ctx", None),
        P("wt", None),
        P("wt", "ctx", None),
        P("wt"),
        P("wt"),
        P("wt", None),
        P("wt"),
        P("wt"),
        P("wt", None),
        P("wt"),
        P("wt"),
        P("wt"),
        P("wt", None),
        P("wt"),
        P("wt", None),
        P("wt"),
    )
    return jax.shard_map(
        local,
        mesh=mesh,
        in_specs=placed,
        out_specs=(
            P("wt", "ctx", None),
            P("wt", "ctx", None),
            P("wt"),
            P("wt"),
            P("wt", None),
            P("wt"),
            P("wt"),
            P("wt", None),
            P("wt"),
            P("wt"),
            P("wt"),
            P("wt", None),
            P("wt"),
            P("wt", None),
            P("wt"),
        ),
        check_vma=False,
    )
```

```python
import math

import jax
import jax.numpy as jnp
from jax import lax
from jax.experimental import pallas as pl
from jax.experimental.pallas import tpu as pltpu
from jax.sharding import PartitionSpec as P

HEADS = 25
HEAD_DIM = 64
GROUP = 7
SPAN = GROUP * HEAD_DIM
EPS = 1e-05
MESH = pl.DeviceIdType.MESH


def cost(micros):
    return pl.CostEstimate(flops=int(micros * 1e9), bytes_accessed=int(micros * 1e6), transcendentals=0)
NEG = -1e30
LOG2E = 1.4426950408889634

def layer_norm(values, gain_row, shift_row):
    centered = values - jnp.mean(values, axis=-1, keepdims=True)
    variance = jnp.mean(centered * centered, axis=-1, keepdims=True)
    return centered * lax.rsqrt(variance + EPS) * gain_row + shift_row


def gelu_tanh(values):
    return jax.nn.gelu(values, approximate=True)


def dot(left, right, left_dim=1, right_dim=0):
    return lax.dot_general(
        left, right, (((left_dim,), (right_dim,)), ((), ())), preferred_element_type=jnp.float32
    )


def greet(peers):
    barrier = pltpu.get_barrier_semaphore()
    for peer in peers:
        pl.semaphore_signal(barrier, inc=1, device_id=peer, device_id_type=MESH)
    pl.semaphore_wait(barrier, len(peers))


def remote(source, target, send, receive, device):
    return pltpu.make_async_remote_copy(source, target, send, receive, device_id=device, device_id_type=MESH)


def greet_ctx(ctx, wt, others):
    barrier = pltpu.get_barrier_semaphore()

    def signal(step, carry):
        pl.semaphore_signal(barrier, inc=1, device_id=((ctx + step) % 32, wt), device_id_type=MESH)
        return carry

    lax.fori_loop(1, 32, signal, 0)
    for other in others:
        pl.semaphore_signal(barrier, inc=1, device_id=other, device_id_type=MESH)
    pl.semaphore_wait(barrier, 31 + len(others))


class RingSum:
    def __init__(self, source, rows, place, at, relay, arrive, send, receive):
        self.source, self.rows, self.place = source, rows, place
        self.relay, self.arrive, self.send, self.receive = relay, arrive, send, receive
        self.up, self.down = (place + 1) % 4, (place + 3) % 4
        self.to = (at(self.up), at(self.down))
        cut = (rows // 32) * 16 + 16
        self.parts = ((0, cut), (cut, rows - cut))

    def block(self, place, part):
        start, extent = self.parts[part]
        return pl.ds(pl.multiple_of(place * self.rows + start, 16), extent)

    def copy(self, index):
        first, second = self.parts
        opposite = (self.place + 2) % 4
        ends = (
            (self.source.at[self.block(opposite, 0)], self.relay.at[0, pl.ds(0, first[1])], 0),
            (self.source.at[self.block(opposite, 1)], self.relay.at[1, pl.ds(0, second[1])], 1),
            (self.source.at[self.block(self.up, 1)], self.arrive.at[0, pl.ds(*second)], 0),
            (self.source.at[self.block(self.down, 0)], self.arrive.at[1, pl.ds(*first)], 1),
            (self.source.at[self.block(self.up, 0)], self.arrive.at[0, pl.ds(*first)], 0),
            (self.source.at[self.block(self.down, 1)], self.arrive.at[1, pl.ds(*second)], 1),
        )
        source, target, way = ends[index]
        return remote(source, target, self.send.at[index], self.receive.at[index], self.to[way])

    def begin(self):
        for index in range(4):
            self.copy(index).start()

    def pass_on(self):
        for way in range(2):
            self.copy(way).wait_recv()
            extent = self.parts[way][1]
            mine = self.block(self.up if way == 0 else self.down, way)
            total = self.source[mine].astype(jnp.float32) + self.relay[way, :extent].astype(jnp.float32)
            self.source[mine] = total.astype(self.source.dtype)
            self.copy(4 + way).start()

    def finish(self):
        for index in (2, 3, 4, 5):
            self.copy(index).wait_recv()
        mine = pl.ds(pl.multiple_of(self.place * self.rows, 16), self.rows)
        total = self.source[mine].astype(jnp.float32)
        return total + self.arrive[0].astype(jnp.float32) + self.arrive[1].astype(jnp.float32)

    def drain(self):
        for index in range(6):
            self.copy(index).wait_send()


class RingSpread:
    def __init__(self, target, place, at, beside, low_x, alone, send, receive):
        self.target, self.place, self.beside, self.send, self.receive = target, place, beside, send, receive
        self.up, self.down, self.opposite = (place + 1) % 4, (place + 3) % 4, (place + 2) % 4
        self.to = (at(self.up), at(self.down))
        rows = target.shape[1]
        ring = rows - alone
        cut = (rows // 32) * 16
        row = lambda start, extent: pl.ds(pl.multiple_of(start, 16), extent)
        self.parts = (pl.ds(0, cut), pl.ds(cut, rows - cut))
        self.mine, self.other = row(low_x * ring, alone), row((1 - low_x) * ring, alone)
        self.common = row(alone, ring - alone)

    def move(self, slot, rows, index, device):
        piece = self.target.at[slot, rows]
        return remote(piece, piece, self.send.at[index], self.receive.at[index], device)

    def early(self, way, slot):
        return self.move(slot, self.mine, way, self.to[way])

    def rest(self, way, slot):
        return self.move(slot, self.common, 2 + way, self.to[way])

    def half(self, way, slot):
        return self.move(slot, self.parts[way], 4 + way, self.to[way])

    def aside(self, way, rows):
        return self.move((self.down, self.up)[way], rows, 6 + way, self.beside)

    def begin(self):
        for way in range(2):
            self.early(way, self.place).start()

    def go_on(self):
        for way in range(2):
            self.rest(way, self.place).start()

    def share(self):
        for way, slot in enumerate((self.down, self.up)):
            self.early(way, slot).wait_recv()
            self.aside(way, self.mine).start()

    def pass_on(self):
        for way, slot in enumerate((self.down, self.up)):
            self.rest(way, slot).wait_recv()
            self.aside(way, self.other).wait_recv()
            self.half(way, slot).start()

    def finish(self):
        for way in range(2):
            self.half(way, self.opposite).wait_recv()

    def drain(self):
        for way, slot in enumerate((self.down, self.up)):
            self.early(way, self.place).wait_send()
            self.rest(way, self.place).wait_send()
            self.aside(way, self.mine).wait_send()
            self.half(way, slot).wait_send()


class Inner:
    def __init__(self, window, inner, place, at, ctx, wt, crosses, bufs, sems):
        self.window, self.inner, self.place, self.at, self.ctx, self.wt, self.crosses = window, inner, place, at, ctx, wt, crosses
        self.came, self.mid, self.pair, self.lanes_out, self.lanes_in, self.all = bufs
        self.inner_send, self.inner_receive, self.lane_send, self.lane_receive, self.all_send, self.all_receive, self.pair_sems = sems
        self.stride = (window.shape[0] - inner) // 3
        self.share = window.shape[1] // 4

    def rows(self, place):
        return pl.ds(pl.multiple_of(self.stride * place, 16), self.inner)

    def outward(self, step):
        other = (self.place + step) % 4
        return remote(
            self.window.at[self.rows(other)], self.came.at[step - 1],
            self.inner_send.at[step - 1], self.inner_receive.at[step - 1], self.at(other),
        )

    def beside(self):
        return remote(self.mid, self.pair, self.pair_sems.at[0], self.pair_sems.at[1], (self.ctx ^ 1, self.wt))

    def lane(self, step):
        return remote(
            self.lanes_out.at[self.wt ^ step], self.lanes_in.at[self.wt],
            self.lane_send.at[step - 1], self.lane_receive.at[step - 1], (self.ctx, self.wt ^ step),
        )

    def around(self, step):
        return remote(
            self.pair, self.all.at[self.place],
            self.all_send.at[step - 1], self.all_receive.at[step - 1], self.at((self.place + step) % 4),
        )

    def begin(self):
        for step in (1, 3, 2):
            self.outward(step).start()

    def add_inner(self):
        for step in (1, 3, 2):
            self.outward(step).wait_recv()
        total = self.window[self.rows(self.place)].astype(jnp.float32)
        for step in range(3):
            total += self.came[step].astype(jnp.float32)
        self.mid[...] = total.astype(self.mid.dtype)
        self.beside().start()

    def add_beside(self):
        self.beside().wait_recv()
        total = (self.mid[...].astype(jnp.float32) + self.pair[...].astype(jnp.float32)).astype(self.mid.dtype)
        self.pair[...] = total
        if self.crosses is False:
            self.spread()
            return
        for owner in range(4):
            self.lanes_out[owner] = total[:, owner * self.share : (owner + 1) * self.share]
        for step in (2, 3, 1):
            self.lane(step).start()
        self.lanes_in[self.wt] = self.lanes_out[self.wt]

    def spread(self):
        for step in (1, 3, 2):
            self.around(step).start()
        self.all[self.place] = self.pair[...]

    def collect(self):
        if self.crosses is False:
            return
        for step in (1, 2, 3):
            self.lane(step).wait_recv()
        for sender in range(4):
            span = slice(sender * self.share, (sender + 1) * self.share)
            part = self.lanes_in[sender]
            if self.crosses is not True:
                part = jnp.where(self.crosses, part, self.pair[:, span])
            self.pair[:, span] = part
        self.spread()

    def fill(self):
        for step in (1, 2, 3):
            self.outward(step).wait_send()
            self.around(step).wait_recv()
        for place in range(4):
            start = self.stride * place
            self.window[start : start + self.inner] = self.all[place]

    def drain(self):
        self.beside().wait_send()
        for step in (1, 2, 3):
            self.around(step).wait_send()
            if self.crosses is not False:
                self.lane(step).wait_send()


def inner_scratch(inner, features):
    low = jnp.bfloat16
    share = features // 4
    return [
        pltpu.VMEM((2, 3, inner, features), low),
        pltpu.VMEM((2, inner, features), low),
        pltpu.VMEM((2, inner, features), low),
        pltpu.VMEM((2, 4, inner, share), low),
        pltpu.VMEM((2, 4, inner, share), low),
        pltpu.VMEM((2, 4, inner, features), low),
    ] + [pltpu.SemaphoreType.DMA((2, 3))] * 6 + [pltpu.SemaphoreType.DMA((2, 2))]


def inners(windows, inner, y, z, at_y, at_z, ctx, wt, crosses, scratch):
    pick = lambda half: [ref.at[half] for ref in scratch]
    return [
        Inner(windows[0], inner, z, at_z, ctx, wt, crosses[0], pick(0)[:6], pick(0)[6:]),
        Inner(windows[1], inner, y, at_y, ctx, wt, crosses[1], pick(1)[:6], pick(1)[6:]),
    ]


COLUMNS = -(-3 * SPAN // 128) * 128


def project(inputs, block_order, vectors, w_qkv, w_fc, w_out, collective):
    rows, features = inputs.shape
    share = w_qkv.shape[0]
    ff = w_fc.shape[1] // 4
    count = vectors.shape[0]
    chunks = 5
    extent = share // chunks
    low = jnp.bfloat16
    wide = COLUMNS
    extra = SPAN - share

    def kernel(token_ref, order_ref, *refs):
        (
            vectors_ref, qkv_ref, fc_ref, w_out_ref,
            received_ref, orders_ref, vec_ref, own_ref, normed_ref, fc_out, wide_ref, placed_ref,
            all_ref, small_ref, columns_ref, pieces_ref, parts_ref, sum_ref, turned_ref, blocks_ref,
            gather_send, gather_receive, cross_send, cross_receive, fc_send, fc_receive, near_send, near_receive,
            head_send, head_receive, edges_ref, edge_send, edge_receive,
        ) = refs
        ctx, wt = lax.axis_index("ctx"), lax.axis_index("wt")
        low_x = ctx % 2
        near, far, beside = (ctx, wt ^ 1), (ctx, wt ^ 2), (ctx ^ 1, wt)
        goes, comes = wt ^ (2 + low_x), wt ^ (3 - low_x)
        across = (ctx ^ 1, goes)
        small_ref[wt, :count] = vectors_ref[...]
        orders_ref[wt, :1, :32] = order_ref[...]
        all_ref[wt] = token_ref[...]

        def columns(slot, owner):
            start = 384 * owner
            queries = qkv_ref[:, pl.ds(pl.multiple_of(start, 128), SPAN)]
            keys = qkv_ref[:, pl.ds(pl.multiple_of(features - 64 + start, 128), SPAN + 64)][:, 64:]
            values = qkv_ref[:, pl.ds(pl.multiple_of(2 * features + start, 128), SPAN)]
            for part, member in enumerate((queries, keys, values)):
                columns_ref[slot, :, part * SPAN : (part + 1) * SPAN] = member
            columns_ref[slot, :, 3 * SPAN :] = jnp.zeros((share, wide - 3 * SPAN), low)

        def edge(way):
            source = (w_out_ref.at[pl.ds(share - extra, extra)], w_out_ref.at[pl.ds(0, extra)])[way]
            other = ((wt + 1) % 4, (wt + 3) % 4)[way]
            target = (edges_ref.at[pl.ds(0, extra)], edges_ref.at[pl.ds(extra + share, extra)])[way]
            return remote(source, target, edge_send.at[way], edge_receive.at[way], (ctx, other))

        def piece(target, slot, owner):
            start = pl.multiple_of(128 * ((25 * owner) // 2), 128)
            held = fc_ref[:, pl.ds(start, ff + 64)]

            @pl.when(owner % 2 == 0)
            def _():
                target[slot] = held[:, :ff]

            @pl.when(owner % 2 == 1)
            def _():
                target[slot] = held[:, 64:]

        gathered = (all_ref, small_ref, orders_ref)

        def gather(item, step, slot, peer):
            ref = gathered[item].at[slot]
            return remote(ref, ref, gather_send.at[item, step], gather_receive.at[item, step], peer)

        def cross(index):
            span = pl.ds(index * extent, extent)
            return remote(columns_ref.at[0, span], own_ref.at[wt, span], cross_send.at[0, index], cross_receive.at[0, index], across)

        def onward(index):
            part = own_ref.at[comes, pl.ds(index * extent, extent)]
            return remote(part, part, cross_send.at[1, index], cross_receive.at[1, index], beside)

        def cross_fc():
            return remote(pieces_ref.at[0], fc_out.at[wt], fc_send, fc_receive, across)

        pair = lambda: remote(columns_ref.at[1], own_ref.at[wt], near_send.at[0], near_receive.at[0], near)
        pair_fc = lambda: remote(pieces_ref.at[1], fc_out.at[wt], near_send.at[1], near_receive.at[1], near)

        columns(0, goes)
        greet_ctx(ctx, wt, (near, far, (ctx, wt ^ 3), across, (ctx ^ 1, comes)))
        for item in range(3):
            gather(item, 0, wt, far).start()
        for index in range(chunks):
            cross(index).start()
        for item in range(3):
            gather(item, 1, wt, near).start()
        for way in range(2):
            edge(way).start()
        columns(1, wt ^ 1)
        pair().start()
        columns(2, wt)
        own_ref[wt] = columns_ref[2]
        piece(pieces_ref, 0, goes)
        piece(pieces_ref, 1, wt ^ 1)
        piece(fc_out, wt, wt)
        for item in range(3):
            gather(item, 0, wt ^ 2, far).wait_recv()
            gather(item, 2, wt ^ 2, near).start()
        for item in range(3):
            gather(item, 1, wt ^ 1, near).wait_recv()
        for item in range(3):
            gather(item, 2, wt ^ 3, near).wait_recv()
        for sender in range(4):
            span = slice(sender * share, (sender + 1) * share)
            vec_ref[:, span] = small_ref[sender, :8].astype(jnp.float32)

        def norm(sequence, carry):
            normed = layer_norm(all_ref[sequence].astype(jnp.float32), vec_ref[0:1], vec_ref[1:2]).astype(low)
            normed_ref[sequence] = normed
            tokens = pl.ds(pl.multiple_of(sequence * rows, rows), rows)
            for sender in range(4):
                parts_ref[sender, tokens] = normed[:, sender * share : (sender + 1) * share]
            return carry

        lax.fori_loop(0, 4, norm, 0)
        start = pl.ds(pl.multiple_of(384 * wt, 128), SPAN)
        bias = (vec_ref[2:3, start], jnp.zeros((1, SPAN), jnp.float32), vec_ref[3:4, start])
        for part in range(3):
            sum_ref[:, part * SPAN : (part + 1) * SPAN] = jnp.broadcast_to(bias[part], (4 * rows, SPAN))
        sum_ref[:, 3 * SPAN :] = jnp.zeros((4 * rows, wide - 3 * SPAN), jnp.float32)

        def add(sender):
            sum_ref[...] += jnp.dot(parts_ref[sender], own_ref[sender], preferred_element_type=jnp.float32)

        def to_head(index):
            return remote(blocks_ref.at[index], received_ref.at[ctx], head_send.at[index], head_receive.at[ctx], (index, wt))

        def heads(sequence, carry):
            tokens = pl.ds(pl.multiple_of(sequence * rows, rows), rows)
            turned_ref[...] = sum_ref[tokens].astype(low).T
            for head in range(GROUP):
                index = sequence * GROUP + head
                for part in range(3):
                    line = part * SPAN + head * HEAD_DIM
                    blocks_ref[index, part * HEAD_DIM : (part + 1) * HEAD_DIM] = turned_ref[line : line + HEAD_DIM]

                @pl.when(index != ctx)
                def _():
                    to_head(index).start()

                @pl.when(index == ctx)
                def _():
                    received_ref[index] = blocks_ref[index]

            return carry

        add(wt)
        pair().wait_recv()
        add(wt ^ 1)
        for index in range(chunks):
            cross(index).wait_recv()
            onward(index).start()
        cross_fc().start()
        pair_fc().start()
        add(comes)
        for index in range(chunks):
            onward(index).wait_recv()
        add(goes)
        lax.fori_loop(0, 4, heads, 0)
        edges_ref[extra : extra + share] = w_out_ref[...]
        placed_ref[...] = jnp.zeros((SPAN, features), low)
        placed_ref[pl.ds(pl.multiple_of(16 * wt, 16), share)] = w_out_ref[...]
        for way in range(2):
            edge(way).wait_recv()
        wide_ref[...] = edges_ref[pl.ds(pl.multiple_of(extra - 16 * wt, 16), SPAN)]

        def head_here(step, carry):
            source = (ctx + step) % 32
            remote(
                blocks_ref.at[0], received_ref.at[source], head_send.at[0], head_receive.at[source], (source, wt)
            ).wait_recv()
            return carry

        @pl.when(ctx < 4 * GROUP)
        def _():
            lax.fori_loop(1, 32, head_here, 0)

        def sent(index, carry):
            @pl.when(index != ctx)
            def _():
                to_head(index).wait_send()

            return carry

        lax.fori_loop(0, 4 * GROUP, sent, 0)
        for item in range(3):
            gather(item, 0, wt, far).wait_send()
            gather(item, 1, wt, near).wait_send()
            gather(item, 2, wt ^ 2, near).wait_send()
        pair().wait_send()
        for way in range(2):
            edge(way).wait_send()
        for index in range(chunks):
            cross(index).wait_send()
            onward(index).wait_send()
        cross_fc().wait()
        pair_fc().wait()

    vmem = pl.BlockSpec(memory_space=pltpu.VMEM)
    hbm = pl.BlockSpec(memory_space=pl.ANY)
    return pl.pallas_call(
        kernel,
        out_shape=(
            jax.ShapeDtypeStruct((32, 3 * HEAD_DIM, rows), low),
            jax.ShapeDtypeStruct((4, 8, 128), jnp.int32),
            jax.ShapeDtypeStruct((8, features), jnp.float32),
            jax.ShapeDtypeStruct((4, share, wide), low),
            jax.ShapeDtypeStruct((4, rows, features), low),
            jax.ShapeDtypeStruct((4, share, ff), low),
            jax.ShapeDtypeStruct((SPAN, features), low),
            jax.ShapeDtypeStruct((SPAN, features), low),
        ),
        in_specs=[vmem] * 6,
        out_specs=(vmem,) * 8,
        scratch_shapes=[
            pltpu.VMEM((4, rows, features), low),
            pltpu.VMEM((4, 16, share), low),
            pltpu.VMEM((3, share, wide), low),
            pltpu.VMEM((2, share, ff), low),
            pltpu.VMEM((4, 4 * rows, share), low),
            pltpu.VMEM((4 * rows, wide), jnp.float32),
            pltpu.VMEM((wide, rows), low),
            pltpu.VMEM((4 * GROUP, 3 * HEAD_DIM, rows), low),
            pltpu.SemaphoreType.DMA((3, 3)),
            pltpu.SemaphoreType.DMA((3, 3)),
            pltpu.SemaphoreType.DMA((2, chunks)),
            pltpu.SemaphoreType.DMA((2, chunks)),
            pltpu.SemaphoreType.DMA,
            pltpu.SemaphoreType.DMA,
            pltpu.SemaphoreType.DMA((2,)),
            pltpu.SemaphoreType.DMA((2,)),
            pltpu.SemaphoreType.DMA((4 * GROUP,)),
            pltpu.SemaphoreType.DMA((32,)),
            pltpu.VMEM((share + 2 * extra, features), low),
            pltpu.SemaphoreType.DMA((2,)),
            pltpu.SemaphoreType.DMA((2,)),
        ],
        compiler_params=pltpu.CompilerParams(
            collective_id=collective, has_side_effects=True, vmem_limit_bytes=56 * 2**20
        ),
        name="project",
    )(inputs, block_order, vectors, w_qkv, w_fc, w_out)


def attend(received, inverse, place, placed_out, tokens, small, pieces, cotangent, collective):
    parts, wide, rows = received.shape
    dim = wide // 3
    features = tokens.shape[1]
    block = math.gcd(1024, parts * rows)
    per = block // rows
    count = parts // per
    chunks = 5
    extent = pieces.shape[1] // chunks
    low = jnp.bfloat16
    hold, off = place // per, place % per

    def kernel(
        inverse_ref, hold_ref, off_ref, in_ref, weight_ref, token_ref, small_ref, pieces_ref, cot_ref,
        q_ref, kt_ref, k_ref, v_ref, att_ref, lse_ref, stacked_ref, middle_ref, all_ref, fc_ref, all_cot_ref,
        vt_ref, blocks_ref, came_ref, turned_ref, terms_ref, bufs,
        head_send, head_receive, term_send, term_receive, all_send, all_receive,
        cross_send, cross_receive, cot_send, cot_receive,
    ):
        ctx, wt = lax.axis_index("ctx"), lax.axis_index("wt")
        low_x = ctx % 2
        near, far, beside = (ctx, wt ^ 1), (ctx, wt ^ 2), (ctx ^ 1, wt)
        comes = wt ^ (3 - low_x)
        greet_ctx(ctx, wt, (near, far))

        def onward(index):
            span = pl.ds(index * extent, extent)
            return remote(
                pieces_ref.at[comes, span], fc_ref.at[comes, span], cross_send.at[index], cross_receive.at[index], beside
            )

        def upstream(step, source, slot, peer):
            return remote(source, all_cot_ref.at[slot], cot_send.at[step], cot_receive.at[step], peer)

        for index in range(chunks):
            onward(index).start()
        upstream(0, cot_ref, wt, far).start()
        upstream(1, cot_ref, wt, near).start()
        def arrange(index, carry):
            for sub in range(per):
                piece = in_ref[inverse_ref[index * per + sub]]
                lanes = pl.ds(sub * rows, rows)
                q_ref[index, :, lanes] = piece[:dim]
                kt_ref[index, :, lanes] = piece[dim : 2 * dim]
                vt_ref[index, :, lanes] = piece[2 * dim :]
                k_ref[index, lanes, :] = piece[dim : 2 * dim].T
                v_ref[index, lanes, :] = piece[2 * dim :].T
            return carry

        lax.fori_loop(0, count, arrange, 0)
        row = lax.broadcasted_iota(jnp.int32, (block, block), 0)
        col = lax.broadcasted_iota(jnp.int32, (block, block), 1)
        factor = LOG2E * dim**-0.5

        def step(qi, kj, carry, diagonal):
            peak, mass, total = carry
            scores = jnp.dot(k_ref[kj], q_ref[qi], preferred_element_type=jnp.float32) * factor
            if diagonal:
                scores = jnp.where(row <= col, scores, NEG)
            new_peak = jnp.maximum(peak, jnp.max(scores, axis=0, keepdims=True))
            weights = jnp.exp2(scores - new_peak)
            shrink = jnp.exp2(peak - new_peak)
            mass = mass * shrink + jnp.sum(weights, axis=0, keepdims=True)
            total = total * shrink + jnp.dot(vt_ref[kj], weights.astype(low), preferred_element_type=jnp.float32)
            return (new_peak, mass, total)

        def query_block(qi, carry):
            start = (
                jnp.full((1, block), NEG, jnp.float32),
                jnp.zeros((1, block), jnp.float32),
                jnp.zeros((dim, block), jnp.float32),
            )
            state = lax.fori_loop(0, qi, lambda kj, cur: step(qi, kj, cur, False), start)
            peak, mass, total = step(qi, qi, state, True)
            att_ref[qi] = total / mass
            lse_ref[qi] = peak + jnp.log2(mass)
            return carry

        lax.fori_loop(0, count, query_block, 0)

        def to_owner(index):
            return remote(blocks_ref.at[index], came_ref.at[ctx], head_send.at[index], head_receive.at[ctx], (index, wt))

        def give_back(index, carry):
            whole = att_ref[hold_ref[index]]
            picked = whole[:, :rows]
            for sub in range(1, per):
                picked = jnp.where(off_ref[index] == sub, whole[:, sub * rows : (sub + 1) * rows], picked)
            blocks_ref[index] = picked.astype(low)

            @pl.when(index != ctx)
            def _():
                to_owner(index).start()

            @pl.when(index == ctx)
            def _():
                came_ref[index] = blocks_ref[index]

            return carry

        @pl.when(ctx < 4 * GROUP)
        def _():
            lax.fori_loop(0, parts, give_back, 0)

        upstream(0, cot_ref, wt ^ 2, far).wait_recv()
        upstream(2, all_cot_ref.at[wt ^ 2], wt ^ 2, near).start()
        all_cot_ref[wt] = cot_ref[...]
        for slot in (wt, wt ^ 1, comes):
            fc_ref[slot] = pieces_ref[slot]

        def owner_here(source, carry):
            @pl.when(source != ctx)
            def _():
                remote(
                    blocks_ref.at[0], came_ref.at[source], head_send.at[0], head_receive.at[source], (source, wt)
                ).wait_recv()

            return carry

        lax.fori_loop(0, 4 * GROUP, owner_here, 0)

        def make_terms(sequence):
            for head in range(GROUP):
                turned_ref[head * dim : (head + 1) * dim] = came_ref[sequence * GROUP + head]
            stacked_ref[sequence] = turned_ref[...].T
            terms_ref[...] = jnp.dot(stacked_ref[sequence], weight_ref[...], preferred_element_type=jnp.float32)

        def term(index, source, target, peer):
            return remote(bufs.at[source], bufs.at[target], term_send.at[index], term_receive.at[index], peer)

        make_terms(wt ^ 3)
        bufs[0] = terms_ref[...].astype(low)
        term(0, 0, 3, near).start()
        make_terms(wt ^ 1)
        bufs[1] = terms_ref[...].astype(low)
        term(1, 1, 4, near).start()
        make_terms(wt ^ 2)
        term(0, 0, 3, near).wait_recv()
        bufs[2] = (terms_ref[...] + bufs[3].astype(jnp.float32)).astype(low)
        term(2, 2, 5, far).start()
        make_terms(wt)
        middle_ref[...] = token_ref[...].astype(jnp.float32) + terms_ref[...] + small_ref[0:1]
        term(1, 1, 4, near).wait_recv()
        middle_ref[...] += bufs[4].astype(jnp.float32)
        term(2, 2, 5, far).wait_recv()
        middle_ref[...] += bufs[5].astype(jnp.float32)
        all_ref[wt] = layer_norm(middle_ref[...], small_ref[1:2], small_ref[2:3]).astype(low)

        def normed(step, slot, peer):
            return remote(all_ref.at[slot], all_ref.at[slot], all_send.at[step], all_receive.at[step], peer)

        normed(0, wt, far).start()
        normed(1, wt, near).start()
        normed(0, wt ^ 2, far).wait_recv()
        normed(2, wt ^ 2, near).start()
        normed(1, wt ^ 1, near).wait_recv()
        normed(2, wt ^ 3, near).wait_recv()
        normed(0, wt, far).wait_send()
        normed(1, wt, near).wait_send()
        normed(2, wt ^ 2, near).wait_send()
        term(0, 0, 3, near).wait_send()
        term(1, 1, 4, near).wait_send()
        term(2, 2, 5, far).wait_send()
        upstream(1, cot_ref, wt ^ 1, near).wait_recv()
        upstream(2, all_cot_ref.at[wt ^ 2], wt ^ 3, near).wait_recv()
        upstream(0, cot_ref, wt, far).wait_send()
        upstream(1, cot_ref, wt, near).wait_send()
        upstream(2, all_cot_ref.at[wt ^ 2], wt ^ 2, near).wait_send()
        for index in range(chunks):
            onward(index).wait()

        def sent(index, carry):
            @pl.when(index != ctx)
            def _():
                to_owner(index).wait_send()

            return carry

        @pl.when(ctx < 4 * GROUP)
        def _():
            lax.fori_loop(0, parts, sent, 0)

    smem = pl.BlockSpec(memory_space=pltpu.SMEM)
    vmem = pl.BlockSpec(memory_space=pltpu.VMEM)
    hbm = pl.BlockSpec(memory_space=pl.ANY)
    lane_first = jax.ShapeDtypeStruct((count, dim, block), low)
    row_first = jax.ShapeDtypeStruct((count, block, dim), low)
    return pl.pallas_call(
        kernel,
        out_shape=(
            lane_first,
            lane_first,
            row_first,
            row_first,
            jax.ShapeDtypeStruct((count, dim, block), jnp.float32),
            jax.ShapeDtypeStruct((count, 1, block), jnp.float32),
            jax.ShapeDtypeStruct((4, rows, SPAN), low),
            jax.ShapeDtypeStruct((rows, features), jnp.float32),
            jax.ShapeDtypeStruct((4, rows, features), low),
            jax.ShapeDtypeStruct(pieces.shape, low),
            jax.ShapeDtypeStruct((4, rows, features), low),
        ),
        in_specs=[smem] * 3 + [vmem] * 6,
        out_specs=(vmem,) * 11,
        scratch_shapes=[
            pltpu.VMEM((count, dim, block), low),
            pltpu.VMEM((parts, dim, rows), low),
            pltpu.VMEM((parts, dim, rows), low),
            pltpu.VMEM((SPAN, rows), low),
            pltpu.VMEM((rows, features), jnp.float32),
            pltpu.VMEM((6, rows, features), low),
            pltpu.SemaphoreType.DMA((parts,)),
            pltpu.SemaphoreType.DMA((parts,)),
            pltpu.SemaphoreType.DMA((3,)),
            pltpu.SemaphoreType.DMA((3,)),
            pltpu.SemaphoreType.DMA((3,)),
            pltpu.SemaphoreType.DMA((3,)),
            pltpu.SemaphoreType.DMA((chunks,)),
            pltpu.SemaphoreType.DMA((chunks,)),
            pltpu.SemaphoreType.DMA((3,)),
            pltpu.SemaphoreType.DMA((3,)),
        ],
        compiler_params=pltpu.CompilerParams(
            collective_id=collective, has_side_effects=True, vmem_limit_bytes=56 * 2**20
        ),
        name="attend",
    )(inverse, hold, off, received, placed_out, tokens, small, pieces, cotangent)


def feed_back(hidden, pre_grad, w_proj, own_fc, grad_fc, grad_proj, middle, gain, cotangent, wide_out, collective):
    rows, features = middle.shape
    block = grad_fc.shape[0] // 4
    low = jnp.bfloat16

    def kernel(
        hidden_ref, pre_ref, w_proj_ref, w_fc_ref, fc_ref, proj_ref, middle_ref, gain_ref, cot_ref, wide_ref,
        out_ref, middle_grad_ref, vectors_ref, all_ref, up_ref, fc_out, proj_out,
        fc_work, proj_work, terms_ref, bufs, relay, arrive, blocks_ref,
        ring_send, ring_receive, term_send, term_receive, all_send, all_receive, head_send, head_receive, fetch,
    ):
        ctx, wt = lax.axis_index("ctx"), lax.axis_index("wt")
        y, z, low_x = ctx // 8, ctx // 2 % 4, ctx % 2
        at_y = lambda place: (place * 8 + z * 2 + low_x, wt)
        at_z = lambda place: (y * 8 + place * 2 + low_x, wt)
        near, far = (ctx, wt ^ 1), (ctx, wt ^ 2)
        loads = [
            pltpu.make_async_copy(source, target, fetch.at[index])
            for index, (source, target) in enumerate(((fc_ref, fc_work), (proj_ref, proj_work)))
        ]
        for load in loads:
            load.start()
        greet_ctx(ctx, wt, (near, far))

        def term(item, step, source, target, peer):
            return remote(
                bufs.at[item, source], bufs.at[item, target], term_send.at[item, step], term_receive.at[item, step], peer
            )

        def tokens(sequence):
            return terms_ref[pl.ds(pl.multiple_of(sequence * rows, rows), rows)]

        def begin_terms(item):
            bufs[item, 0] = tokens(wt ^ 3).astype(low)
            term(item, 0, 0, 3, near).start()
            bufs[item, 1] = tokens(wt ^ 1).astype(low)
            term(item, 1, 1, 4, near).start()

        def pass_terms(item):
            term(item, 0, 0, 3, near).wait_recv()
            bufs[item, 2] = (tokens(wt ^ 2) + bufs[item, 3].astype(jnp.float32)).astype(low)
            term(item, 2, 2, 5, far).start()

        def end_terms(item):
            term(item, 1, 1, 4, near).wait_recv()
            total = tokens(wt) + bufs[item, 4].astype(jnp.float32)
            term(item, 2, 2, 5, far).wait_recv()
            return total + bufs[item, 5].astype(jnp.float32)

        rings = [
            RingSum(fc_work, block, y, at_y, relay.at[0], arrive.at[0], ring_send.at[0], ring_receive.at[0]),
            RingSum(proj_work, block, z, at_z, relay.at[1], arrive.at[1], ring_send.at[1], ring_receive.at[1]),
        ]
        for load, ring in zip(loads, rings):
            load.wait()
            ring.begin()
        terms_ref[...] = lax.dot_general(
            pre_ref[...], w_fc_ref[...], (((1,), (1,)), ((), ())), preferred_element_type=jnp.float32
        )
        begin_terms(0)
        pass_terms(0)
        grad = end_terms(0)
        values = middle_ref[...]
        centered = values - jnp.mean(values, axis=-1, keepdims=True)
        scale = lax.rsqrt(jnp.mean(centered * centered, axis=-1, keepdims=True) + EPS)
        normed = centered * scale
        vectors_ref[0:1] = jnp.sum(grad * normed, axis=0, keepdims=True)
        vectors_ref[1:2] = jnp.sum(grad, axis=0, keepdims=True)
        weighted = grad * gain_ref[...]
        part = weighted - jnp.mean(weighted, axis=-1, keepdims=True)
        part = part - normed * jnp.mean(weighted * normed, axis=-1, keepdims=True)
        middle_grad = cot_ref[...].astype(jnp.float32) + scale * part
        middle_grad_ref[...] = middle_grad
        all_ref[wt] = middle_grad.astype(low)

        def branch(step, slot, peer):
            return remote(all_ref.at[slot], all_ref.at[slot], all_send.at[step], all_receive.at[step], peer)

        branch(0, wt, far).start()
        branch(1, wt, near).start()

        def to_head(index, other):
            return remote(
                blocks_ref.at[index], up_ref.at[ctx], head_send.at[index], head_receive.at[ctx], (other, wt)
            )

        def heads(turn, sequence):
            grads = lax.dot_general(
                wide_ref[...], all_ref[sequence], (((1,), (1,)), ((), ())), preferred_element_type=jnp.float32
            ).astype(low)
            for head in range(GROUP):
                index, other = turn * GROUP + head, sequence * GROUP + head
                blocks_ref[index] = grads[head * HEAD_DIM : (head + 1) * HEAD_DIM]

                @pl.when(other != ctx)
                def _():
                    to_head(index, other).start()

                @pl.when(other == ctx)
                def _():
                    up_ref[other] = blocks_ref[index]

        heads(0, wt)
        terms_ref[...] = jnp.dot(hidden_ref[...], w_proj_ref[...], preferred_element_type=jnp.float32)
        begin_terms(1)
        branch(0, wt ^ 2, far).wait_recv()
        branch(2, wt ^ 2, near).start()
        branch(1, wt ^ 1, near).wait_recv()
        heads(1, wt ^ 1)
        heads(2, wt ^ 2)
        pass_terms(1)
        branch(2, wt ^ 3, near).wait_recv()
        heads(3, wt ^ 3)
        for ring in rings:
            ring.pass_on()
        out_ref[...] = end_terms(1)
        fc_out[...] = rings[0].finish().astype(low)
        proj_out[...] = rings[1].finish().astype(low)

        def head_here(step, carry):
            source = (ctx + step) % 32
            remote(blocks_ref.at[0], up_ref.at[source], head_send.at[0], head_receive.at[source], (source, wt)).wait_recv()
            return carry

        @pl.when(ctx < 4 * GROUP)
        def _():
            lax.fori_loop(1, 32, head_here, 0)

        for turn, sequence in enumerate((wt, wt ^ 1, wt ^ 2, wt ^ 3)):
            for head in range(GROUP):
                index, other = turn * GROUP + head, sequence * GROUP + head

                @pl.when(other != ctx)
                def _():
                    to_head(index, other).wait_send()

        for item in range(2):
            term(item, 0, 0, 3, near).wait_send()
            term(item, 1, 1, 4, near).wait_send()
            term(item, 2, 2, 5, far).wait_send()
        branch(0, wt, far).wait_send()
        branch(1, wt, near).wait_send()
        branch(2, wt ^ 2, near).wait_send()
        for ring in rings:
            ring.drain()

    vmem = pl.BlockSpec(memory_space=pltpu.VMEM)
    hbm = pl.BlockSpec(memory_space=pl.ANY)
    cut = (block // 32) * 16 + 16
    return pl.pallas_call(
        kernel,
        out_shape=(
            jax.ShapeDtypeStruct((rows, features), jnp.float32),
            jax.ShapeDtypeStruct((rows, features), jnp.float32),
            jax.ShapeDtypeStruct((8, features), jnp.float32),
            jax.ShapeDtypeStruct((4, rows, features), low),
            jax.ShapeDtypeStruct((32, HEAD_DIM, rows), low),
            jax.ShapeDtypeStruct((block, features), low),
            jax.ShapeDtypeStruct((block, features), low),
        ),
        in_specs=[vmem] * 4 + [hbm] * 2 + [vmem] * 4,
        out_specs=(vmem,) * 7,
        scratch_shapes=[
            pltpu.VMEM(grad_fc.shape, low),
            pltpu.VMEM(grad_proj.shape, low),
            pltpu.VMEM((4 * rows, features), jnp.float32),
            pltpu.VMEM((2, 6, rows, features), low),
            pltpu.VMEM((2, 2, cut, features), low),
            pltpu.VMEM((2, 2, block, features), low),
            pltpu.VMEM((4 * GROUP, HEAD_DIM, rows), low),
            pltpu.SemaphoreType.DMA((2, 6)),
            pltpu.SemaphoreType.DMA((2, 6)),
            pltpu.SemaphoreType.DMA((2, 3)),
            pltpu.SemaphoreType.DMA((2, 3)),
            pltpu.SemaphoreType.DMA((3,)),
            pltpu.SemaphoreType.DMA((3,)),
            pltpu.SemaphoreType.DMA((4 * GROUP,)),
            pltpu.SemaphoreType.DMA((32,)),
            pltpu.SemaphoreType.DMA((2,)),
        ],
        compiler_params=pltpu.CompilerParams(
            collective_id=collective, has_side_effects=True, vmem_limit_bytes=56 * 2**20
        ),
        name="feed_back",
    )(hidden, pre_grad, w_proj, own_fc, grad_fc, grad_proj, middle, gain, cotangent, wide_out)


def attend_back(upstream, inverse, place, saved, window_fc, window_proj, own_qkv, collective):
    parts, dim, rows = upstream.shape
    q, kt, k, v, attended, lse = saved
    count, block = k.shape[:2]
    per = block // rows
    features = window_fc.shape[1]
    inner = 112
    low = jnp.bfloat16
    hold, off = place // per, place % per

    def kernel(
        inverse_ref, hold_ref, off_ref, up_ref, q_ref, kt_ref, k_ref, v_ref, att_ref, lse_ref, fc_ref, proj_ref, qkv_ref,
        own_ref, grad_ref, fc_out, proj_out,
        up_sorted, up_rows, q_rows, delta_ref, gq_ref, gk_ref, gv_ref, blocks_ref, came_ref, turned_ref, plain_ref, terms_ref, bufs,
        head_send, head_receive, term_send, term_receive, *scratch,
    ):
        ctx, wt = lax.axis_index("ctx"), lax.axis_index("wt")
        y, z, low_x = ctx // 8, ctx // 2 % 4, ctx % 2
        at_y = lambda where: (where * 8 + z * 2 + low_x, wt)
        at_z = lambda where: (y * 8 + where * 2 + low_x, wt)
        near, far = (ctx, wt ^ 1), (ctx, wt ^ 2)
        fc_out[...] = fc_ref[...]
        proj_out[...] = proj_ref[...]
        greet_ctx(ctx, wt, (near, far, (ctx, wt ^ 3)))
        steps = inners((fc_out, proj_out), inner, y, z, at_y, at_z, ctx, wt, (True, False), scratch)
        for one in steps:
            one.begin()

        def arrange(index, carry):
            for sub in range(per):
                piece = up_ref[inverse_ref[index * per + sub]]
                lanes = pl.ds(sub * rows, rows)
                up_sorted[index, :, lanes] = piece
                up_rows[index, lanes, :] = piece.T
            q_rows[index] = q_ref[index].T
            delta_ref[index] = jnp.sum(up_sorted[index].astype(jnp.float32) * att_ref[index], axis=0, keepdims=True)
            gk_ref[index] = jnp.zeros((block, dim), jnp.float32)
            gv_ref[index] = jnp.zeros((block, dim), jnp.float32)
            return carry

        lax.fori_loop(0, count, arrange, 0)
        row = lax.broadcasted_iota(jnp.int32, (block, block), 0)
        col = lax.broadcasted_iota(jnp.int32, (block, block), 1)
        factor = LOG2E * dim**-0.5

        def step(qi, kj, total, diagonal):
            scores = jnp.dot(k_ref[kj], q_ref[qi], preferred_element_type=jnp.float32) * factor
            weights = jnp.exp2(scores - lse_ref[qi])
            if diagonal:
                weights = jnp.where(row <= col, weights, 0.0)
            prob_grad = jnp.dot(v_ref[kj], up_sorted[qi], preferred_element_type=jnp.float32)
            score_grad = (weights * (prob_grad - delta_ref[qi])).astype(low)
            gv_ref[kj] += jnp.dot(weights.astype(low), up_rows[qi], preferred_element_type=jnp.float32)
            gk_ref[kj] += jnp.dot(score_grad, q_rows[qi], preferred_element_type=jnp.float32)
            return total + jnp.dot(kt_ref[kj], score_grad, preferred_element_type=jnp.float32)

        def query_block(qi, carry):
            total = lax.fori_loop(
                0, qi, lambda kj, cur: step(qi, kj, cur, False), jnp.zeros((dim, block), jnp.float32)
            )
            gq_ref[qi] = step(qi, qi, total, True) * dim**-0.5
            return carry

        lax.fori_loop(0, count - 1, query_block, 0)
        for one in steps:
            one.add_inner()
        lax.fori_loop(count - 1, count, query_block, 0)

        def to_owner(index):
            return remote(blocks_ref.at[index], came_ref.at[ctx], head_send.at[index], head_receive.at[ctx], (index, wt))

        def give_back(index, carry):
            def pick(whole, axis):
                cuts = [lax.slice_in_dim(whole, sub * rows, (sub + 1) * rows, axis=axis) for sub in range(per)]
                picked = cuts[0]
                for sub in range(1, per):
                    picked = jnp.where(off_ref[index] == sub, cuts[sub], picked)
                return picked

            blocks_ref[index, :dim] = pick(gq_ref[hold_ref[index]], 1).astype(low)
            blocks_ref[index, dim : 2 * dim] = (pick(gk_ref[hold_ref[index]], 0) * dim**-0.5).T.astype(low)
            blocks_ref[index, 2 * dim :] = pick(gv_ref[hold_ref[index]], 0).T.astype(low)

            @pl.when(index != ctx)
            def _():
                to_owner(index).start()

            @pl.when(index == ctx)
            def _():
                came_ref[index] = blocks_ref[index]

            return carry

        @pl.when(ctx < 4 * GROUP)
        def _():
            lax.fori_loop(0, parts, give_back, 0)

        for one in steps:
            one.add_beside()

        def owner_here(source, carry):
            @pl.when(source != ctx)
            def _():
                remote(
                    blocks_ref.at[0], came_ref.at[source], head_send.at[0], head_receive.at[source], (source, wt)
                ).wait_recv()

            return carry

        lax.fori_loop(0, 4 * GROUP, owner_here, 0)
        for one in steps:
            one.collect()
        feature = lax.broadcasted_iota(jnp.int32, (dim, rows), 0)
        turned_ref[3 * SPAN :] = jnp.zeros((COLUMNS - 3 * SPAN, rows), low)

        def make_terms(sequence):
            for head in range(GROUP):
                piece = came_ref[sequence * GROUP + head]
                place_in = feature + head * dim
                mine = (place_in >= 16 * wt) & (place_in < 16 * wt + features // 4)
                for part in range(3):
                    line = piece[part * dim : (part + 1) * dim]
                    start = part * SPAN + head * dim
                    plain_ref[part, head * dim : (head + 1) * dim] = line
                    turned_ref[start : start + dim] = jnp.where(mine, line.astype(jnp.float32), 0.0).astype(low)
            tokens = pl.ds(pl.multiple_of(sequence * rows, rows), rows)
            for part in range(3):
                lines = plain_ref[part, pl.ds(pl.multiple_of(16 * wt, 16), features // 4)]
                own_ref[part * (features // 4) : (part + 1) * (features // 4), tokens] = lines
            terms_ref[...] = lax.dot_general(
                turned_ref[...].T, qkv_ref[...], (((1,), (1,)), ((), ())), preferred_element_type=jnp.float32
            )

        def term(index, source, target, peer):
            return remote(bufs.at[source], bufs.at[target], term_send.at[index], term_receive.at[index], peer)

        make_terms(wt ^ 3)
        bufs[0] = terms_ref[...].astype(low)
        term(0, 0, 3, near).start()
        make_terms(wt ^ 1)
        bufs[1] = terms_ref[...].astype(low)
        term(1, 1, 4, near).start()
        make_terms(wt ^ 2)
        term(0, 0, 3, near).wait_recv()
        bufs[2] = (terms_ref[...] + bufs[3].astype(jnp.float32)).astype(low)
        term(2, 2, 5, far).start()
        make_terms(wt)
        term(1, 1, 4, near).wait_recv()
        grad_ref[...] = terms_ref[...] + bufs[4].astype(jnp.float32)
        term(2, 2, 5, far).wait_recv()
        grad_ref[...] += bufs[5].astype(jnp.float32)
        term(0, 0, 3, near).wait_send()
        term(1, 1, 4, near).wait_send()
        term(2, 2, 5, far).wait_send()

        def sent(index, carry):
            @pl.when(index != ctx)
            def _():
                to_owner(index).wait_send()

            return carry

        @pl.when(ctx < 4 * GROUP)
        def _():
            lax.fori_loop(0, parts, sent, 0)

        for one in steps:
            one.fill()
        for one in steps:
            one.drain()

    smem = pl.BlockSpec(memory_space=pltpu.SMEM)
    vmem = pl.BlockSpec(memory_space=pltpu.VMEM)
    return pl.pallas_call(
        kernel,
        out_shape=(
            jax.ShapeDtypeStruct((3 * features // 4, 4 * rows), low),
            jax.ShapeDtypeStruct((rows, features), jnp.float32),
            jax.ShapeDtypeStruct(window_fc.shape, low),
            jax.ShapeDtypeStruct(window_proj.shape, low),
        ),
        in_specs=[smem] * 3 + [vmem] * 10,
        out_specs=(vmem,) * 4,
        scratch_shapes=[
            pltpu.VMEM((count, dim, block), low),
            pltpu.VMEM((count, block, dim), low),
            pltpu.VMEM((count, block, dim), low),
            pltpu.VMEM((count, 1, block), jnp.float32),
            pltpu.VMEM((count, dim, block), jnp.float32),
            pltpu.VMEM((count, block, dim), jnp.float32),
            pltpu.VMEM((count, block, dim), jnp.float32),
            pltpu.VMEM((parts, 3 * dim, rows), low),
            pltpu.VMEM((parts, 3 * dim, rows), low),
            pltpu.VMEM((COLUMNS, rows), low),
            pltpu.VMEM((3, SPAN, rows), low),
            pltpu.VMEM((rows, features), jnp.float32),
            pltpu.VMEM((6, rows, features), low),
            pltpu.SemaphoreType.DMA((parts,)),
            pltpu.SemaphoreType.DMA((parts,)),
            pltpu.SemaphoreType.DMA((3,)),
            pltpu.SemaphoreType.DMA((3,)),
        ]
        + inner_scratch(inner, features),
        compiler_params=pltpu.CompilerParams(
            collective_id=collective, has_side_effects=True, vmem_limit_bytes=56 * 2**20
        ),
        name="attend_back",
    )(inverse, hold, off, upstream, q, kt, k, v, attended, lse, window_fc, window_proj, own_qkv)


def finish_gradients(grad_qkv, grad_out, crossed, kept, window_fc, window_proj, collective):
    share, features = grad_out.shape
    extra = crossed.shape[0]
    size = (share + extra) // 2
    block = window_fc.shape[0]
    inner = 64
    low = jnp.bfloat16

    def kernel(
        qkv_ref, out_ref, crossed_ref, kept_ref, fc_ref, proj_ref,
        qkv_turned, out_rows, crossed_rows, kept_rows, fc_turned, proj_out,
        first_out, second_out, fc_out, work, relay, arrive, ring_send, ring_receive, mlp_send, mlp_receive, out_send, out_receive, fetch, *scratch,
    ):
        ctx, wt = lax.axis_index("ctx"), lax.axis_index("wt")
        y, z, low_x = ctx // 8, ctx // 2 % 4, ctx % 2
        at_y = lambda place: (place * 8 + z * 2 + low_x, wt)
        at_z = lambda place: (y * 8 + place * 2 + low_x, wt)
        moves = [
            (qkv_ref.at[pl.ds(0, share)], work.at[0, pl.ds(0, share)]),
            (crossed_ref, work.at[0, pl.ds(share, extra)]),
            (qkv_ref.at[pl.ds(share, share)], work.at[0, pl.ds(share + extra, share)]),
            (qkv_ref.at[pl.ds(2 * share, share)], work.at[1, pl.ds(0, share)]),
            (out_ref, work.at[1, pl.ds(share + extra, share)]),
            (kept_ref, work.at[1, pl.ds(2 * share + extra, extra)]),
        ]
        moves += [(fc_ref, fc_out.at[y]), (proj_ref, proj_out.at[z])]
        loads = [pltpu.make_async_copy(source, target, fetch.at[index]) for index, (source, target) in enumerate(moves)]
        work[0, 2 * share + extra :] = jnp.zeros((extra, features), low)
        work[1, share : share + extra] = jnp.zeros((extra, features), low)
        for load in loads:
            load.start()
        peers = [at_y((y + step) % 4) for step in (1, 2, 3)] + [at_z((z + step) % 4) for step in (1, 2, 3)]
        greet(peers + [(ctx ^ 1, wt)] + [(ctx, wt ^ step) for step in (1, 2, 3)])
        for load in loads[:6]:
            load.wait()
        rings = [
            RingSum(work.at[0], size, y, at_y, relay.at[0], arrive.at[0], ring_send.at[0], ring_receive.at[0]),
            RingSum(work.at[1], size, z, at_z, relay.at[1], arrive.at[1], ring_send.at[1], ring_receive.at[1]),
        ]
        beside = (ctx ^ 1, wt)
        mlp = [
            RingSpread(fc_out, y, at_y, beside, low_x, 144, mlp_send.at[0], mlp_receive.at[0]),
            RingSpread(proj_out, z, at_z, beside, low_x, 144, mlp_send.at[1], mlp_receive.at[1]),
        ]
        for load in loads[6:]:
            load.wait()
        for one in mlp:
            one.begin()
        for ring in rings:
            ring.begin()
        for one in mlp:
            one.share()
        for ring in rings:
            ring.pass_on()
        for one in mlp:
            one.go_on()
        first_out[y] = rings[0].finish().astype(low)
        second_out[z] = rings[1].finish().astype(low)
        steps = inners(
            (first_out.at[y], second_out.at[z]), inner, y, z, at_y, at_z, ctx, wt, (True, z < 2), scratch
        )
        for one in steps:
            one.begin()
        for one in steps:
            one.add_inner()
        for one in steps:
            one.add_beside()
        for one in steps:
            one.collect()
        for one in mlp:
            one.pass_on()
        for one in steps:
            one.fill()
        spreads = [
            RingSpread(first_out, y, at_y, beside, low_x, 32, out_send.at[0], out_receive.at[0]),
            RingSpread(second_out, z, at_z, beside, low_x, 32, out_send.at[1], out_receive.at[1]),
        ]
        for one in spreads:
            one.begin()
            one.go_on()
        for one in mlp:
            one.finish()
        for one in spreads:
            one.share()

        def turn(source, place, extent, target, start, width):
            for sender in range(4):
                part = source[place, :extent, sender * share : (sender + 1) * share].astype(jnp.float32).T.astype(low)
                at = start + sender * width
                target[:, at : at + extent] = part

        turn(fc_out, 0, block, fc_turned, 0, 4 * block)
        for one in spreads:
            one.pass_on()
        for place in range(1, 4):
            turn(fc_out, place, block, fc_turned, place * block, 4 * block)
        for one in spreads:
            one.finish()
        left = share - size
        for part, (source, place) in enumerate(((first_out, 0), (first_out, 2), (second_out, 0))):
            turn(source, place, size, qkv_turned, part * features, share)
            turn(source, place + 1, left, qkv_turned, part * features + size, share)
        out_rows[:size] = second_out[2]
        out_rows[size:] = second_out[3, :left]
        crossed_rows[...] = first_out[1, left:]
        kept_rows[...] = second_out[3, left:]
        for one in rings + steps + mlp + spreads:
            one.drain()

    vmem = pl.BlockSpec(memory_space=pltpu.VMEM)
    hbm = pl.BlockSpec(memory_space=pl.ANY)
    cut = (size // 32) * 16 + 16
    return pl.pallas_call(
        kernel,
        out_shape=(
            jax.ShapeDtypeStruct((share, 3 * features), low),
            jax.ShapeDtypeStruct((share, features), low),
            jax.ShapeDtypeStruct((extra, features), low),
            jax.ShapeDtypeStruct((extra, features), low),
            jax.ShapeDtypeStruct((share, 16 * block), low),
            jax.ShapeDtypeStruct((4, block, features), low),
        ),
        in_specs=[hbm] * 6,
        out_specs=(vmem,) * 6,
        scratch_shapes=[
            pltpu.VMEM((4, size, features), low),
            pltpu.VMEM((4, size, features), low),
            pltpu.VMEM((4, block, features), low),
            pltpu.VMEM((2, 4 * size, features), low),
            pltpu.VMEM((2, 2, cut, features), low),
            pltpu.VMEM((2, 2, size, features), low),
            pltpu.SemaphoreType.DMA((2, 6)),
            pltpu.SemaphoreType.DMA((2, 6)),
            pltpu.SemaphoreType.DMA((2, 8)),
            pltpu.SemaphoreType.DMA((2, 8)),
            pltpu.SemaphoreType.DMA((2, 8)),
            pltpu.SemaphoreType.DMA((2, 8)),
            pltpu.SemaphoreType.DMA((8,)),
        ]
        + inner_scratch(inner, features),
        compiler_params=pltpu.CompilerParams(
            collective_id=collective, has_side_effects=True, vmem_limit_bytes=56 * 2**20
        ),
        name="finish_gradients",
    )(grad_qkv, grad_out, crossed, kept, window_fc, window_proj)


def local(
    inputs,
    block_order,
    cotangent,
    ln1_gain,
    ln1_bias,
    w_qkv,
    bias_q,
    bias_v,
    w_out,
    bias_out,
    ln2_gain,
    ln2_bias,
    w_fc,
    bias_fc,
    w_proj,
    bias_proj,
):
    ctx, wt = lax.axis_index("ctx"), lax.axis_index("wt")
    ctx_count = lax.axis_size("ctx")
    rows, features = inputs.shape[1:]
    share = features // 4
    ff = w_fc.shape[1] // 4
    shift = 16 * wt

    small = jnp.stack([ln1_gain, ln1_bias, bias_q, bias_v, bias_out, ln2_gain, ln2_bias, bias_proj])
    received, all_order, vectors, own_qkv, normed_one, pieces, wide_out, placed_out = project(
        inputs[0], block_order, small, w_qkv, w_fc, w_out, 1
    )
    own_qkv = own_qkv.reshape(features, COLUMNS)
    normed_one = normed_one.reshape(4 * rows, features)
    gain_one, shift_one, _, _, full_bout, gain_two, shift_two, full_bproj = vectors
    orders = all_order[:, 0, :ctx_count]
    place = lax.dynamic_index_in_dim(orders, jnp.minimum(ctx // GROUP, 3), 0, keepdims=False)
    slots = jnp.arange(ctx_count, dtype=jnp.int32)
    inverse = jnp.sum(jnp.where(place[None, :] == slots[:, None], slots[None, :], 0), axis=1)
    *saved, attended, middle, all_two, own_fc, group_cot = attend(
        received,
        inverse,
        place,
        placed_out,
        inputs[0],
        jnp.concatenate([full_bout[None], gain_two[None], shift_two[None], jnp.zeros((5, features), jnp.float32)]),
        pieces,
        cotangent[0],
        4,
    )

    tokens = inputs[0].astype(jnp.float32)
    all_two = all_two.reshape(4 * rows, features)
    own_fc = own_fc.reshape(features, ff)
    group_cot = group_cot.reshape(4 * rows, features)
    hidden_pre = dot(all_two, own_fc) + bias_fc.astype(jnp.float32)
    hidden_low = gelu_tanh(hidden_pre).astype(jnp.bfloat16)
    hidden_grad = dot(group_cot, w_proj, 1, 1)
    unused_gelu, gelu_back = jax.vjp(gelu_tanh, hidden_pre)
    pre_grad = gelu_back(hidden_grad)[0].astype(jnp.bfloat16)
    low = jnp.bfloat16
    grad_fc = dot(pre_grad, all_two, 0, 0).astype(low)
    grad_proj = dot(hidden_low, group_cot, 0, 0).astype(low)
    projected_out, middle_grad, norm_sums, all_branch, upstream, window_fc, window_proj = feed_back(
        hidden_low,
        pre_grad,
        w_proj,
        own_fc,
        grad_fc,
        grad_proj,
        middle,
        gain_two[None],
        cotangent[0],
        wide_out,
        7,
    )
    outputs = middle + projected_out + full_bproj
    grad_gain_two, grad_shift_two = norm_sums[0], norm_sums[1]
    all_branch = all_branch.reshape(4 * rows, features)

    own_stacked, normed_one_grad, window_fc, window_proj = attend_back(
        upstream, inverse, place, saved, window_fc, window_proj, own_qkv, 8
    )
    unused_first, first_back = jax.vjp(layer_norm, tokens, gain_one, shift_one)
    input_part, grad_gain_one, grad_shift_one = first_back(normed_one_grad)
    input_grad = middle_grad + input_part

    own_attended = lax.dynamic_slice_in_dim(attended.reshape(4 * rows, SPAN), shift, share, 1)
    grad_qkv = dot(own_stacked, normed_one).astype(low)
    grad_out = dot(own_attended, all_branch, 0, 0).astype(low)
    column = lambda value: lax.dynamic_slice_in_dim(value, share * wt, share, 0)
    sums = jnp.sum(own_stacked.astype(jnp.float32), axis=1).reshape(3, share)
    grad_bout = column(jnp.sum(all_branch.astype(jnp.float32), axis=0))
    grad_bproj = column(jnp.sum(group_cot.astype(jnp.float32), axis=0))
    grad_bfc = jnp.sum(pre_grad.astype(jnp.float32), axis=0)
    crossed_vectors = jnp.stack([grad_gain_one, grad_shift_one, grad_gain_two, grad_shift_two]).astype(low)
    kept_vectors = jnp.stack([jnp.concatenate([sums[0], sums[2], grad_bout, grad_bproj]), grad_bfc]).astype(low)
    tail = lambda value: jnp.pad(value, ((0, 16 - value.shape[0]), (0, 0)))
    sum_qkv, sum_out, crossed, kept, sum_fc, sum_proj = finish_gradients(
        grad_qkv, grad_out, tail(crossed_vectors), tail(kept_vectors), window_fc, window_proj, 9
    )
    sum_qkv, sum_out, sum_fc = (member.astype(jnp.float32) for member in (sum_qkv, sum_out, sum_fc))
    sum_proj = sum_proj.reshape(ff, features).astype(jnp.float32)
    norms = jnp.sum(crossed[:4].reshape(4, 4, share).astype(jnp.float32), axis=1)
    kept_sums = kept[:2].astype(jnp.float32)
    sum_bq, sum_bv, sum_bout, sum_bproj = kept_sums[0].reshape(4, share)
    return (
        outputs.astype(jnp.bfloat16)[None],
        input_grad[None],
        norms[0],
        norms[1],
        sum_qkv,
        sum_bq,
        sum_bv,
        sum_out,
        sum_bout,
        norms[2],
        norms[3],
        sum_fc,
        kept_sums[1],
        sum_proj,
        sum_bproj,
    )


def solution(mesh):
    placed = (
        P("wt", "ctx", None),
        P("wt", None),
        P("wt", "ctx", None),
        P("wt"),
        P("wt"),
        P("wt", None),
        P("wt"),
        P("wt"),
        P("wt", None),
        P("wt"),
        P("wt"),
        P("wt"),
        P("wt", None),
        P("wt"),
        P("wt", None),
        P("wt"),
    )
    return jax.shard_map(
        local,
        mesh=mesh,
        in_specs=placed,
        out_specs=(
            P("wt", "ctx", None),
            P("wt", "ctx", None),
            P("wt"),
            P("wt"),
            P("wt", None),
            P("wt"),
            P("wt"),
            P("wt", None),
            P("wt"),
            P("wt"),
            P("wt"),
            P("wt", None),
            P("wt"),
            P("wt", None),
            P("wt"),
        ),
        check_vma=False,
    )
```

```python
import math

import jax
import jax.numpy as jnp
from jax import lax
from jax.experimental import pallas as pl
from jax.experimental.pallas import tpu as pltpu
from jax.sharding import PartitionSpec as P

HEADS = 25
HEAD_DIM = 64
GROUP = 7
SPAN = GROUP * HEAD_DIM
EPS = 1e-05
MESH = pl.DeviceIdType.MESH


def cost(micros):
    return pl.CostEstimate(flops=int(micros * 1e9), bytes_accessed=int(micros * 1e6), transcendentals=0)
NEG = -1e30
LOG2E = 1.4426950408889634

def layer_norm(values, gain_row, shift_row):
    centered = values - jnp.mean(values, axis=-1, keepdims=True)
    variance = jnp.mean(centered * centered, axis=-1, keepdims=True)
    return centered * lax.rsqrt(variance + EPS) * gain_row + shift_row


def gelu_tanh(values):
    return jax.nn.gelu(values, approximate=True)


def dot(left, right, left_dim=1, right_dim=0):
    return lax.dot_general(
        left, right, (((left_dim,), (right_dim,)), ((), ())), preferred_element_type=jnp.float32
    )


def greet(peers):
    barrier = pltpu.get_barrier_semaphore()
    for peer in peers:
        pl.semaphore_signal(barrier, inc=1, device_id=peer, device_id_type=MESH)
    pl.semaphore_wait(barrier, len(peers))


def remote(source, target, send, receive, device):
    return pltpu.make_async_remote_copy(source, target, send, receive, device_id=device, device_id_type=MESH)


def greet_ctx(ctx, wt, others):
    barrier = pltpu.get_barrier_semaphore()

    def signal(step, carry):
        pl.semaphore_signal(barrier, inc=1, device_id=((ctx + step) % 32, wt), device_id_type=MESH)
        return carry

    lax.fori_loop(1, 32, signal, 0)
    for other in others:
        pl.semaphore_signal(barrier, inc=1, device_id=other, device_id_type=MESH)
    pl.semaphore_wait(barrier, 31 + len(others))


class RingSum:
    def __init__(self, source, rows, place, at, relay, arrive, send, receive):
        self.source, self.rows, self.place = source, rows, place
        self.relay, self.arrive, self.send, self.receive = relay, arrive, send, receive
        self.up, self.down = (place + 1) % 4, (place + 3) % 4
        self.to = (at(self.up), at(self.down))
        cut = (rows // 32) * 16 + 16
        self.parts = ((0, cut), (cut, rows - cut))

    def block(self, place, part):
        start, extent = self.parts[part]
        return pl.ds(pl.multiple_of(place * self.rows + start, 16), extent)

    def copy(self, index):
        first, second = self.parts
        opposite = (self.place + 2) % 4
        ends = (
            (self.source.at[self.block(opposite, 0)], self.relay.at[0, pl.ds(0, first[1])], 0),
            (self.source.at[self.block(opposite, 1)], self.relay.at[1, pl.ds(0, second[1])], 1),
            (self.source.at[self.block(self.up, 1)], self.arrive.at[0, pl.ds(*second)], 0),
            (self.source.at[self.block(self.down, 0)], self.arrive.at[1, pl.ds(*first)], 1),
            (self.source.at[self.block(self.up, 0)], self.arrive.at[0, pl.ds(*first)], 0),
            (self.source.at[self.block(self.down, 1)], self.arrive.at[1, pl.ds(*second)], 1),
        )
        source, target, way = ends[index]
        return remote(source, target, self.send.at[index], self.receive.at[index], self.to[way])

    def begin(self):
        for index in range(4):
            self.copy(index).start()

    def pass_on(self):
        for way in range(2):
            self.copy(way).wait_recv()
            extent = self.parts[way][1]
            mine = self.block(self.up if way == 0 else self.down, way)
            total = self.source[mine].astype(jnp.float32) + self.relay[way, :extent].astype(jnp.float32)
            self.source[mine] = total.astype(self.source.dtype)
            self.copy(4 + way).start()

    def finish(self):
        for index in (2, 3, 4, 5):
            self.copy(index).wait_recv()
        mine = pl.ds(pl.multiple_of(self.place * self.rows, 16), self.rows)
        total = self.source[mine].astype(jnp.float32)
        return total + self.arrive[0].astype(jnp.float32) + self.arrive[1].astype(jnp.float32)

    def drain(self):
        for index in range(6):
            self.copy(index).wait_send()


class RingSpread:
    def __init__(self, target, place, at, beside, low_x, alone, send, receive):
        self.target, self.place, self.beside, self.send, self.receive = target, place, beside, send, receive
        self.up, self.down, self.opposite = (place + 1) % 4, (place + 3) % 4, (place + 2) % 4
        self.to = (at(self.up), at(self.down))
        rows = target.shape[1]
        ring = rows - alone
        cut = (rows // 32) * 16
        row = lambda start, extent: pl.ds(pl.multiple_of(start, 16), extent)
        self.parts = (pl.ds(0, cut), pl.ds(cut, rows - cut))
        self.mine, self.other = row(low_x * ring, alone), row((1 - low_x) * ring, alone)
        self.common = row(alone, ring - alone)

    def move(self, slot, rows, index, device):
        piece = self.target.at[slot, rows]
        return remote(piece, piece, self.send.at[index], self.receive.at[index], device)

    def early(self, way, slot):
        return self.move(slot, self.mine, way, self.to[way])

    def rest(self, way, slot):
        return self.move(slot, self.common, 2 + way, self.to[way])

    def half(self, way, slot):
        return self.move(slot, self.parts[way], 4 + way, self.to[way])

    def aside(self, way, rows):
        return self.move((self.down, self.up)[way], rows, 6 + way, self.beside)

    def begin(self):
        for way in range(2):
            self.early(way, self.place).start()

    def go_on(self):
        for way in range(2):
            self.rest(way, self.place).start()

    def share(self):
        for way, slot in enumerate((self.down, self.up)):
            self.early(way, slot).wait_recv()
            self.aside(way, self.mine).start()

    def pass_on(self):
        for way, slot in enumerate((self.down, self.up)):
            self.rest(way, slot).wait_recv()
            self.aside(way, self.other).wait_recv()
            self.half(way, slot).start()

    def finish(self):
        for way in range(2):
            self.half(way, self.opposite).wait_recv()

    def drain(self):
        for way, slot in enumerate((self.down, self.up)):
            self.early(way, self.place).wait_send()
            self.rest(way, self.place).wait_send()
            self.aside(way, self.mine).wait_send()
            self.half(way, slot).wait_send()


class Inner:
    def __init__(self, window, inner, place, at, ctx, wt, crosses, bufs, sems):
        self.window, self.inner, self.place, self.at, self.ctx, self.wt, self.crosses = window, inner, place, at, ctx, wt, crosses
        self.came, self.mid, self.pair, self.lanes_out, self.lanes_in, self.all = bufs
        self.inner_send, self.inner_receive, self.lane_send, self.lane_receive, self.all_send, self.all_receive, self.pair_sems = sems
        self.stride = (window.shape[0] - inner) // 3
        self.share = window.shape[1] // 4

    def rows(self, place):
        return pl.ds(pl.multiple_of(self.stride * place, 16), self.inner)

    def outward(self, step):
        other = (self.place + step) % 4
        return remote(
            self.window.at[self.rows(other)], self.came.at[step - 1],
            self.inner_send.at[step - 1], self.inner_receive.at[step - 1], self.at(other),
        )

    def beside(self):
        return remote(self.mid, self.pair, self.pair_sems.at[0], self.pair_sems.at[1], (self.ctx ^ 1, self.wt))

    def lane(self, step):
        return remote(
            self.lanes_out.at[self.wt ^ step], self.lanes_in.at[self.wt],
            self.lane_send.at[step - 1], self.lane_receive.at[step - 1], (self.ctx, self.wt ^ step),
        )

    def around(self, step):
        return remote(
            self.pair, self.all.at[self.place],
            self.all_send.at[step - 1], self.all_receive.at[step - 1], self.at((self.place + step) % 4),
        )

    def begin(self):
        for step in (1, 3, 2):
            self.outward(step).start()

    def add_inner(self):
        for step in (1, 3, 2):
            self.outward(step).wait_recv()
        total = self.window[self.rows(self.place)].astype(jnp.float32)
        for step in range(3):
            total += self.came[step].astype(jnp.float32)
        self.mid[...] = total.astype(self.mid.dtype)
        self.beside().start()

    def add_beside(self):
        self.beside().wait_recv()
        total = (self.mid[...].astype(jnp.float32) + self.pair[...].astype(jnp.float32)).astype(self.mid.dtype)
        self.pair[...] = total
        if self.crosses is False:
            self.spread()
            return
        for owner in range(4):
            self.lanes_out[owner] = total[:, owner * self.share : (owner + 1) * self.share]
        for step in (2, 3, 1):
            self.lane(step).start()
        self.lanes_in[self.wt] = self.lanes_out[self.wt]

    def spread(self):
        for step in (1, 3, 2):
            self.around(step).start()
        self.all[self.place] = self.pair[...]

    def collect(self):
        if self.crosses is False:
            return
        for step in (1, 2, 3):
            self.lane(step).wait_recv()
        for sender in range(4):
            span = slice(sender * self.share, (sender + 1) * self.share)
            part = self.lanes_in[sender]
            if self.crosses is not True:
                part = jnp.where(self.crosses, part, self.pair[:, span])
            self.pair[:, span] = part
        self.spread()

    def fill(self):
        for step in (1, 2, 3):
            self.outward(step).wait_send()
            self.around(step).wait_recv()
        for place in range(4):
            start = self.stride * place
            self.window[start : start + self.inner] = self.all[place]

    def drain(self):
        self.beside().wait_send()
        for step in (1, 2, 3):
            self.around(step).wait_send()
            if self.crosses is not False:
                self.lane(step).wait_send()


def inner_scratch(inner, features):
    low = jnp.bfloat16
    share = features // 4
    return [
        pltpu.VMEM((2, 3, inner, features), low),
        pltpu.VMEM((2, inner, features), low),
        pltpu.VMEM((2, inner, features), low),
        pltpu.VMEM((2, 4, inner, share), low),
        pltpu.VMEM((2, 4, inner, share), low),
        pltpu.VMEM((2, 4, inner, features), low),
    ] + [pltpu.SemaphoreType.DMA((2, 3))] * 6 + [pltpu.SemaphoreType.DMA((2, 2))]


def inners(windows, inner, y, z, at_y, at_z, ctx, wt, crosses, scratch):
    pick = lambda half: [ref.at[half] for ref in scratch]
    return [
        Inner(windows[0], inner, z, at_z, ctx, wt, crosses[0], pick(0)[:6], pick(0)[6:]),
        Inner(windows[1], inner, y, at_y, ctx, wt, crosses[1], pick(1)[:6], pick(1)[6:]),
    ]


COLUMNS = -(-3 * SPAN // 128) * 128


def project(inputs, block_order, vectors, w_qkv, w_fc, w_out, collective):
    rows, features = inputs.shape
    share = w_qkv.shape[0]
    ff = w_fc.shape[1] // 4
    count = vectors.shape[0]
    chunks = 5
    extent = share // chunks
    low = jnp.bfloat16
    wide = COLUMNS
    extra = SPAN - share

    def kernel(token_ref, order_ref, *refs):
        (
            vectors_ref, qkv_ref, fc_ref, w_out_ref,
            received_ref, orders_ref, vec_ref, own_ref, normed_ref, fc_out, wide_ref, placed_ref,
            all_ref, small_ref, columns_ref, pieces_ref, parts_ref, sum_ref, turned_ref, blocks_ref,
            gather_send, gather_receive, cross_send, cross_receive, fc_send, fc_receive, near_send, near_receive,
            head_send, head_receive, edges_ref, edge_send, edge_receive,
        ) = refs
        ctx, wt = lax.axis_index("ctx"), lax.axis_index("wt")
        low_x = ctx % 2
        near, far, beside = (ctx, wt ^ 1), (ctx, wt ^ 2), (ctx ^ 1, wt)
        goes, comes = wt ^ (2 + low_x), wt ^ (3 - low_x)
        across = (ctx ^ 1, goes)
        small_ref[wt, :count] = vectors_ref[...]
        orders_ref[wt, :1, :32] = order_ref[...]
        all_ref[wt] = token_ref[...]

        def columns(slot, owner):
            start = 384 * owner
            queries = qkv_ref[:, pl.ds(pl.multiple_of(start, 128), SPAN)]
            keys = qkv_ref[:, pl.ds(pl.multiple_of(features - 64 + start, 128), SPAN + 64)][:, 64:]
            values = qkv_ref[:, pl.ds(pl.multiple_of(2 * features + start, 128), SPAN)]
            for part, member in enumerate((queries, keys, values)):
                columns_ref[slot, :, part * SPAN : (part + 1) * SPAN] = member
            columns_ref[slot, :, 3 * SPAN :] = jnp.zeros((share, wide - 3 * SPAN), low)

        def edge(way):
            source = (w_out_ref.at[pl.ds(share - extra, extra)], w_out_ref.at[pl.ds(0, extra)])[way]
            other = ((wt + 1) % 4, (wt + 3) % 4)[way]
            target = (edges_ref.at[pl.ds(0, extra)], edges_ref.at[pl.ds(extra + share, extra)])[way]
            return remote(source, target, edge_send.at[way], edge_receive.at[way], (ctx, other))

        def piece(target, slot, owner):
            start = pl.multiple_of(128 * ((25 * owner) // 2), 128)
            held = fc_ref[:, pl.ds(start, ff + 64)]

            @pl.when(owner % 2 == 0)
            def _():
                target[slot] = held[:, :ff]

            @pl.when(owner % 2 == 1)
            def _():
                target[slot] = held[:, 64:]

        gathered = (all_ref, small_ref, orders_ref)

        def gather(item, step, slot, peer):
            ref = gathered[item].at[slot]
            return remote(ref, ref, gather_send.at[item, step], gather_receive.at[item, step], peer)

        def cross(index):
            span = pl.ds(index * extent, extent)
            return remote(columns_ref.at[0, span], own_ref.at[wt, span], cross_send.at[0, index], cross_receive.at[0, index], across)

        def onward(index):
            part = own_ref.at[comes, pl.ds(index * extent, extent)]
            return remote(part, part, cross_send.at[1, index], cross_receive.at[1, index], beside)

        def cross_fc():
            return remote(pieces_ref.at[0], fc_out.at[wt], fc_send, fc_receive, across)

        pair = lambda: remote(columns_ref.at[1], own_ref.at[wt], near_send.at[0], near_receive.at[0], near)
        pair_fc = lambda: remote(pieces_ref.at[1], fc_out.at[wt], near_send.at[1], near_receive.at[1], near)

        columns(0, goes)
        greet_ctx(ctx, wt, (near, far, (ctx, wt ^ 3), across, (ctx ^ 1, comes)))
        for item in range(3):
            gather(item, 0, wt, far).start()
        for index in range(chunks):
            cross(index).start()
        for item in range(3):
            gather(item, 1, wt, near).start()
        for way in range(2):
            edge(way).start()
        columns(1, wt ^ 1)
        pair().start()
        columns(2, wt)
        own_ref[wt] = columns_ref[2]
        for item in range(3):
            gather(item, 0, wt ^ 2, far).wait_recv()
            gather(item, 2, wt ^ 2, near).start()
        for item in range(3):
            gather(item, 1, wt ^ 1, near).wait_recv()
        for item in range(3):
            gather(item, 2, wt ^ 3, near).wait_recv()
        for sender in range(4):
            span = slice(sender * share, (sender + 1) * share)
            vec_ref[:, span] = small_ref[sender, :8].astype(jnp.float32)

        def norm(sequence, carry):
            normed = layer_norm(all_ref[sequence].astype(jnp.float32), vec_ref[0:1], vec_ref[1:2]).astype(low)
            normed_ref[sequence] = normed
            tokens = pl.ds(pl.multiple_of(sequence * rows, rows), rows)
            for sender in range(4):
                parts_ref[sender, tokens] = normed[:, sender * share : (sender + 1) * share]
            return carry

        lax.fori_loop(0, 4, norm, 0)
        start = pl.ds(pl.multiple_of(384 * wt, 128), SPAN)
        bias = (vec_ref[2:3, start], jnp.zeros((1, SPAN), jnp.float32), vec_ref[3:4, start])
        for part in range(3):
            sum_ref[:, part * SPAN : (part + 1) * SPAN] = jnp.broadcast_to(bias[part], (4 * rows, SPAN))
        sum_ref[:, 3 * SPAN :] = jnp.zeros((4 * rows, wide - 3 * SPAN), jnp.float32)

        def add(sender):
            sum_ref[...] += jnp.dot(parts_ref[sender], own_ref[sender], preferred_element_type=jnp.float32)

        def to_head(index):
            return remote(blocks_ref.at[index], received_ref.at[ctx], head_send.at[index], head_receive.at[ctx], (index, wt))

        def heads(sequence, carry):
            tokens = pl.ds(pl.multiple_of(sequence * rows, rows), rows)
            turned_ref[...] = sum_ref[tokens].astype(low).T
            for head in range(GROUP):
                index = sequence * GROUP + head
                for part in range(3):
                    line = part * SPAN + head * HEAD_DIM
                    blocks_ref[index, part * HEAD_DIM : (part + 1) * HEAD_DIM] = turned_ref[line : line + HEAD_DIM]

                @pl.when(index != ctx)
                def _():
                    to_head(index).start()

                @pl.when(index == ctx)
                def _():
                    received_ref[index] = blocks_ref[index]

            return carry

        add(wt)
        pair().wait_recv()
        add(wt ^ 1)
        piece(pieces_ref, 0, goes)
        piece(pieces_ref, 1, wt ^ 1)
        piece(fc_out, wt, wt)
        for index in range(chunks):
            cross(index).wait_recv()
            onward(index).start()
        cross_fc().start()
        pair_fc().start()
        add(comes)
        for index in range(chunks):
            onward(index).wait_recv()
        add(goes)
        lax.fori_loop(0, 4, heads, 0)
        edges_ref[extra : extra + share] = w_out_ref[...]
        placed_ref[...] = jnp.zeros((SPAN, features), low)
        placed_ref[pl.ds(pl.multiple_of(16 * wt, 16), share)] = w_out_ref[...]
        for way in range(2):
            edge(way).wait_recv()
        wide_ref[...] = edges_ref[pl.ds(pl.multiple_of(extra - 16 * wt, 16), SPAN)]

        def head_here(step, carry):
            source = (ctx + step) % 32
            remote(
                blocks_ref.at[0], received_ref.at[source], head_send.at[0], head_receive.at[source], (source, wt)
            ).wait_recv()
            return carry

        @pl.when(ctx < 4 * GROUP)
        def _():
            lax.fori_loop(1, 32, head_here, 0)

        def sent(index, carry):
            @pl.when(index != ctx)
            def _():
                to_head(index).wait_send()

            return carry

        lax.fori_loop(0, 4 * GROUP, sent, 0)
        for item in range(3):
            gather(item, 0, wt, far).wait_send()
            gather(item, 1, wt, near).wait_send()
            gather(item, 2, wt ^ 2, near).wait_send()
        pair().wait_send()
        for way in range(2):
            edge(way).wait_send()
        for index in range(chunks):
            cross(index).wait_send()
            onward(index).wait_send()
        cross_fc().wait()
        pair_fc().wait()

    vmem = pl.BlockSpec(memory_space=pltpu.VMEM)
    hbm = pl.BlockSpec(memory_space=pl.ANY)
    return pl.pallas_call(
        kernel,
        out_shape=(
            jax.ShapeDtypeStruct((32, 3 * HEAD_DIM, rows), low),
            jax.ShapeDtypeStruct((4, 8, 128), jnp.int32),
            jax.ShapeDtypeStruct((8, features), jnp.float32),
            jax.ShapeDtypeStruct((4, share, wide), low),
            jax.ShapeDtypeStruct((4, rows, features), low),
            jax.ShapeDtypeStruct((4, share, ff), low),
            jax.ShapeDtypeStruct((SPAN, features), low),
            jax.ShapeDtypeStruct((SPAN, features), low),
        ),
        in_specs=[vmem] * 6,
        out_specs=(vmem,) * 8,
        scratch_shapes=[
            pltpu.VMEM((4, rows, features), low),
            pltpu.VMEM((4, 16, share), low),
            pltpu.VMEM((3, share, wide), low),
            pltpu.VMEM((2, share, ff), low),
            pltpu.VMEM((4, 4 * rows, share), low),
            pltpu.VMEM((4 * rows, wide), jnp.float32),
            pltpu.VMEM((wide, rows), low),
            pltpu.VMEM((4 * GROUP, 3 * HEAD_DIM, rows), low),
            pltpu.SemaphoreType.DMA((3, 3)),
            pltpu.SemaphoreType.DMA((3, 3)),
            pltpu.SemaphoreType.DMA((2, chunks)),
            pltpu.SemaphoreType.DMA((2, chunks)),
            pltpu.SemaphoreType.DMA,
            pltpu.SemaphoreType.DMA,
            pltpu.SemaphoreType.DMA((2,)),
            pltpu.SemaphoreType.DMA((2,)),
            pltpu.SemaphoreType.DMA((4 * GROUP,)),
            pltpu.SemaphoreType.DMA((32,)),
            pltpu.VMEM((share + 2 * extra, features), low),
            pltpu.SemaphoreType.DMA((2,)),
            pltpu.SemaphoreType.DMA((2,)),
        ],
        compiler_params=pltpu.CompilerParams(
            collective_id=collective, has_side_effects=True, vmem_limit_bytes=56 * 2**20
        ),
        name="project",
    )(inputs, block_order, vectors, w_qkv, w_fc, w_out)


def attend(received, inverse, place, placed_out, tokens, small, pieces, cotangent, collective):
    parts, wide, rows = received.shape
    dim = wide // 3
    features = tokens.shape[1]
    block = math.gcd(1024, parts * rows)
    per = block // rows
    count = parts // per
    chunks = 5
    extent = pieces.shape[1] // chunks
    low = jnp.bfloat16
    hold, off = place // per, place % per

    def kernel(
        inverse_ref, hold_ref, off_ref, in_ref, weight_ref, token_ref, small_ref, pieces_ref, cot_ref,
        q_ref, kt_ref, k_ref, v_ref, att_ref, lse_ref, stacked_ref, middle_ref, all_ref, fc_ref, all_cot_ref,
        vt_ref, blocks_ref, came_ref, turned_ref, terms_ref, bufs,
        head_send, head_receive, term_send, term_receive, all_send, all_receive,
        cross_send, cross_receive, cot_send, cot_receive,
    ):
        ctx, wt = lax.axis_index("ctx"), lax.axis_index("wt")
        low_x = ctx % 2
        near, far, beside = (ctx, wt ^ 1), (ctx, wt ^ 2), (ctx ^ 1, wt)
        comes = wt ^ (3 - low_x)
        greet_ctx(ctx, wt, (near, far))

        def onward(index):
            span = pl.ds(index * extent, extent)
            return remote(
                pieces_ref.at[comes, span], fc_ref.at[comes, span], cross_send.at[index], cross_receive.at[index], beside
            )

        def upstream(step, source, slot, peer):
            return remote(source, all_cot_ref.at[slot], cot_send.at[step], cot_receive.at[step], peer)

        for index in range(chunks):
            onward(index).start()
        upstream(0, cot_ref, wt, far).start()
        upstream(1, cot_ref, wt, near).start()
        def arrange(index, carry):
            for sub in range(per):
                piece = in_ref[inverse_ref[index * per + sub]]
                lanes = pl.ds(sub * rows, rows)
                q_ref[index, :, lanes] = piece[:dim]
                kt_ref[index, :, lanes] = piece[dim : 2 * dim]
                vt_ref[index, :, lanes] = piece[2 * dim :]
                k_ref[index, lanes, :] = piece[dim : 2 * dim].T
                v_ref[index, lanes, :] = piece[2 * dim :].T
            return carry

        lax.fori_loop(0, count, arrange, 0)
        row = lax.broadcasted_iota(jnp.int32, (block, block), 0)
        col = lax.broadcasted_iota(jnp.int32, (block, block), 1)
        factor = LOG2E * dim**-0.5

        def step(qi, kj, carry, diagonal):
            peak, mass, total = carry
            scores = jnp.dot(k_ref[kj], q_ref[qi], preferred_element_type=jnp.float32) * factor
            if diagonal:
                scores = jnp.where(row <= col, scores, NEG)
            new_peak = jnp.maximum(peak, jnp.max(scores, axis=0, keepdims=True))
            weights = jnp.exp2(scores - new_peak)
            shrink = jnp.exp2(peak - new_peak)
            mass = mass * shrink + jnp.sum(weights, axis=0, keepdims=True)
            total = total * shrink + jnp.dot(vt_ref[kj], weights.astype(low), preferred_element_type=jnp.float32)
            return (new_peak, mass, total)

        def query_block(qi, carry):
            start = (
                jnp.full((1, block), NEG, jnp.float32),
                jnp.zeros((1, block), jnp.float32),
                jnp.zeros((dim, block), jnp.float32),
            )
            state = lax.fori_loop(0, qi, lambda kj, cur: step(qi, kj, cur, False), start)
            peak, mass, total = step(qi, qi, state, True)
            att_ref[qi] = total / mass
            lse_ref[qi] = peak + jnp.log2(mass)
            return carry

        lax.fori_loop(0, count, query_block, 0)

        def to_owner(index):
            return remote(blocks_ref.at[index], came_ref.at[ctx], head_send.at[index], head_receive.at[ctx], (index, wt))

        def give_back(index, carry):
            whole = att_ref[hold_ref[index]]
            picked = whole[:, :rows]
            for sub in range(1, per):
                picked = jnp.where(off_ref[index] == sub, whole[:, sub * rows : (sub + 1) * rows], picked)
            blocks_ref[index] = picked.astype(low)

            @pl.when(index != ctx)
            def _():
                to_owner(index).start()

            @pl.when(index == ctx)
            def _():
                came_ref[index] = blocks_ref[index]

            return carry

        @pl.when(ctx < 4 * GROUP)
        def _():
            lax.fori_loop(0, parts, give_back, 0)

        upstream(0, cot_ref, wt ^ 2, far).wait_recv()
        upstream(2, all_cot_ref.at[wt ^ 2], wt ^ 2, near).start()
        all_cot_ref[wt] = cot_ref[...]
        for slot in (wt, wt ^ 1, comes):
            fc_ref[slot] = pieces_ref[slot]

        def owner_here(source, carry):
            @pl.when(source != ctx)
            def _():
                remote(
                    blocks_ref.at[0], came_ref.at[source], head_send.at[0], head_receive.at[source], (source, wt)
                ).wait_recv()

            return carry

        lax.fori_loop(0, 4 * GROUP, owner_here, 0)

        def make_terms(sequence):
            for head in range(GROUP):
                turned_ref[head * dim : (head + 1) * dim] = came_ref[sequence * GROUP + head]
            stacked_ref[sequence] = turned_ref[...].T
            terms_ref[...] = jnp.dot(stacked_ref[sequence], weight_ref[...], preferred_element_type=jnp.float32)

        def term(index, source, target, peer):
            return remote(bufs.at[source], bufs.at[target], term_send.at[index], term_receive.at[index], peer)

        make_terms(wt ^ 3)
        bufs[0] = terms_ref[...].astype(low)
        term(0, 0, 3, near).start()
        make_terms(wt ^ 1)
        bufs[1] = terms_ref[...].astype(low)
        term(1, 1, 4, near).start()
        make_terms(wt ^ 2)
        term(0, 0, 3, near).wait_recv()
        bufs[2] = (terms_ref[...] + bufs[3].astype(jnp.float32)).astype(low)
        term(2, 2, 5, far).start()
        make_terms(wt)
        middle_ref[...] = token_ref[...].astype(jnp.float32) + terms_ref[...] + small_ref[0:1]
        term(1, 1, 4, near).wait_recv()
        middle_ref[...] += bufs[4].astype(jnp.float32)
        term(2, 2, 5, far).wait_recv()
        middle_ref[...] += bufs[5].astype(jnp.float32)
        all_ref[wt] = layer_norm(middle_ref[...], small_ref[1:2], small_ref[2:3]).astype(low)

        def normed(step, slot, peer):
            return remote(all_ref.at[slot], all_ref.at[slot], all_send.at[step], all_receive.at[step], peer)

        normed(0, wt, far).start()
        normed(1, wt, near).start()
        normed(0, wt ^ 2, far).wait_recv()
        normed(2, wt ^ 2, near).start()
        normed(1, wt ^ 1, near).wait_recv()
        normed(2, wt ^ 3, near).wait_recv()
        normed(0, wt, far).wait_send()
        normed(1, wt, near).wait_send()
        normed(2, wt ^ 2, near).wait_send()
        term(0, 0, 3, near).wait_send()
        term(1, 1, 4, near).wait_send()
        term(2, 2, 5, far).wait_send()
        upstream(1, cot_ref, wt ^ 1, near).wait_recv()
        upstream(2, all_cot_ref.at[wt ^ 2], wt ^ 3, near).wait_recv()
        upstream(0, cot_ref, wt, far).wait_send()
        upstream(1, cot_ref, wt, near).wait_send()
        upstream(2, all_cot_ref.at[wt ^ 2], wt ^ 2, near).wait_send()
        for index in range(chunks):
            onward(index).wait()

        def sent(index, carry):
            @pl.when(index != ctx)
            def _():
                to_owner(index).wait_send()

            return carry

        @pl.when(ctx < 4 * GROUP)
        def _():
            lax.fori_loop(0, parts, sent, 0)

    smem = pl.BlockSpec(memory_space=pltpu.SMEM)
    vmem = pl.BlockSpec(memory_space=pltpu.VMEM)
    hbm = pl.BlockSpec(memory_space=pl.ANY)
    lane_first = jax.ShapeDtypeStruct((count, dim, block), low)
    row_first = jax.ShapeDtypeStruct((count, block, dim), low)
    return pl.pallas_call(
        kernel,
        out_shape=(
            lane_first,
            lane_first,
            row_first,
            row_first,
            jax.ShapeDtypeStruct((count, dim, block), jnp.float32),
            jax.ShapeDtypeStruct((count, 1, block), jnp.float32),
            jax.ShapeDtypeStruct((4, rows, SPAN), low),
            jax.ShapeDtypeStruct((rows, features), jnp.float32),
            jax.ShapeDtypeStruct((4, rows, features), low),
            jax.ShapeDtypeStruct(pieces.shape, low),
            jax.ShapeDtypeStruct((4, rows, features), low),
        ),
        in_specs=[smem] * 3 + [vmem] * 6,
        out_specs=(vmem,) * 11,
        scratch_shapes=[
            pltpu.VMEM((count, dim, block), low),
            pltpu.VMEM((parts, dim, rows), low),
            pltpu.VMEM((parts, dim, rows), low),
            pltpu.VMEM((SPAN, rows), low),
            pltpu.VMEM((rows, features), jnp.float32),
            pltpu.VMEM((6, rows, features), low),
            pltpu.SemaphoreType.DMA((parts,)),
            pltpu.SemaphoreType.DMA((parts,)),
            pltpu.SemaphoreType.DMA((3,)),
            pltpu.SemaphoreType.DMA((3,)),
            pltpu.SemaphoreType.DMA((3,)),
            pltpu.SemaphoreType.DMA((3,)),
            pltpu.SemaphoreType.DMA((chunks,)),
            pltpu.SemaphoreType.DMA((chunks,)),
            pltpu.SemaphoreType.DMA((3,)),
            pltpu.SemaphoreType.DMA((3,)),
        ],
        compiler_params=pltpu.CompilerParams(
            collective_id=collective, has_side_effects=True, vmem_limit_bytes=56 * 2**20
        ),
        name="attend",
    )(inverse, hold, off, received, placed_out, tokens, small, pieces, cotangent)


def feed_back(hidden, pre_grad, w_proj, own_fc, grad_fc, grad_proj, middle, gain, cotangent, wide_out, collective):
    rows, features = middle.shape
    block = grad_fc.shape[0] // 4
    low = jnp.bfloat16

    def kernel(
        hidden_ref, pre_ref, w_proj_ref, w_fc_ref, fc_ref, proj_ref, middle_ref, gain_ref, cot_ref, wide_ref,
        out_ref, middle_grad_ref, vectors_ref, all_ref, up_ref, fc_out, proj_out,
        fc_work, proj_work, terms_ref, bufs, relay, arrive, blocks_ref,
        ring_send, ring_receive, term_send, term_receive, all_send, all_receive, head_send, head_receive, fetch,
    ):
        ctx, wt = lax.axis_index("ctx"), lax.axis_index("wt")
        y, z, low_x = ctx // 8, ctx // 2 % 4, ctx % 2
        at_y = lambda place: (place * 8 + z * 2 + low_x, wt)
        at_z = lambda place: (y * 8 + place * 2 + low_x, wt)
        near, far = (ctx, wt ^ 1), (ctx, wt ^ 2)
        loads = [
            pltpu.make_async_copy(source, target, fetch.at[index])
            for index, (source, target) in enumerate(((fc_ref, fc_work), (proj_ref, proj_work)))
        ]
        for load in loads:
            load.start()
        greet_ctx(ctx, wt, (near, far))

        def term(item, step, source, target, peer):
            return remote(
                bufs.at[item, source], bufs.at[item, target], term_send.at[item, step], term_receive.at[item, step], peer
            )

        def tokens(sequence):
            return terms_ref[pl.ds(pl.multiple_of(sequence * rows, rows), rows)]

        def begin_terms(item):
            bufs[item, 0] = tokens(wt ^ 3).astype(low)
            term(item, 0, 0, 3, near).start()
            bufs[item, 1] = tokens(wt ^ 1).astype(low)
            term(item, 1, 1, 4, near).start()

        def pass_terms(item):
            term(item, 0, 0, 3, near).wait_recv()
            bufs[item, 2] = (tokens(wt ^ 2) + bufs[item, 3].astype(jnp.float32)).astype(low)
            term(item, 2, 2, 5, far).start()

        def end_terms(item):
            term(item, 1, 1, 4, near).wait_recv()
            total = tokens(wt) + bufs[item, 4].astype(jnp.float32)
            term(item, 2, 2, 5, far).wait_recv()
            return total + bufs[item, 5].astype(jnp.float32)

        rings = [
            RingSum(fc_work, block, y, at_y, relay.at[0], arrive.at[0], ring_send.at[0], ring_receive.at[0]),
            RingSum(proj_work, block, z, at_z, relay.at[1], arrive.at[1], ring_send.at[1], ring_receive.at[1]),
        ]
        for load, ring in zip(loads, rings):
            load.wait()
            ring.begin()
        terms_ref[...] = lax.dot_general(
            pre_ref[...], w_fc_ref[...], (((1,), (1,)), ((), ())), preferred_element_type=jnp.float32
        )
        begin_terms(0)
        pass_terms(0)
        grad = end_terms(0)
        values = middle_ref[...]
        centered = values - jnp.mean(values, axis=-1, keepdims=True)
        scale = lax.rsqrt(jnp.mean(centered * centered, axis=-1, keepdims=True) + EPS)
        normed = centered * scale
        vectors_ref[0:1] = jnp.sum(grad * normed, axis=0, keepdims=True)
        vectors_ref[1:2] = jnp.sum(grad, axis=0, keepdims=True)
        weighted = grad * gain_ref[...]
        part = weighted - jnp.mean(weighted, axis=-1, keepdims=True)
        part = part - normed * jnp.mean(weighted * normed, axis=-1, keepdims=True)
        middle_grad = cot_ref[...].astype(jnp.float32) + scale * part
        middle_grad_ref[...] = middle_grad
        all_ref[wt] = middle_grad.astype(low)

        def branch(step, slot, peer):
            return remote(all_ref.at[slot], all_ref.at[slot], all_send.at[step], all_receive.at[step], peer)

        branch(0, wt, far).start()
        branch(1, wt, near).start()

        def to_head(index, other):
            return remote(
                blocks_ref.at[index], up_ref.at[ctx], head_send.at[index], head_receive.at[ctx], (other, wt)
            )

        def heads(turn, sequence):
            grads = lax.dot_general(
                wide_ref[...], all_ref[sequence], (((1,), (1,)), ((), ())), preferred_element_type=jnp.float32
            ).astype(low)
            for head in range(GROUP):
                index, other = turn * GROUP + head, sequence * GROUP + head
                blocks_ref[index] = grads[head * HEAD_DIM : (head + 1) * HEAD_DIM]

                @pl.when(other != ctx)
                def _():
                    to_head(index, other).start()

                @pl.when(other == ctx)
                def _():
                    up_ref[other] = blocks_ref[index]

        heads(0, wt)
        terms_ref[...] = jnp.dot(hidden_ref[...], w_proj_ref[...], preferred_element_type=jnp.float32)
        begin_terms(1)
        branch(0, wt ^ 2, far).wait_recv()
        branch(2, wt ^ 2, near).start()
        branch(1, wt ^ 1, near).wait_recv()
        heads(1, wt ^ 1)
        heads(2, wt ^ 2)
        pass_terms(1)
        branch(2, wt ^ 3, near).wait_recv()
        heads(3, wt ^ 3)
        for ring in rings:
            ring.pass_on()
        out_ref[...] = end_terms(1)
        fc_out[...] = rings[0].finish().astype(low)
        proj_out[...] = rings[1].finish().astype(low)

        def head_here(step, carry):
            source = (ctx + step) % 32
            remote(blocks_ref.at[0], up_ref.at[source], head_send.at[0], head_receive.at[source], (source, wt)).wait_recv()
            return carry

        @pl.when(ctx < 4 * GROUP)
        def _():
            lax.fori_loop(1, 32, head_here, 0)

        for turn, sequence in enumerate((wt, wt ^ 1, wt ^ 2, wt ^ 3)):
            for head in range(GROUP):
                index, other = turn * GROUP + head, sequence * GROUP + head

                @pl.when(other != ctx)
                def _():
                    to_head(index, other).wait_send()

        for item in range(2):
            term(item, 0, 0, 3, near).wait_send()
            term(item, 1, 1, 4, near).wait_send()
            term(item, 2, 2, 5, far).wait_send()
        branch(0, wt, far).wait_send()
        branch(1, wt, near).wait_send()
        branch(2, wt ^ 2, near).wait_send()
        for ring in rings:
            ring.drain()

    vmem = pl.BlockSpec(memory_space=pltpu.VMEM)
    hbm = pl.BlockSpec(memory_space=pl.ANY)
    cut = (block // 32) * 16 + 16
    return pl.pallas_call(
        kernel,
        out_shape=(
            jax.ShapeDtypeStruct((rows, features), jnp.float32),
            jax.ShapeDtypeStruct((rows, features), jnp.float32),
            jax.ShapeDtypeStruct((8, features), jnp.float32),
            jax.ShapeDtypeStruct((4, rows, features), low),
            jax.ShapeDtypeStruct((32, HEAD_DIM, rows), low),
            jax.ShapeDtypeStruct((block, features), low),
            jax.ShapeDtypeStruct((block, features), low),
        ),
        in_specs=[vmem] * 4 + [hbm] * 2 + [vmem] * 4,
        out_specs=(vmem,) * 7,
        scratch_shapes=[
            pltpu.VMEM(grad_fc.shape, low),
            pltpu.VMEM(grad_proj.shape, low),
            pltpu.VMEM((4 * rows, features), jnp.float32),
            pltpu.VMEM((2, 6, rows, features), low),
            pltpu.VMEM((2, 2, cut, features), low),
            pltpu.VMEM((2, 2, block, features), low),
            pltpu.VMEM((4 * GROUP, HEAD_DIM, rows), low),
            pltpu.SemaphoreType.DMA((2, 6)),
            pltpu.SemaphoreType.DMA((2, 6)),
            pltpu.SemaphoreType.DMA((2, 3)),
            pltpu.SemaphoreType.DMA((2, 3)),
            pltpu.SemaphoreType.DMA((3,)),
            pltpu.SemaphoreType.DMA((3,)),
            pltpu.SemaphoreType.DMA((4 * GROUP,)),
            pltpu.SemaphoreType.DMA((32,)),
            pltpu.SemaphoreType.DMA((2,)),
        ],
        compiler_params=pltpu.CompilerParams(
            collective_id=collective, has_side_effects=True, vmem_limit_bytes=56 * 2**20
        ),
        name="feed_back",
    )(hidden, pre_grad, w_proj, own_fc, grad_fc, grad_proj, middle, gain, cotangent, wide_out)


def attend_back(upstream, inverse, place, saved, window_fc, window_proj, own_qkv, collective):
    parts, dim, rows = upstream.shape
    q, kt, k, v, attended, lse = saved
    count, block = k.shape[:2]
    per = block // rows
    features = window_fc.shape[1]
    inner = 112
    low = jnp.bfloat16
    hold, off = place // per, place % per

    def kernel(
        inverse_ref, hold_ref, off_ref, up_ref, q_ref, kt_ref, k_ref, v_ref, att_ref, lse_ref, fc_ref, proj_ref, qkv_ref,
        own_ref, grad_ref, fc_out, proj_out,
        up_sorted, up_rows, q_rows, delta_ref, gq_ref, gk_ref, gv_ref, blocks_ref, came_ref, turned_ref, plain_ref, terms_ref, bufs,
        head_send, head_receive, term_send, term_receive, *scratch,
    ):
        ctx, wt = lax.axis_index("ctx"), lax.axis_index("wt")
        y, z, low_x = ctx // 8, ctx // 2 % 4, ctx % 2
        at_y = lambda where: (where * 8 + z * 2 + low_x, wt)
        at_z = lambda where: (y * 8 + where * 2 + low_x, wt)
        near, far = (ctx, wt ^ 1), (ctx, wt ^ 2)
        fc_out[...] = fc_ref[...]
        proj_out[...] = proj_ref[...]
        greet_ctx(ctx, wt, (near, far, (ctx, wt ^ 3)))
        steps = inners((fc_out, proj_out), inner, y, z, at_y, at_z, ctx, wt, (True, False), scratch)
        for one in steps:
            one.begin()

        def arrange(index, carry):
            for sub in range(per):
                piece = up_ref[inverse_ref[index * per + sub]]
                lanes = pl.ds(sub * rows, rows)
                up_sorted[index, :, lanes] = piece
                up_rows[index, lanes, :] = piece.T
            q_rows[index] = q_ref[index].T
            delta_ref[index] = jnp.sum(up_sorted[index].astype(jnp.float32) * att_ref[index], axis=0, keepdims=True)
            gk_ref[index] = jnp.zeros((block, dim), jnp.float32)
            gv_ref[index] = jnp.zeros((block, dim), jnp.float32)
            return carry

        lax.fori_loop(0, count, arrange, 0)
        row = lax.broadcasted_iota(jnp.int32, (block, block), 0)
        col = lax.broadcasted_iota(jnp.int32, (block, block), 1)
        factor = LOG2E * dim**-0.5

        def step(qi, kj, total, diagonal):
            scores = jnp.dot(k_ref[kj], q_ref[qi], preferred_element_type=jnp.float32) * factor
            weights = jnp.exp2(scores - lse_ref[qi])
            if diagonal:
                weights = jnp.where(row <= col, weights, 0.0)
            prob_grad = jnp.dot(v_ref[kj], up_sorted[qi], preferred_element_type=jnp.float32)
            score_grad = (weights * (prob_grad - delta_ref[qi])).astype(low)
            gv_ref[kj] += jnp.dot(weights.astype(low), up_rows[qi], preferred_element_type=jnp.float32)
            gk_ref[kj] += jnp.dot(score_grad, q_rows[qi], preferred_element_type=jnp.float32)
            return total + jnp.dot(kt_ref[kj], score_grad, preferred_element_type=jnp.float32)

        def query_block(qi, carry):
            total = lax.fori_loop(
                0, qi, lambda kj, cur: step(qi, kj, cur, False), jnp.zeros((dim, block), jnp.float32)
            )
            gq_ref[qi] = step(qi, qi, total, True) * dim**-0.5
            return carry

        lax.fori_loop(0, count - 1, query_block, 0)
        for one in steps:
            one.add_inner()
        lax.fori_loop(count - 1, count, query_block, 0)

        def to_owner(index):
            return remote(blocks_ref.at[index], came_ref.at[ctx], head_send.at[index], head_receive.at[ctx], (index, wt))

        def give_back(index, carry):
            def pick(whole, axis):
                cuts = [lax.slice_in_dim(whole, sub * rows, (sub + 1) * rows, axis=axis) for sub in range(per)]
                picked = cuts[0]
                for sub in range(1, per):
                    picked = jnp.where(off_ref[index] == sub, cuts[sub], picked)
                return picked

            blocks_ref[index, :dim] = pick(gq_ref[hold_ref[index]], 1).astype(low)
            blocks_ref[index, dim : 2 * dim] = (pick(gk_ref[hold_ref[index]], 0) * dim**-0.5).T.astype(low)
            blocks_ref[index, 2 * dim :] = pick(gv_ref[hold_ref[index]], 0).T.astype(low)

            @pl.when(index != ctx)
            def _():
                to_owner(index).start()

            @pl.when(index == ctx)
            def _():
                came_ref[index] = blocks_ref[index]

            return carry

        @pl.when(ctx < 4 * GROUP)
        def _():
            lax.fori_loop(0, parts, give_back, 0)

        for one in steps:
            one.add_beside()

        def owner_here(source, carry):
            @pl.when(source != ctx)
            def _():
                remote(
                    blocks_ref.at[0], came_ref.at[source], head_send.at[0], head_receive.at[source], (source, wt)
                ).wait_recv()

            return carry

        lax.fori_loop(0, 4 * GROUP, owner_here, 0)
        for one in steps:
            one.collect()
        feature = lax.broadcasted_iota(jnp.int32, (dim, rows), 0)
        turned_ref[3 * SPAN :] = jnp.zeros((COLUMNS - 3 * SPAN, rows), low)

        def make_terms(sequence):
            for head in range(GROUP):
                piece = came_ref[sequence * GROUP + head]
                place_in = feature + head * dim
                mine = (place_in >= 16 * wt) & (place_in < 16 * wt + features // 4)
                for part in range(3):
                    line = piece[part * dim : (part + 1) * dim]
                    start = part * SPAN + head * dim
                    plain_ref[part, head * dim : (head + 1) * dim] = line
                    turned_ref[start : start + dim] = jnp.where(mine, line.astype(jnp.float32), 0.0).astype(low)
            tokens = pl.ds(pl.multiple_of(sequence * rows, rows), rows)
            for part in range(3):
                lines = plain_ref[part, pl.ds(pl.multiple_of(16 * wt, 16), features // 4)]
                own_ref[part * (features // 4) : (part + 1) * (features // 4), tokens] = lines
            terms_ref[...] = lax.dot_general(
                turned_ref[...].T, qkv_ref[...], (((1,), (1,)), ((), ())), preferred_element_type=jnp.float32
            )

        def term(index, source, target, peer):
            return remote(bufs.at[source], bufs.at[target], term_send.at[index], term_receive.at[index], peer)

        make_terms(wt ^ 3)
        bufs[0] = terms_ref[...].astype(low)
        term(0, 0, 3, near).start()
        make_terms(wt ^ 1)
        bufs[1] = terms_ref[...].astype(low)
        term(1, 1, 4, near).start()
        make_terms(wt ^ 2)
        term(0, 0, 3, near).wait_recv()
        bufs[2] = (terms_ref[...] + bufs[3].astype(jnp.float32)).astype(low)
        term(2, 2, 5, far).start()
        make_terms(wt)
        term(1, 1, 4, near).wait_recv()
        grad_ref[...] = terms_ref[...] + bufs[4].astype(jnp.float32)
        term(2, 2, 5, far).wait_recv()
        grad_ref[...] += bufs[5].astype(jnp.float32)
        term(0, 0, 3, near).wait_send()
        term(1, 1, 4, near).wait_send()
        term(2, 2, 5, far).wait_send()

        def sent(index, carry):
            @pl.when(index != ctx)
            def _():
                to_owner(index).wait_send()

            return carry

        @pl.when(ctx < 4 * GROUP)
        def _():
            lax.fori_loop(0, parts, sent, 0)

        for one in steps:
            one.fill()
        for one in steps:
            one.drain()

    smem = pl.BlockSpec(memory_space=pltpu.SMEM)
    vmem = pl.BlockSpec(memory_space=pltpu.VMEM)
    return pl.pallas_call(
        kernel,
        out_shape=(
            jax.ShapeDtypeStruct((3 * features // 4, 4 * rows), low),
            jax.ShapeDtypeStruct((rows, features), jnp.float32),
            jax.ShapeDtypeStruct(window_fc.shape, low),
            jax.ShapeDtypeStruct(window_proj.shape, low),
        ),
        in_specs=[smem] * 3 + [vmem] * 10,
        out_specs=(vmem,) * 4,
        scratch_shapes=[
            pltpu.VMEM((count, dim, block), low),
            pltpu.VMEM((count, block, dim), low),
            pltpu.VMEM((count, block, dim), low),
            pltpu.VMEM((count, 1, block), jnp.float32),
            pltpu.VMEM((count, dim, block), jnp.float32),
            pltpu.VMEM((count, block, dim), jnp.float32),
            pltpu.VMEM((count, block, dim), jnp.float32),
            pltpu.VMEM((parts, 3 * dim, rows), low),
            pltpu.VMEM((parts, 3 * dim, rows), low),
            pltpu.VMEM((COLUMNS, rows), low),
            pltpu.VMEM((3, SPAN, rows), low),
            pltpu.VMEM((rows, features), jnp.float32),
            pltpu.VMEM((6, rows, features), low),
            pltpu.SemaphoreType.DMA((parts,)),
            pltpu.SemaphoreType.DMA((parts,)),
            pltpu.SemaphoreType.DMA((3,)),
            pltpu.SemaphoreType.DMA((3,)),
        ]
        + inner_scratch(inner, features),
        compiler_params=pltpu.CompilerParams(
            collective_id=collective, has_side_effects=True, vmem_limit_bytes=56 * 2**20
        ),
        name="attend_back",
    )(inverse, hold, off, upstream, q, kt, k, v, attended, lse, window_fc, window_proj, own_qkv)


def finish_gradients(grad_qkv, grad_out, crossed, kept, window_fc, window_proj, collective):
    share, features = grad_out.shape
    extra = crossed.shape[0]
    size = (share + extra) // 2
    block = window_fc.shape[0]
    inner = 64
    low = jnp.bfloat16

    def kernel(
        qkv_ref, out_ref, crossed_ref, kept_ref, fc_ref, proj_ref,
        qkv_turned, out_rows, crossed_rows, kept_rows, fc_turned, proj_out,
        first_out, second_out, fc_out, work, relay, arrive, ring_send, ring_receive, mlp_send, mlp_receive, out_send, out_receive, fetch, *scratch,
    ):
        ctx, wt = lax.axis_index("ctx"), lax.axis_index("wt")
        y, z, low_x = ctx // 8, ctx // 2 % 4, ctx % 2
        at_y = lambda place: (place * 8 + z * 2 + low_x, wt)
        at_z = lambda place: (y * 8 + place * 2 + low_x, wt)
        moves = [
            (qkv_ref.at[pl.ds(0, share)], work.at[0, pl.ds(0, share)]),
            (crossed_ref, work.at[0, pl.ds(share, extra)]),
            (qkv_ref.at[pl.ds(share, share)], work.at[0, pl.ds(share + extra, share)]),
            (qkv_ref.at[pl.ds(2 * share, share)], work.at[1, pl.ds(0, share)]),
            (out_ref, work.at[1, pl.ds(share + extra, share)]),
            (kept_ref, work.at[1, pl.ds(2 * share + extra, extra)]),
        ]
        moves += [(fc_ref, fc_out.at[y]), (proj_ref, proj_out.at[z])]
        loads = [pltpu.make_async_copy(source, target, fetch.at[index]) for index, (source, target) in enumerate(moves)]
        work[0, 2 * share + extra :] = jnp.zeros((extra, features), low)
        work[1, share : share + extra] = jnp.zeros((extra, features), low)
        for load in loads:
            load.start()
        peers = [at_y((y + step) % 4) for step in (1, 2, 3)] + [at_z((z + step) % 4) for step in (1, 2, 3)]
        greet(peers + [(ctx ^ 1, wt)] + [(ctx, wt ^ step) for step in (1, 2, 3)])
        for load in loads[:6]:
            load.wait()
        rings = [
            RingSum(work.at[0], size, y, at_y, relay.at[0], arrive.at[0], ring_send.at[0], ring_receive.at[0]),
            RingSum(work.at[1], size, z, at_z, relay.at[1], arrive.at[1], ring_send.at[1], ring_receive.at[1]),
        ]
        beside = (ctx ^ 1, wt)
        mlp = [
            RingSpread(fc_out, y, at_y, beside, low_x, 144, mlp_send.at[0], mlp_receive.at[0]),
            RingSpread(proj_out, z, at_z, beside, low_x, 144, mlp_send.at[1], mlp_receive.at[1]),
        ]
        for load in loads[6:]:
            load.wait()
        for one in mlp:
            one.begin()
        for ring in rings:
            ring.begin()
        for one in mlp:
            one.share()
        for ring in rings:
            ring.pass_on()
        for one in mlp:
            one.go_on()
        first_out[y] = rings[0].finish().astype(low)
        second_out[z] = rings[1].finish().astype(low)
        steps = inners(
            (first_out.at[y], second_out.at[z]), inner, y, z, at_y, at_z, ctx, wt, (True, z < 2), scratch
        )
        for one in steps:
            one.begin()
        for one in steps:
            one.add_inner()
        for one in steps:
            one.add_beside()
        for one in steps:
            one.collect()
        for one in mlp:
            one.pass_on()
        for one in steps:
            one.fill()
        spreads = [
            RingSpread(first_out, y, at_y, beside, low_x, 32, out_send.at[0], out_receive.at[0]),
            RingSpread(second_out, z, at_z, beside, low_x, 32, out_send.at[1], out_receive.at[1]),
        ]
        for one in spreads:
            one.begin()
            one.go_on()
        for one in mlp:
            one.finish()
        for one in spreads:
            one.share()

        def turn(source, place, extent, target, start, width):
            for sender in range(4):
                part = source[place, :extent, sender * share : (sender + 1) * share].astype(jnp.float32).T.astype(low)
                at = start + sender * width
                target[:, at : at + extent] = part

        turn(fc_out, 0, block, fc_turned, 0, 4 * block)
        for one in spreads:
            one.pass_on()
        for place in range(1, 4):
            turn(fc_out, place, block, fc_turned, place * block, 4 * block)
        for one in spreads:
            one.finish()
        left = share - size
        for part, (source, place) in enumerate(((first_out, 0), (first_out, 2), (second_out, 0))):
            turn(source, place, size, qkv_turned, part * features, share)
            turn(source, place + 1, left, qkv_turned, part * features + size, share)
        out_rows[:size] = second_out[2]
        out_rows[size:] = second_out[3, :left]
        crossed_rows[...] = first_out[1, left:]
        kept_rows[...] = second_out[3, left:]
        for one in rings + steps + mlp + spreads:
            one.drain()

    vmem = pl.BlockSpec(memory_space=pltpu.VMEM)
    hbm = pl.BlockSpec(memory_space=pl.ANY)
    cut = (size // 32) * 16 + 16
    return pl.pallas_call(
        kernel,
        out_shape=(
            jax.ShapeDtypeStruct((share, 3 * features), low),
            jax.ShapeDtypeStruct((share, features), low),
            jax.ShapeDtypeStruct((extra, features), low),
            jax.ShapeDtypeStruct((extra, features), low),
            jax.ShapeDtypeStruct((share, 16 * block), low),
            jax.ShapeDtypeStruct((4, block, features), low),
        ),
        in_specs=[hbm] * 6,
        out_specs=(vmem,) * 6,
        scratch_shapes=[
            pltpu.VMEM((4, size, features), low),
            pltpu.VMEM((4, size, features), low),
            pltpu.VMEM((4, block, features), low),
            pltpu.VMEM((2, 4 * size, features), low),
            pltpu.VMEM((2, 2, cut, features), low),
            pltpu.VMEM((2, 2, size, features), low),
            pltpu.SemaphoreType.DMA((2, 6)),
            pltpu.SemaphoreType.DMA((2, 6)),
            pltpu.SemaphoreType.DMA((2, 8)),
            pltpu.SemaphoreType.DMA((2, 8)),
            pltpu.SemaphoreType.DMA((2, 8)),
            pltpu.SemaphoreType.DMA((2, 8)),
            pltpu.SemaphoreType.DMA((8,)),
        ]
        + inner_scratch(inner, features),
        compiler_params=pltpu.CompilerParams(
            collective_id=collective, has_side_effects=True, vmem_limit_bytes=56 * 2**20
        ),
        name="finish_gradients",
    )(grad_qkv, grad_out, crossed, kept, window_fc, window_proj)


def local(
    inputs,
    block_order,
    cotangent,
    ln1_gain,
    ln1_bias,
    w_qkv,
    bias_q,
    bias_v,
    w_out,
    bias_out,
    ln2_gain,
    ln2_bias,
    w_fc,
    bias_fc,
    w_proj,
    bias_proj,
):
    ctx, wt = lax.axis_index("ctx"), lax.axis_index("wt")
    ctx_count = lax.axis_size("ctx")
    rows, features = inputs.shape[1:]
    share = features // 4
    ff = w_fc.shape[1] // 4
    shift = 16 * wt

    small = jnp.stack([ln1_gain, ln1_bias, bias_q, bias_v, bias_out, ln2_gain, ln2_bias, bias_proj])
    received, all_order, vectors, own_qkv, normed_one, pieces, wide_out, placed_out = project(
        inputs[0], block_order, small, w_qkv, w_fc, w_out, 1
    )
    own_qkv = own_qkv.reshape(features, COLUMNS)
    normed_one = normed_one.reshape(4 * rows, features)
    gain_one, shift_one, _, _, full_bout, gain_two, shift_two, full_bproj = vectors
    orders = all_order[:, 0, :ctx_count]
    place = lax.dynamic_index_in_dim(orders, jnp.minimum(ctx // GROUP, 3), 0, keepdims=False)
    slots = jnp.arange(ctx_count, dtype=jnp.int32)
    inverse = jnp.sum(jnp.where(place[None, :] == slots[:, None], slots[None, :], 0), axis=1)
    *saved, attended, middle, all_two, own_fc, group_cot = attend(
        received,
        inverse,
        place,
        placed_out,
        inputs[0],
        jnp.concatenate([full_bout[None], gain_two[None], shift_two[None], jnp.zeros((5, features), jnp.float32)]),
        pieces,
        cotangent[0],
        4,
    )

    tokens = inputs[0].astype(jnp.float32)
    all_two = all_two.reshape(4 * rows, features)
    own_fc = own_fc.reshape(features, ff)
    group_cot = group_cot.reshape(4 * rows, features)
    hidden_pre = dot(all_two, own_fc) + bias_fc.astype(jnp.float32)
    hidden_low = gelu_tanh(hidden_pre).astype(jnp.bfloat16)
    hidden_grad = dot(group_cot, w_proj, 1, 1)
    unused_gelu, gelu_back = jax.vjp(gelu_tanh, hidden_pre)
    pre_grad = gelu_back(hidden_grad)[0].astype(jnp.bfloat16)
    low = jnp.bfloat16
    grad_fc = dot(pre_grad, all_two, 0, 0).astype(low)
    grad_proj = dot(hidden_low, group_cot, 0, 0).astype(low)
    projected_out, middle_grad, norm_sums, all_branch, upstream, window_fc, window_proj = feed_back(
        hidden_low,
        pre_grad,
        w_proj,
        own_fc,
        grad_fc,
        grad_proj,
        middle,
        gain_two[None],
        cotangent[0],
        wide_out,
        7,
    )
    outputs = middle + projected_out + full_bproj
    grad_gain_two, grad_shift_two = norm_sums[0], norm_sums[1]
    all_branch = all_branch.reshape(4 * rows, features)

    own_stacked, normed_one_grad, window_fc, window_proj = attend_back(
        upstream, inverse, place, saved, window_fc, window_proj, own_qkv, 8
    )
    unused_first, first_back = jax.vjp(layer_norm, tokens, gain_one, shift_one)
    input_part, grad_gain_one, grad_shift_one = first_back(normed_one_grad)
    input_grad = middle_grad + input_part

    own_attended = lax.dynamic_slice_in_dim(attended.reshape(4 * rows, SPAN), shift, share, 1)
    grad_qkv = dot(own_stacked, normed_one).astype(low)
    grad_out = dot(own_attended, all_branch, 0, 0).astype(low)
    column = lambda value: lax.dynamic_slice_in_dim(value, share * wt, share, 0)
    sums = jnp.sum(own_stacked.astype(jnp.float32), axis=1).reshape(3, share)
    grad_bout = column(jnp.sum(all_branch.astype(jnp.float32), axis=0))
    grad_bproj = column(jnp.sum(group_cot.astype(jnp.float32), axis=0))
    grad_bfc = jnp.sum(pre_grad.astype(jnp.float32), axis=0)
    crossed_vectors = jnp.stack([grad_gain_one, grad_shift_one, grad_gain_two, grad_shift_two]).astype(low)
    kept_vectors = jnp.stack([jnp.concatenate([sums[0], sums[2], grad_bout, grad_bproj]), grad_bfc]).astype(low)
    tail = lambda value: jnp.pad(value, ((0, 16 - value.shape[0]), (0, 0)))
    sum_qkv, sum_out, crossed, kept, sum_fc, sum_proj = finish_gradients(
        grad_qkv, grad_out, tail(crossed_vectors), tail(kept_vectors), window_fc, window_proj, 9
    )
    sum_qkv, sum_out, sum_fc = (member.astype(jnp.float32) for member in (sum_qkv, sum_out, sum_fc))
    sum_proj = sum_proj.reshape(ff, features).astype(jnp.float32)
    norms = jnp.sum(crossed[:4].reshape(4, 4, share).astype(jnp.float32), axis=1)
    kept_sums = kept[:2].astype(jnp.float32)
    sum_bq, sum_bv, sum_bout, sum_bproj = kept_sums[0].reshape(4, share)
    return (
        outputs.astype(jnp.bfloat16)[None],
        input_grad[None],
        norms[0],
        norms[1],
        sum_qkv,
        sum_bq,
        sum_bv,
        sum_out,
        sum_bout,
        norms[2],
        norms[3],
        sum_fc,
        kept_sums[1],
        sum_proj,
        sum_bproj,
    )


def solution(mesh):
    placed = (
        P("wt", "ctx", None),
        P("wt", None),
        P("wt", "ctx", None),
        P("wt"),
        P("wt"),
        P("wt", None),
        P("wt"),
        P("wt"),
        P("wt", None),
        P("wt"),
        P("wt"),
        P("wt"),
        P("wt", None),
        P("wt"),
        P("wt", None),
        P("wt"),
    )
    return jax.shard_map(
        local,
        mesh=mesh,
        in_specs=placed,
        out_specs=(
            P("wt", "ctx", None),
            P("wt", "ctx", None),
            P("wt"),
            P("wt"),
            P("wt", None),
            P("wt"),
            P("wt"),
            P("wt", None),
            P("wt"),
            P("wt"),
            P("wt"),
            P("wt", None),
            P("wt"),
            P("wt", None),
            P("wt"),
        ),
        check_vma=False,
    )
```
